32 devices in a mesh: row: 8 (over y, x, core), col: 4 (over z).
Axes of the slice: x: 2, y: 2, z: 4, core: 2. Of those that a mesh axis runs over, the one named last changes fastest.
Arguments:
- flow: float32 [2, 8, 64, 1024], P(None, None, 'row', 'col'), may hold values from -4 to 4
- temp: float32 [8, 64, 1024], P(None, 'row', 'col'), may hold values from -4 to 4
- tracers: float32 [8, 16, 8, 16, 512], P('row', None, None, None, 'col'), may hold values from -4 to 4
- bottom: int32 [64, 1024], P('row', 'col'), may hold values from 0 to 8
- sunlight: float32 [64, 1024], P('row', 'col'), may hold values from 0.5 to 2
- rates: float32 [16, 16], replicated, may hold values from -2 to 2
Outputs:
- flow_out: float32 [2, 8, 64, 1024], P(None, None, 'row', 'col')
- temp_out: float32 [8, 64, 1024], P(None, 'row', 'col')
- tracers_out: float32 [8, 16, 8, 16, 512], P('row', None, None, None, 'col')
The draws below stay inside these ranges and needn't reach their ends.
Inputs may be any that keep to these rules, and one draw needn't show every extreme that they name: Columns are water at levels 0 to bottom - 1; 0 marks land.
All inputs are finite; a program needn't handle non-finite values.
Results may differ from the reference program's by a relative error of at most 0.0001.
Values sent between devices are 32-bit elements; how exact they have to be, the bound alone decides.
No kernel may reach another device: no remote copies, remote signals or barrier semaphores. Data moves between devices by JAX's collectives and lax.ppermute only.
A program may use at most 64 MiB of HBM per device.

```python
import math
import jax
import jax.numpy as jnp
from jax import lax

NTR = 16
NZ = 8
KL = 4
STEPS = 2
LAT_DEV = 8
LON_DEV = 256
NLAT = 64
NLON = 1024
N_ROW = 8
N_COL = 4


def touch_ends(result, rng, least, high):
    longest = result.shape.index(max(result.shape))
    spots = []
    for shift in (0, 1):
        where = [jax.random.randint(jax.random.fold_in(rng, axis), (), 0, length) for axis, length in enumerate(result.shape)]
        where[longest] = (where[longest] + shift) % result.shape[longest]
        spots.append(tuple(where))
    return result.at[spots[0]].set(least).at[spots[1]].set(high)


def level_of(rng, extent, split, smallest, high):
    def one(axis_at, blocks):
        heights = jax.random.uniform(jax.random.fold_in(jax.random.fold_in(rng, 6), axis_at), (blocks,), jnp.float32, smallest / len(split), high / len(split))
        return jnp.repeat(jnp.exp(heights), extent[axis_at] // blocks).reshape((-1,) + (1,) * (len(extent) - axis_at - 1))

    gain = one(*split[0])
    for cut in split[1:]:
        gain = gain * one(*cut)
    return gain


def noise(own_key, dims, deviation, limit, pieces=(), kind=jnp.bfloat16):
    loudness = level_of(own_key, dims, pieces, -0.22, 0.18) if pieces else 1.0
    array = jax.random.normal(own_key, dims, jnp.float32) * deviation * loudness
    return jnp.minimum(jnp.maximum(array, -limit), limit).astype(kind)


def setup_inputs(seed: int = 0) -> dict:
    splits = jax.random.split(jax.random.key(seed), 7)
    flow = noise(splits[0], (2, NZ, NLAT, NLON), 1.0, 4.0, ((2, 8), (3, 4)), jnp.float32)
    temp = noise(splits[1], (NZ, NLAT, NLON), 1.0, 4.0, ((1, 8), (2, 4)), jnp.float32)
    tracers = noise(splits[2], (N_ROW, NTR, NZ, 2 * LAT_DEV, NLON // 2), 1.0, 4.0, ((0, 8), (4, 4)), jnp.float32)
    bottom = touch_ends(jax.random.randint(splits[3], (NLAT, NLON), 0, NZ + 1), jax.random.fold_in(splits[3], 1), 0, NZ).astype(jnp.int32)
    sunlight = jnp.clip(jnp.exp(math.log(2.0) - 1.3862944 * jax.random.uniform(splits[4], (NLAT, NLON), jnp.float32) ** level_of(splits[4], (NLAT, NLON), ((0, 8), (1, 4)), -0.2, 0.2)), 0.5, 2.0)
    rates = noise(splits[5], (NTR, NTR), 0.5, 2.0, (), jnp.float32)
    return dict(flow=flow, temp=temp, tracers=tracers, bottom=bottom, sunlight=sunlight, rates=rates)


time_step = 0.2
viscosity = 0.2
expansion = 0.05
coriolis_base = 0.5
kappa_base = 0.05
kappa_shear = 0.2
react_step = 0.25
water_absorb = 0.1
pigment_absorb = 0.6
heat_gain = 1.0

def pad_edges(field):
    widths = [(0, 0)] * (field.ndim - 2) + [(1, 1), (1, 1)]
    return jnp.pad(field, widths)

def neighbour_sides(padded):
    middle = padded[..., 1:-1, 1:-1]
    return (middle, padded[..., 1:-1, 2:], padded[..., 1:-1, :-2], padded[..., 2:, 1:-1], padded[..., :-2, 1:-1])

def shear_kappa(flow_u, flow_v):
    below_u = jnp.concatenate([flow_u[1:], flow_u[-1:]], axis=0)
    below_v = jnp.concatenate([flow_v[1:], flow_v[-1:]], axis=0)
    shear_sq = (flow_u - below_u) ** 2 + (flow_v - below_v) ** 2
    return kappa_base + kappa_shear * shear_sq / (1.0 + shear_sq)

def make_faces(padded):
    kappa_pad = shear_kappa(padded[0], padded[1])
    u_mid, u_east, u_west, u_north, u_south = neighbour_sides(padded[0])
    v_mid, v_east, v_west, v_north, v_south = neighbour_sides(padded[1])
    m_mid, m_east, m_west, m_north, m_south = neighbour_sides(padded[3])
    k_mid, k_east, k_west, k_north, k_south = neighbour_sides(kappa_pad)
    open_e = m_mid * m_east
    open_w = m_mid * m_west
    open_n = m_mid * m_north
    open_s = m_mid * m_south
    return jnp.stack([0.5 * (u_mid + u_east) * open_e, 0.5 * (u_mid + u_west) * open_w, 0.5 * (v_mid + v_north) * open_n, 0.5 * (v_mid + v_south) * open_s, 0.5 * (k_mid + k_east) * open_e, 0.5 * (k_mid + k_west) * open_w, 0.5 * (k_mid + k_north) * open_n, 0.5 * (k_mid + k_south) * open_s, m_mid])

def transport(face_terms, padded):
    east_flux, west_flux, north_flux, south_flux = (face_terms[0], face_terms[1], face_terms[2], face_terms[3])
    east_cond, west_cond, north_cond, south_cond = (face_terms[4], face_terms[5], face_terms[6], face_terms[7])
    wet_mask = face_terms[8]
    middle, eastward, westward, northward, southward = neighbour_sides(padded)
    divergence = east_flux - west_flux + north_flux - south_flux
    upward = -lax.cumsum(divergence, axis=0, reverse=True)
    zero_top = jnp.zeros_like(upward[:1])
    w_bottom = jnp.concatenate([upward[1:], zero_top], axis=0)
    w_top = jnp.concatenate([zero_top, upward[1:]], axis=0)
    above_val = jnp.concatenate([middle[..., :1, :, :], middle[..., :-1, :, :]], axis=-3)
    below_val = jnp.concatenate([middle[..., 1:, :, :], middle[..., -1:, :, :]], axis=-3)
    advection = east_flux * 0.5 * (middle + eastward) - west_flux * 0.5 * (middle + westward) + north_flux * 0.5 * (middle + northward) - south_flux * 0.5 * (middle + southward) + w_top * 0.5 * (middle + above_val) - w_bottom * 0.5 * (middle + below_val)
    diffusion = east_cond * (eastward - middle) + west_cond * (westward - middle) + north_cond * (northward - middle) + south_cond * (southward - middle)
    return wet_mask * (middle + time_step * (diffusion - advection))

def momentum(padded, coriolis):
    pressure = -expansion * jnp.cumsum(padded[2], axis=0)
    p_mid, p_east, p_west, p_north, p_south = neighbour_sides(pressure)
    u_mid, u_east, u_west, u_north, u_south = neighbour_sides(padded[0])
    v_mid, v_east, v_west, v_north, v_south = neighbour_sides(padded[1])
    m_mid, m_east, m_west, m_north, m_south = neighbour_sides(padded[3])
    lap_u = m_mid * (m_east * (u_east - u_mid) + m_west * (u_west - u_mid) + m_north * (u_north - u_mid) + m_south * (u_south - u_mid))
    lap_v = m_mid * (m_east * (v_east - v_mid) + m_west * (v_west - v_mid) + m_north * (v_north - v_mid) + m_south * (v_south - v_mid))
    new_u = m_mid * (u_mid + time_step * (coriolis * v_mid - 0.5 * (p_east - p_west) + viscosity * lap_u))
    new_v = m_mid * (v_mid + time_step * (-coriolis * u_mid - 0.5 * (p_north - p_south) + viscosity * lap_v))
    return (new_u, new_v)

def absorption(pigment_top):
    squared = pigment_top * pigment_top
    transmit = jnp.exp(-(water_absorb + pigment_absorb * squared / (1.0 + squared)))
    above_light = jnp.cumprod(jnp.concatenate([jnp.ones_like(transmit[:1]), transmit[:-1]], axis=0), axis=0)
    return above_light * (1.0 - transmit)

def reaction(moved_field, rates, wet_mask):
    saturated = moved_field / jnp.sqrt(1.0 + moved_field * moved_field)

    def one_tracer(row_rates):
        return jnp.tensordot(row_rates, saturated, axes=1, precision=lax.Precision.HIGHEST)
    coupling = lax.map(one_tracer, rates)
    return moved_field + react_step * wet_mask * coupling

def blocks_to_grid(blocks):
    shaped = blocks.reshape(N_ROW // 2, 2, NTR, NZ, 2 * LAT_DEV, N_COL, LON_DEV // 2)
    shaped = jnp.transpose(shaped, (2, 3, 0, 4, 5, 1, 6))
    return shaped.reshape(NTR, NZ, NLAT, NLON)

def grid_to_blocks(field):
    shaped = field.reshape(NTR, NZ, N_ROW // 2, 2 * LAT_DEV, N_COL, 2, LON_DEV // 2)
    shaped = jnp.transpose(shaped, (2, 5, 0, 1, 3, 4, 6))
    return shaped.reshape(N_ROW, NTR, NZ, 2 * LAT_DEV, NLON // 2)

def reference(flow, temp, tracers, bottom, sunlight, rates):
    levels = jnp.arange(NZ, dtype=jnp.int32)[:, None, None]
    wet_mask = (levels < bottom[None]).astype(jnp.float32)
    latitude = jnp.arange(NLAT, dtype=jnp.int32).astype(jnp.float32)
    coriolis = (coriolis_base * (2.0 * (latitude + 0.5) / NLAT - 1.0))[:, None]
    flow_u = flow[0] * wet_mask
    flow_v = flow[1] * wet_mask
    heat_field = temp * wet_mask
    tracer_field = blocks_to_grid(tracers) * wet_mask
    for step_index in range(STEPS):
        padded = pad_edges(jnp.stack([flow_u, flow_v, heat_field, wet_mask]))
        face_terms = make_faces(padded)
        flow_u, flow_v = momentum(padded, coriolis)
        heat_field = transport(face_terms, padded[2])
        moved_field = lax.map(lambda single: transport(face_terms, pad_edges(single)), tracer_field)
        tracer_field = reaction(moved_field, rates, wet_mask)
        profile = absorption(tracer_field[0, :KL])
        heat_field = heat_field.at[:KL].add(heat_gain * sunlight * wet_mask[:KL] * profile)
    return (jnp.stack([flow_u, flow_v]), heat_field, grid_to_blocks(tracer_field))
```

```python
import functools
import jax
import jax.numpy as jnp
from jax import lax
from jax.experimental import pallas as pl
from jax.experimental.pallas import tpu as pltpu
from jax.sharding import PartitionSpec as P

KL = 4
STEPS = 2

time_step = 0.2
viscosity = 0.2
expansion = 0.05
coriolis_base = 0.5
kappa_base = 0.05
kappa_shear = 0.2
react_step = 0.25
water_absorb = 0.1
pigment_absorb = 0.6
heat_gain = 1.0

EXTRA = 4
WIN = 4


def up(x):
    return pltpu.roll(x, 1, 0)


def down(x):
    return pltpu.roll(x, x.shape[0] - 1, 0)


def lanes_of(shape):
    return lax.broadcasted_iota(jnp.int32, shape, 1)


def levels_of(shape):
    return lax.broadcasted_iota(jnp.int32, shape, 0)


def window(x, lat, into):
    lon = x.shape[1]
    lane = lanes_of(x.shape)
    base = WIN * (lat + 1)
    moved = pltpu.roll(x, (base + 2) % lon, 1)
    return jnp.where((lane >= base) & (lane < base + WIN), moved, into)


def pack_kernel(sc, flow, temp, tracers, bottom, sunlight, mine, other, g_send, g_other):
    nz, lat_dev, lon_dev = temp.shape
    ntr, _, lat_blk, lon = tracers.shape
    first = sc[0] == 0
    zero = jnp.zeros((nz, lon), jnp.float32)
    level = levels_of((nz, lon_dev))
    own = [zero] * EXTRA
    far = [zero] * EXTRA
    for t in range(lat_dev):
        depth = jnp.broadcast_to(bottom[t : t + 1, :], (nz, lon_dev))
        light = jnp.broadcast_to(sunlight[t : t + 1, :], (nz, lon_dev))
        wet = (level < depth).astype(jnp.float32)
        aux = jnp.where(level == 0, depth.astype(jnp.float32), jnp.where(level == 1, light, 0.0))
        for f, tile in enumerate((flow[0, :, t, :] * wet, flow[1, :, t, :] * wet, temp[:, t, :] * wet, aux)):
            low, high = (tile[:, :lon], tile[:, lon:])
            a, b = (jnp.where(first, low, high), jnp.where(first, high, low))
            mine[f, t] = a
            other[f, t] = b
            own[f] = window(a, t, own[f])
            far[f] = window(b, t, far[f])
    shift = sc[0] * (WIN * lat_dev)
    for f in range(EXTRA):
        g_send[ntr + f] = pltpu.roll(own[f], shift, 1)
        g_other[f] = pltpu.roll(far[f], shift, 1)

    def one(n, _):
        g = zero
        for t in range(lat_blk):
            g = window(tracers[n, :, t, :], t, g)
        g_send[n] = g
        return 0

    lax.fori_loop(0, ntr, one, 0)


def in_half(shape, half, lat_dev):
    lane = lanes_of(shape)
    base = WIN * (lat_dev * half + 1)
    return (lane >= base) & (lane < base + WIN * lat_dev)


def join_kernel(sc, mine, got, g_send, ocean, g_own):
    _, lat_dev, nz, lon = mine.shape
    ntr = g_send.shape[0] - EXTRA
    half = sc[0]
    own_lanes = in_half((nz, lon), half, lat_dev)
    zero = jnp.zeros((nz, lon), jnp.float32)
    g_own[:ntr] = g_send[:ntr]
    shift = (1 - half) * (WIN * lat_dev)
    for f in range(EXTRA):
        g = zero
        for t in range(lat_dev):
            ocean[f, half * lat_dev + t] = mine[f, t]
            ocean[f, (1 - half) * lat_dev + t] = got[f, t]
            g = window(got[f, t], t, g)
        g_own[ntr + f] = jnp.where(own_lanes, g_send[ntr + f], pltpu.roll(g, shift, 1))


def edge_kernel(sc, tracers, ocean, g_partner, g_other, g_outer, z, to_a, to_b):
    ntr, nz, lat_blk, lon = tracers.shape
    nf = ntr + EXTRA
    half = sc[0]
    tile = (nz, lon)
    own_lanes = in_half(tile, half, lat_blk // 2)
    west = lanes_of(tile) % WIN < 2
    outer_ok = sc[2] > 0
    even = sc[1] == 0
    lane = lanes_of(tile)
    low_corner = jnp.zeros(tile, jnp.float32)
    high_corner = low_corner
    for f in range(nf):
        partner = g_partner[f]
        if f >= ntr:
            partner = jnp.where(own_lanes, g_other[f - ntr], partner)
        outer = jnp.where(outer_ok, g_outer[f], 0.0)
        from_partner = (west.astype(jnp.int32) == half)
        cols = jnp.where(from_partner, partner, outer)
        z[f] = cols
        at = (lane >= WIN * f) & (lane < WIN * f + WIN)
        low_corner = jnp.where(at, pltpu.roll(cols, (WIN * f - WIN) % lon, 1), low_corner)
        high_corner = jnp.where(at, pltpu.roll(cols, (WIN * f - WIN * lat_blk) % lon, 1), high_corner)

    def fill(out, high):
        start = lat_blk - 2 if high else 0
        for i in range(2):
            for n in range(ntr):
                out[2 * n + i] = tracers[n, :, start + i, :]
            for f in range(EXTRA):
                out[2 * (ntr + f) + i] = ocean[f, start + i]
        out[2 * nf] = high_corner if high else low_corner

    @pl.when(even)
    def _():
        fill(to_a, True)
        fill(to_b, False)

    @pl.when(jnp.logical_not(even))
    def _():
        fill(to_a, False)
        fill(to_b, True)


def kappa_of(u, v):
    level = levels_of(u.shape)
    du, dv = (u - down(u), v - down(v))
    sq = jnp.where(level < u.shape[0] - 1, du * du + dv * dv, 0.0)
    return kappa_base + kappa_shear * sq / (1.0 + sq)


def pressure_of(heat):
    level = levels_of(heat.shape)
    total = heat
    k = 1
    while k < heat.shape[0]:
        total = total + jnp.where(level >= k, pltpu.roll(total, k, 0), 0.0)
        k *= 2
    return -expansion * total


def wet_of(aux):
    depth = jnp.broadcast_to(aux[0:1, :], aux.shape)
    return (levels_of(aux.shape).astype(jnp.float32) < depth).astype(jnp.float32)


def light_of(aux):
    return jnp.broadcast_to(aux[1:2, :], aux.shape)


def dynamics(u, v, wet, kap, prs, coriolis):
    um, ue, uw, un, us = u
    vm, ve, vw, vn, vs = v
    wm, we, ww, wn, ws = wet
    km, ke, kw, kn, ks = kap
    _, pe, pw, pn, ps = prs
    level = levels_of(um.shape)
    nz = um.shape[0]
    oe, ow, on, os_ = (wm * we, wm * ww, wm * wn, wm * ws)
    fe, fw, fn, fs = (0.5 * (um + ue) * oe, 0.5 * (um + uw) * ow, 0.5 * (vm + vn) * on, 0.5 * (vm + vs) * os_)
    ce, cw, cn, cs = (0.5 * (km + ke) * oe, 0.5 * (km + kw) * ow, 0.5 * (km + kn) * on, 0.5 * (km + ks) * os_)
    div = fe - fw + fn - fs
    total = div
    k = 1
    while k < nz:
        total = total + jnp.where(level < nz - k, pltpu.roll(total, nz - k, 0), 0.0)
        k *= 2
    w_top = jnp.where(level >= 1, -total, 0.0)
    w_bot = jnp.where(level < nz - 1, -down(total), 0.0)
    weights = (
        wm * (1.0 - time_step * (ce + cw + cn + cs + 0.5 * (div + w_top - w_bot))),
        time_step * (ce - 0.5 * fe),
        time_step * (cw + 0.5 * fw),
        time_step * (cn - 0.5 * fn),
        time_step * (cs + 0.5 * fs),
        (-0.5 * time_step) * wm * w_top,
        (0.5 * time_step) * wm * w_bot,
    )
    lap_u = oe * (ue - um) + ow * (uw - um) + on * (un - um) + os_ * (us - um)
    lap_v = oe * (ve - vm) + ow * (vw - vm) + on * (vn - vm) + os_ * (vs - vm)
    new_u = wm * (um + time_step * (coriolis * vm - 0.5 * (pe - pw) + viscosity * lap_u))
    new_v = wm * (vm + time_step * (-coriolis * um - 0.5 * (pn - ps) + viscosity * lap_v))
    return (new_u, new_v, weights)


def transport(weights, x, east, west, north, south):
    a0, ae, aw, an, as_, at, ab = weights
    return (a0 * x + ae * east) + (aw * west + an * north) + (as_ * south + at * up(x)) + ab * down(x)


def saturated(x):
    return x * lax.rsqrt(1.0 + x * x)


def absorbed(pigment):
    level = levels_of(pigment.shape)
    sq = pigment * pigment
    depth = water_absorb + pigment_absorb * (sq / (1.0 + sq))
    above = jnp.where(level >= 1, up(depth), 0.0)
    k = 1
    while k < KL:
        above = above + jnp.where(level >= k, pltpu.roll(above, k, 0), 0.0)
        k *= 2
    return jnp.where(level < KL, jnp.exp(-above) * (1.0 - jnp.exp(-depth)), 0.0)


def steps_kernel(total_lat, sc, tracers, ocean, z_in, g_in, got_a, got_b, mix, out, keep, send, m0, m1, dv, z0, z1, g0, zd, sat, uvh):
    ntr, nz, lat_blk, lon = tracers.shape
    nf = ntr + EXTRA
    U, V, H, X = (ntr, ntr + 1, ntr + 2, ntr + 3)
    KAP, PRS, WET = (0, 1, 2)
    tile = (nz, lon)
    lane = lanes_of(tile)
    col = lane % WIN
    at_first, at_last = (lane == 0, lane == lon - 1)
    even = sc[1] == 0
    south_ok, north_ok = (sc[3] > 0, sc[4] > 0)
    first_lat = sc[5] * lat_blk
    rows = lat_blk + 4

    def got(high, index):
        a, b = (got_a[index], got_b[index])
        picked = jnp.where(even, a, b) if high else jnp.where(even, b, a)
        return jnp.where(north_ok if high else south_ok, picked, 0.0)

    for f in range(EXTRA):
        for i in range(2):
            m0[ntr + f, i] = got(False, 2 * (ntr + f) + i)
            m0[ntr + f, lat_blk + 2 + i] = got(True, 2 * (ntr + f) + i)
        for t in range(lat_blk):
            m0[ntr + f, t + 2] = ocean[f, t]

    def derive0(r, _):
        dv[WET, r] = wet_of(m0[X, r])
        dv[KAP, r] = kappa_of(m0[U, r], m0[V, r])
        dv[PRS, r] = pressure_of(m0[H, r])
        return 0

    lax.fori_loop(0, rows, derive0, 0)

    for i in range(2):
        for n in range(ntr):
            m0[n, i] = got(False, 2 * n + i) * dv[WET, i]
            m0[n, lat_blk + 2 + i] = got(True, 2 * n + i) * dv[WET, lat_blk + 2 + i]

    def load(t, _):
        wet = dv[WET, t + 2]
        for n in range(ntr):
            m0[n, t + 2] = tracers[n, :, t, :] * wet
        return 0

    for t in range(lat_blk):
        load(t, 0)

    low_corner, high_corner = (got(False, 2 * nf), got(True, 2 * nf))
    at_low, at_high = (lane < WIN, (lane >= WIN * (lat_blk + 1)) & (lane < WIN * (lat_blk + 2)))
    for f in reversed(range(nf)):
        cols = jnp.where(at_low, pltpu.roll(low_corner, (-WIN * f) % lon, 1), z_in[f])
        cols = jnp.where(at_high, pltpu.roll(high_corner, (WIN * (lat_blk + 1) - WIN * f) % lon, 1), cols)
        own = g_in[f]
        if f == X:
            wet_z, wet_g = (wet_of(cols), wet_of(own))
            light_z = light_of(cols)
        if f < ntr:
            cols, own = (cols * wet_z, own * wet_g)
        z0[f] = cols
        g0[f] = own
    zd[KAP] = kappa_of(z0[U], z0[V])
    zd[PRS] = pressure_of(z0[H])
    zd[WET] = wet_z

    def coriolis_at(lat):
        return coriolis_base * (2.0 * (lat.astype(jnp.float32) + 0.5) / total_lat - 1.0)

    def react(moved, wet):
        for n in range(ntr):
            sat[n * nz : (n + 1) * nz, :] = saturated(moved[n])
        mixed = jnp.dot(mix[...], sat[...], precision=lax.Precision.HIGHEST, preferred_element_type=jnp.float32)
        gain = react_step * wet
        return [moved[n] + gain * mixed[n * nz : (n + 1) * nz, :] for n in range(ntr)]

    def around_z(x, own):
        west = pltpu.roll(jnp.where(col == 0, x, own), 1, 1)
        east = pltpu.roll(jnp.where(col == WIN - 1, x, own), lon - 1, 1)
        return (x, east, west, pltpu.roll(x, lon - WIN, 1), pltpu.roll(x, WIN, 1))

    own_u, own_v = (g0[U], g0[V])
    new_u, new_v, weights = dynamics(
        around_z(z0[U], own_u),
        around_z(z0[V], own_v),
        around_z(wet_z, wet_g),
        around_z(zd[KAP], kappa_of(own_u, own_v)),
        around_z(zd[PRS], pressure_of(g0[H])),
        coriolis_at(first_lat + lane // WIN - 1),
    )
    moved = [transport(weights, *around_z(z0[n], g0[n])) for n in range(ntr)]
    done = react(moved, wet_z)
    for n in range(ntr):
        z1[n] = done[n]
    z1[U] = new_u
    z1[V] = new_v
    z1[H] = transport(weights, *around_z(z0[H], g0[H])) + heat_gain * light_z * wet_z * absorbed(done[0])

    def row_step(r, m, z):
        shift = lon - 2 - WIN * (r - 1)

        def sides(x, cols):
            beside = pltpu.roll(cols, shift, 1)
            west = pltpu.roll(jnp.where(at_last, beside, x), 1, 1)
            east = pltpu.roll(jnp.where(at_first, beside, x), lon - 1, 1)
            return (east, west)

        def around(f):
            x = m[f, r]
            return (x, *sides(x, z[f]), m[f, r + 1], m[f, r - 1])

        def around_dv(f):
            x = dv[f, r]
            return (x, *sides(x, zd[f]), dv[f, r + 1], dv[f, r - 1])

        wet = around_dv(WET)
        new_u, new_v, weights = dynamics(
            around(U), around(V), wet, around_dv(KAP), around_dv(PRS), coriolis_at(first_lat + r - 2)
        )
        moved = [transport(weights, *around(n)) for n in range(ntr)]
        done = react(moved, wet[0])
        heat = transport(weights, *around(H)) + heat_gain * light_of(m0[X, r]) * wet[0] * absorbed(done[0])
        return (done, new_u, new_v, heat)

    def first(r, _):
        done, new_u, new_v, heat = row_step(r, m0, z0)
        for n in range(ntr):
            m1[n, r] = done[n]
        m1[U, r] = new_u
        m1[V, r] = new_v
        m1[H, r] = heat
        return 0

    lax.fori_loop(1, rows - 1, first, 0)

    def derive1(r, _):
        dv[KAP, r] = kappa_of(m1[U, r], m1[V, r])
        dv[PRS, r] = pressure_of(m1[H, r])
        return 0

    lax.fori_loop(1, rows - 1, derive1, 0)
    zd[KAP] = kappa_of(z1[U], z1[V])
    zd[PRS] = pressure_of(z1[H])

    def second(r, _):
        done, new_u, new_v, heat = row_step(r, m1, z1)
        for n in range(ntr):
            m0[n, r] = done[n]
        uvh[0, r - 2] = new_u
        uvh[1, r - 2] = new_v
        uvh[2, r - 2] = heat
        return 0

    lax.fori_loop(2, rows - 2, second, 0)
    for t in range(lat_blk):
        for n in range(ntr):
            out[n, :, t, :] = m0[n, t + 2]
    half = lat_blk // 2
    for f in range(3):
        for t in range(half):
            keep[f, t] = uvh[f, sc[0] * half + t]
            send[f, t] = uvh[f, (1 - sc[0]) * half + t]


def unpack_kernel(sc, keep, got, flow, temp):
    _, lat_dev, nz, lon = keep.shape
    first = sc[0] == 0
    for t in range(lat_dev):
        for f in range(3):
            a, b = (keep[f, t], got[f, t])
            low, high = (jnp.where(first, a, b), jnp.where(first, b, a))
            if f < 2:
                flow[f, :, t, :lon] = low
                flow[f, :, t, lon:] = high
            else:
                temp[:, t, :lon] = low
                temp[:, t, lon:] = high


def call(kernel, outs, *args, scratch=()):
    vmem = pl.BlockSpec(memory_space=pltpu.VMEM)
    return pl.pallas_call(
        kernel,
        out_shape=[jax.ShapeDtypeStruct(s, jnp.float32) for s in outs],
        in_specs=[pl.BlockSpec(memory_space=pltpu.SMEM)] + [vmem] * (len(args) - 1),
        out_specs=[vmem] * len(outs),
        scratch_shapes=[pltpu.VMEM(s, jnp.float32) for s in scratch],
        compiler_params=pltpu.CompilerParams(vmem_limit_bytes=40 * 2**20),
    )(*args)


def both_ways(pairs):
    return sorted(pairs + [(b, a) for a, b in pairs])


def exchanges(n_row, n_col):
    chips = n_row // 2

    def dev(p, h, c):
        return (2 * p + h) * n_col + c

    partner = [(dev(p, 0, c), dev(p, 1, c)) for p in range(chips) for c in range(n_col)]
    outer = [(dev(p, 1, c), dev(p, 0, c + 1)) for p in range(chips) for c in range(n_col - 1)]
    for p in range(0, chips - 1, 2):
        outer += [(dev(p, 0, 0), dev(p + 1, 0, 0)), (dev(p, 1, n_col - 1), dev(p + 1, 1, n_col - 1))]
    lat_a = [(dev(p, h, c), dev(p + 1, h, c)) for p in range(0, chips - 1, 2) for h in (0, 1) for c in range(n_col)]
    lat_b = [(dev(p, h, c), dev(p + 1, h, c)) for p in range(1, chips - 1, 2) for h in (0, 1) for c in range(n_col)]
    if chips % 2 == 0 and chips > 2:
        lat_b += [(dev(0, h, c), dev(chips - 1, h, c)) for h in (0, 1) for c in range(n_col)]
    return [both_ways(x) for x in (partner, outer, lat_a, lat_b)]


def on_device(n_row, n_col, flow, temp, tracers, bottom, sunlight, rates):
    nz, lat_dev, lon_dev = temp.shape
    _, ntr, _, lat_blk, lon = tracers.shape
    nf = ntr + EXTRA
    chips = n_row // 2
    row, column = (lax.axis_index("row"), lax.axis_index("col"))
    half, place = (row % 2, row // 2)
    outer_ok = jnp.where(half == 0, column > 0, column < n_col - 1)
    sc = jnp.stack([half, place % 2, outer_ok, place > 0, place < chips - 1, place]).astype(jnp.int32)
    partner, outer, lat_a, lat_b = exchanges(n_row, n_col)

    def swap(x, pairs):
        return lax.ppermute(x, ("row", "col"), pairs)

    block = tracers[0]
    mix = jnp.kron(rates, jnp.eye(nz, dtype=jnp.float32))
    half_shape = (EXTRA, lat_dev, nz, lon)
    mine, other, g_send, g_other = call(
        pack_kernel, [half_shape, half_shape, (nf, nz, lon), (EXTRA, nz, lon)], sc, flow, temp, block, bottom, sunlight
    )
    got, g_partner = swap((other, g_send), partner)
    ocean, g_own = call(join_kernel, [(EXTRA, lat_blk, nz, lon), (nf, nz, lon)], sc, mine, got, g_send)
    g_outer = swap(g_own, outer)
    edge_shape = (2 * nf + 1, nz, lon)
    z, to_a, to_b = call(
        edge_kernel, [(nf, nz, lon), edge_shape, edge_shape], sc, block, ocean, g_partner, g_other, g_outer
    )
    got_a, got_b = (swap(to_a, lat_a), swap(to_b, lat_b))
    rows = lat_blk + 4
    cols = (nf, nz, lon)
    third = (3, lat_dev, nz, lon)
    out, keep, send = call(
        functools.partial(steps_kernel, n_row * lat_dev),
        [(ntr, nz, lat_blk, lon), third, third],
        sc,
        block,
        ocean,
        z,
        g_own,
        got_a,
        got_b,
        mix,
        scratch=[
            (nf, rows, nz, lon),
            (nf, rows, nz, lon),
            (3, rows, nz, lon),
            cols,
            cols,
            cols,
            (3, nz, lon),
            (ntr * nz, lon),
            (3, lat_blk, nz, lon),
        ],
    )
    flow_out, temp_out = call(
        unpack_kernel, [(2, nz, lat_dev, lon_dev), (nz, lat_dev, lon_dev)], sc, keep, swap(send, partner)
    )
    return (flow_out, temp_out, out[None])


def solution(mesh):
    in_specs = (
        P(None, None, "row", "col"),
        P(None, "row", "col"),
        P("row", None, None, None, "col"),
        P("row", "col"),
        P("row", "col"),
        P(),
    )
    out_specs = (
        P(None, None, "row", "col"),
        P(None, "row", "col"),
        P("row", None, None, None, "col"),
    )
    return jax.shard_map(
        functools.partial(on_device, mesh.shape["row"], mesh.shape["col"]),
        mesh=mesh,
        in_specs=in_specs,
        out_specs=out_specs,
        check_vma=False,
    )
```

```python
import functools
import jax
import jax.numpy as jnp
from jax import lax
from jax.experimental import pallas as pl
from jax.experimental.pallas import tpu as pltpu
from jax.sharding import PartitionSpec as P

KL = 4
STEPS = 2

time_step = 0.2
viscosity = 0.2
expansion = 0.05
coriolis_base = 0.5
kappa_base = 0.05
kappa_shear = 0.2
react_step = 0.25
water_absorb = 0.1
pigment_absorb = 0.6
heat_gain = 1.0

EXTRA = 4
WIN = 4


def up(x):
    return pltpu.roll(x, 1, x.ndim - 2)


def down(x):
    return pltpu.roll(x, x.shape[-2] - 1, x.ndim - 2)


def lanes_of(shape):
    return lax.broadcasted_iota(jnp.int32, shape, len(shape) - 1)


def levels_of(shape):
    return lax.broadcasted_iota(jnp.int32, shape, len(shape) - 2)


def window(x, lat, into):
    lon = x.shape[1]
    lane = lanes_of(x.shape)
    base = WIN * (lat + 1)
    moved = pltpu.roll(x, (base + 2) % lon, 1)
    return jnp.where((lane >= base) & (lane < base + WIN), moved, into)


def place():
    row = lax.axis_index("row")
    return (row % 2, row // 2, lax.axis_index("col"))


def pack_kernel(surface, tracers_in, mine, other, g_send, g_other, turned, tracers, sem):
    _, lat_dev, lon_dev = surface.shape
    ntr, nz, lat_blk, lon = tracers.shape
    half, _, _ = place()
    first = half == 0
    big = [
        pltpu.make_async_copy(tracers_in.at[pl.ds(n, GROUP)], tracers.at[pl.ds(n, GROUP)], sem.at[n // GROUP])
        for n in range(0, ntr, GROUP)
    ]
    for copy in big:
        copy.start()
    zero = jnp.zeros((nz, lon), jnp.float32)
    level = levels_of((nz, lon_dev))
    own = [zero] * EXTRA
    far = [zero] * EXTRA
    for t in range(lat_dev):
        depth = jnp.broadcast_to(surface[3 * nz, t : t + 1, :], (nz, lon_dev))
        light = jnp.broadcast_to(surface[3 * nz + 1, t : t + 1, :], (nz, lon_dev))
        wet = (level.astype(jnp.float32) < depth).astype(jnp.float32)
        aux = jnp.where(level == 0, depth, jnp.where(level == 1, light, 0.0))
        for f, tile in enumerate([surface[f * nz : (f + 1) * nz, t, :] * wet for f in range(3)] + [aux]):
            low, high = (tile[:, :lon], tile[:, lon:])
            a, b = (jnp.where(first, low, high), jnp.where(first, high, low))
            mine[f, t] = a
            other[f, t] = b
            own[f] = window(a, t, own[f])
            far[f] = window(b, t, far[f])
    shift = half * (WIN * lat_dev)
    for f in range(EXTRA):
        g_send[ntr + f] = pltpu.roll(own[f], shift, 1)
        g_other[f] = pltpu.roll(far[f], shift, 1)
    for i, copy in enumerate(big):
        copy.wait()
        g = [zero] * GROUP
        for t in range(lat_blk):
            for k in range(GROUP):
                x = tracers[i * GROUP + k, :, t, :]
                turned[i * GROUP + k, t] = x
                g[k] = window(x, t, g[k])
        for k in range(GROUP):
            g_send[i * GROUP + k] = g[k]


def in_half(shape, half, lat_dev):
    lane = lanes_of(shape)
    base = WIN * (lat_dev * half + 1)
    return (lane >= base) & (lane < base + WIN * lat_dev)


def join_kernel(mine, got, g_send, ocean, g_own):
    _, lat_dev, nz, lon = mine.shape
    ntr = g_send.shape[0] - EXTRA
    half, _, _ = place()
    own_lanes = in_half((nz, lon), half, lat_dev)
    zero = jnp.zeros((nz, lon), jnp.float32)
    g_own[:ntr] = g_send[:ntr]
    shift = (1 - half) * (WIN * lat_dev)
    for f in range(EXTRA):
        g = zero
        for t in range(lat_dev):
            ocean[f, half * lat_dev + t] = mine[f, t]
            ocean[f, (1 - half) * lat_dev + t] = got[f, t]
            g = window(got[f, t], t, g)
        g_own[ntr + f] = jnp.where(own_lanes, g_send[ntr + f], pltpu.roll(g, shift, 1))


def edge_kernel(turned, ocean, g_partner, g_other, g_outer, z, to_a, to_b):
    ntr, lat_blk, nz, lon = turned.shape
    nf = ntr + EXTRA
    half, chip, column = place()
    n_col = lax.axis_size("col")
    tile = (nz, lon)
    own_lanes = in_half(tile, half, lat_blk // 2)
    west = lanes_of(tile) % WIN < 2
    outer_ok = jnp.where(half == 0, column > 0, column < n_col - 1)
    even = chip % 2 == 0
    lane = lanes_of(tile)
    low_corner = jnp.zeros(tile, jnp.float32)
    high_corner = low_corner
    for f in range(nf):
        partner = g_partner[f]
        if f >= ntr:
            partner = jnp.where(own_lanes, g_other[f - ntr], partner)
        outer = jnp.where(outer_ok, g_outer[f], 0.0)
        from_partner = (west.astype(jnp.int32) == half)
        cols = jnp.where(from_partner, partner, outer)
        z[f] = cols
        at = (lane >= WIN * f) & (lane < WIN * f + WIN)
        low_corner = jnp.where(at, pltpu.roll(cols, (WIN * f - WIN) % lon, 1), low_corner)
        high_corner = jnp.where(at, pltpu.roll(cols, (WIN * f - WIN * lat_blk) % lon, 1), high_corner)

    def fill(out, high):
        start = lat_blk - 2 if high else 0
        for i in range(2):
            for n in range(ntr):
                out[2 * n + i] = turned[n, start + i]
            for f in range(EXTRA):
                out[2 * (ntr + f) + i] = ocean[f, start + i]
        out[2 * nf] = high_corner if high else low_corner

    @pl.when(even)
    def _():
        fill(to_a, True)
        fill(to_b, False)

    @pl.when(jnp.logical_not(even))
    def _():
        fill(to_a, False)
        fill(to_b, True)


def kappa_of(u, v):
    du, dv = (u - down(u), v - down(v))
    sq = jnp.where(levels_of(u.shape) < u.shape[-2] - 1, du * du + dv * dv, 0.0)
    return kappa_base + kappa_shear * sq / (1.0 + sq)


def sum_above(x):
    level = levels_of(x.shape)
    k = 1
    while k < x.shape[-2]:
        x = x + jnp.where(level >= k, pltpu.roll(x, k, x.ndim - 2), 0.0)
        k *= 2
    return x


def sum_below(x):
    level, nz = (levels_of(x.shape), x.shape[-2])
    k = 1
    while k < nz:
        x = x + jnp.where(level < nz - k, pltpu.roll(x, nz - k, x.ndim - 2), 0.0)
        k *= 2
    return x


def pressure_of(heat):
    return -expansion * sum_above(heat)


def wet_of(aux):
    depth = jnp.broadcast_to(aux[..., 0:1, :], aux.shape)
    return (levels_of(aux.shape).astype(jnp.float32) < depth).astype(jnp.float32)


def light_of(aux):
    return jnp.broadcast_to(aux[..., 1:2, :], aux.shape)


def dynamics(u, v, wet, kap, prs, coriolis):
    um, ue, uw, un, us = u
    vm, ve, vw, vn, vs = v
    wm, we, ww, wn, ws = wet
    km, ke, kw, kn, ks = kap
    _, pe, pw, pn, ps = prs
    level, nz = (levels_of(um.shape), um.shape[-2])
    oe, ow, on, os_ = (wm * we, wm * ww, wm * wn, wm * ws)
    fe, fw, fn, fs = (0.5 * (um + ue) * oe, 0.5 * (um + uw) * ow, 0.5 * (vm + vn) * on, 0.5 * (vm + vs) * os_)
    ce, cw, cn, cs = (0.5 * (km + ke) * oe, 0.5 * (km + kw) * ow, 0.5 * (km + kn) * on, 0.5 * (km + ks) * os_)
    div = fe - fw + fn - fs
    total = sum_below(div)
    w_top = jnp.where(level >= 1, -total, 0.0)
    w_bot = jnp.where(level < nz - 1, -down(total), 0.0)
    weights = (
        wm * (1.0 - time_step * (ce + cw + cn + cs + 0.5 * (div + w_top - w_bot))),
        time_step * (ce - 0.5 * fe),
        time_step * (cw + 0.5 * fw),
        time_step * (cn - 0.5 * fn),
        time_step * (cs + 0.5 * fs),
        (-0.5 * time_step) * wm * w_top,
        (0.5 * time_step) * wm * w_bot,
    )
    lap_u = oe * (ue - um) + ow * (uw - um) + on * (un - um) + os_ * (us - um)
    lap_v = oe * (ve - vm) + ow * (vw - vm) + on * (vn - vm) + os_ * (vs - vm)
    new_u = wm * (um + time_step * (coriolis * vm - 0.5 * (pe - pw) + viscosity * lap_u))
    new_v = wm * (vm + time_step * (-coriolis * um - 0.5 * (pn - ps) + viscosity * lap_v))
    return (new_u, new_v, weights)


def transport(weights, x, east, west, north, south):
    a0, ae, aw, an, as_, at, ab = weights
    return (a0 * x + ae * east) + (aw * west + an * north) + (as_ * south + at * up(x)) + ab * down(x)


def saturated(x):
    return x * lax.rsqrt(1.0 + x * x)


def absorbed(pigment):
    level = levels_of(pigment.shape)
    sq = pigment * pigment
    depth = water_absorb + pigment_absorb * (sq / (1.0 + sq))
    above = jnp.where(level >= 1, up(depth), 0.0)
    k = 1
    while k < KL:
        above = above + jnp.where(level >= k, pltpu.roll(above, k, above.ndim - 2), 0.0)
        k *= 2
    return jnp.where(level < KL, jnp.exp(-above) * (1.0 - jnp.exp(-depth)), 0.0)


def two_parts(x):
    high = x.astype(jnp.bfloat16)
    return (high, (x - high.astype(jnp.float32)).astype(jnp.bfloat16))


def mix_matrix(mix):
    high, low = two_parts(mix)
    top = jnp.concatenate([high, high], axis=1)
    return jnp.concatenate([top, jnp.concatenate([low, jnp.zeros_like(low)], axis=1)], axis=0)


def beside(z, r, lon):
    return pltpu.roll(z, lon - 2 - WIN * (r - 1), z.ndim - 1)


def sides(x, edge):
    lane, lon = (lanes_of(x.shape), x.shape[-1])
    west = pltpu.roll(jnp.where(lane == lon - 1, edge, x), 1, x.ndim - 1)
    east = pltpu.roll(jnp.where(lane == 0, edge, x), lon - 1, x.ndim - 1)
    return (east, west)


def around_rows(m, f, z, r, count):
    x = m[f, pl.ds(r, count)]
    edge = jnp.stack([beside(z, r + i, x.shape[-1]) for i in range(count)])
    return (x, *sides(x, edge), m[f, pl.ds(r + 1, count)], m[f, pl.ds(r - 1, count)])


def around_columns(x, own):
    lane, lon = (lanes_of(x.shape), x.shape[-1])
    west = pltpu.roll(jnp.where(lane % WIN == 0, x, own), 1, x.ndim - 1)
    east = pltpu.roll(jnp.where(lane % WIN == WIN - 1, x, own), lon - 1, x.ndim - 1)
    return (x, east, west, pltpu.roll(x, lon - WIN, x.ndim - 1), pltpu.roll(x, WIN, x.ndim - 1))


KAP, PRS, WET = (0, 1, 2)
GROUP = 4


def chunks(start, stop, most, body):
    count = max(k for k in range(1, most + 1) if (stop - start) % k == 0)

    def one(i, _):
        body(start + i * count, count)
        return 0

    lax.fori_loop(0, (stop - start) // count, one, 0)


def derive_rows(m, dv, ntr, start, stop):
    def body(r, count):
        at = pl.ds(r, count)
        dv[KAP, at] = kappa_of(m[ntr, at], m[ntr + 1, at])
        dv[PRS, at] = pressure_of(m[ntr + 2, at])

    chunks(start, stop, 10, body)


def derive_columns(z, zd, ntr):
    zd[KAP] = kappa_of(z[ntr], z[ntr + 1])
    zd[PRS] = pressure_of(z[ntr + 2])


def ocean_rows(m, dv, z, zd, wts, new, coriolis_at, ntr, start, stop):
    def body(r, count):
        at = pl.ds(r, count)
        lat = lax.broadcasted_iota(jnp.int32, (count, *m.shape[2:]), 0) + (r - 2)
        new_u, new_v, weights = dynamics(
            around_rows(m, ntr, z[ntr], r, count),
            around_rows(m, ntr + 1, z[ntr + 1], r, count),
            around_rows(dv, WET, zd[WET], r, count),
            around_rows(dv, KAP, zd[KAP], r, count),
            around_rows(dv, PRS, zd[PRS], r, count),
            coriolis_at(lat),
        )
        new[ntr, at] = new_u
        new[ntr + 1, at] = new_v
        for i, w in enumerate(weights):
            wts[i, at] = w

    chunks(start, stop, 9, body)


def tracer_rows(m, z, wts, new, sat, ntr, start, stop):
    nz, lon = m.shape[2:]
    half = ntr * nz

    def row(r):
        weights = [wts[i, r] for i in range(7)]
        for n in range(0, ntr, GROUP):
            x = m[n : n + GROUP, r]
            edge = beside(z[n : n + GROUP], r, lon)
            moved = transport(weights, x, *sides(x, edge), m[n : n + GROUP, r + 1], m[n : n + GROUP, r - 1])
            new[n : n + GROUP, r] = moved
            high, low = two_parts(saturated(moved).reshape(GROUP * nz, lon))
            sat[r, n * nz : (n + GROUP) * nz, :] = high
            sat[r, half + n * nz : half + (n + GROUP) * nz, :] = low
        h = ntr + 2
        x = m[h, r]
        new[h, r] = transport(weights, x, *sides(x, beside(z[h], r, lon)), m[h, r + 1], m[h, r - 1])

    def body(r, count):
        for i in range(count):
            row(r + i)

    chunks(start, stop, 3, body)


def react_rows(dv, mix, new, sat, ntr, start, stop):
    nz, lon = new.shape[2:]
    half = ntr * nz

    def body(r, count):
        both = jnp.concatenate([sat[r + i] for i in range(count)], axis=1)
        res = jnp.dot(mix[...], both, preferred_element_type=jnp.float32)
        res = res[:half] + res[half:]
        for i in range(count):
            gain = react_step * dv[WET, r + i]
            for n in range(ntr):
                new[n, r + i] = new[n, r + i] + gain * res[n * nz : (n + 1) * nz, i * lon : (i + 1) * lon]

    chunks(start, stop, 18, body)


def light_rows(m, dv, new, ntr, start, stop):
    def body(r, count):
        at = pl.ds(r, count)
        new[ntr + 2, at] += heat_gain * light_of(m[ntr + 3, at]) * dv[WET, at] * absorbed(new[0, at])

    chunks(start, stop, 9, body)


def column_step(z0, g0, zd, gd, z1, mix, coriolis, ntr):
    nz, lon = z0.shape[1:]
    half = ntr * nz
    wet = zd[WET]
    new_u, new_v, weights = dynamics(
        around_columns(z0[ntr], g0[ntr]),
        around_columns(z0[ntr + 1], g0[ntr + 1]),
        around_columns(wet, gd[WET]),
        around_columns(zd[KAP], gd[KAP]),
        around_columns(zd[PRS], gd[PRS]),
        coriolis,
    )
    moved = transport(weights, *around_columns(z0[:ntr], g0[:ntr]))
    high, low = two_parts(saturated(moved).reshape(half, lon))
    res = jnp.dot(mix[...], jnp.concatenate([high, low], axis=0), preferred_element_type=jnp.float32)
    done = moved + (react_step * wet) * (res[:half] + res[half:]).reshape(ntr, nz, lon)
    z1[:ntr] = done
    z1[ntr] = new_u
    z1[ntr + 1] = new_v
    heat = transport(weights, *around_columns(z0[ntr + 2], g0[ntr + 2]))
    z1[ntr + 2] = heat + heat_gain * light_of(z0[ntr + 3]) * wet * absorbed(done[0])


def fill_ocean(ocean, got, m0, dv, ntr):
    lat_blk = ocean.shape[1]
    rows = lat_blk + 4
    for f in range(EXTRA):
        for i in range(2):
            m0[ntr + f, i] = got(False, 2 * (ntr + f) + i)
            m0[ntr + f, lat_blk + 2 + i] = got(True, 2 * (ntr + f) + i)
        m0[ntr + f, 2 : lat_blk + 2] = ocean[f]

    def wets(r, count):
        at = pl.ds(r, count)
        dv[WET, at] = wet_of(m0[ntr + 3, at])

    chunks(0, rows, 10, wets)


def fill_tracers(turned, got, m0, dv):
    ntr, lat_blk, _, _ = turned.shape
    for i in range(2):
        for n in range(ntr):
            m0[n, i] = got(False, 2 * n + i) * dv[WET, i]
            m0[n, lat_blk + 2 + i] = got(True, 2 * n + i) * dv[WET, lat_blk + 2 + i]

    def some(t, _):
        wet = dv[WET, t + 2]
        for n in range(ntr):
            m0[n, t + 2] = turned[n, t] * wet
        return 0

    lax.fori_loop(0, lat_blk, some, 0)


def fill_columns(z_in, g_in, got, z0, g0, zd, gd, ntr, lat_blk):
    nf = ntr + EXTRA
    nz, lon = z_in.shape[1:]
    lane = lanes_of((nz, lon))
    low_corner, high_corner = (got(False, 2 * nf), got(True, 2 * nf))
    at_low, at_high = (lane < WIN, (lane >= WIN * (lat_blk + 1)) & (lane < WIN * (lat_blk + 2)))
    for f in reversed(range(nf)):
        cols = jnp.where(at_low, pltpu.roll(low_corner, (-WIN * f) % lon, 1), z_in[f])
        cols = jnp.where(at_high, pltpu.roll(high_corner, (WIN * (lat_blk + 1) - WIN * f) % lon, 1), cols)
        own = g_in[f]
        if f == nf - 1:
            wet_z, wet_g = (wet_of(cols), wet_of(own))
            zd[WET] = wet_z
            gd[WET] = wet_g
        if f < ntr:
            cols, own = (cols * wet_z, own * wet_g)
        z0[f] = cols
        g0[f] = own


def write_out(m, out, ntr):
    lat_blk = out.shape[2]

    def some(t, _):
        for n in range(ntr):
            out[n, :, t, :] = m[n, t + 2]
        return 0

    lax.fori_loop(0, lat_blk, some, 0)


def steps_kernel(turned, ocean, z_in, g_in, got_a, got_b, rate_mix, out, keep, send, m0, m1, dv, wts, sat, mix, z0, z1, g0, zd, gd):
    ntr, lat_blk, nz, lon = turned.shape
    place_half, chip, _ = place()
    chips = lax.axis_size("row") // 2
    even = chip % 2 == 0
    south_ok, north_ok = (chip > 0, chip < chips - 1)
    rows = lat_blk + 4

    def got(high, index):
        a, b = (got_a[index], got_b[index])
        picked = jnp.where(even, a, b) if high else jnp.where(even, b, a)
        return jnp.where(north_ok if high else south_ok, picked, 0.0)

    def coriolis_at(lat):
        latitude = (lat + chip * lat_blk).astype(jnp.float32)
        return coriolis_base * (2.0 * (latitude + 0.5) / (chips * lat_blk) - 1.0)

    mix[...] = mix_matrix(rate_mix[...])
    fill_ocean(ocean, got, m0, dv, ntr)
    fill_tracers(turned, got, m0, dv)
    fill_columns(z_in, g_in, got, z0, g0, zd, gd, ntr, lat_blk)
    derive_rows(m0, dv, ntr, 0, rows)
    derive_columns(z0, zd, ntr)
    derive_columns(g0, gd, ntr)
    column_step(z0, g0, zd, gd, z1, mix, coriolis_at(lanes_of((nz, lon)) // WIN - 1), ntr)
    ocean_rows(m0, dv, z0, zd, wts, m1, coriolis_at, ntr, 1, rows - 1)
    tracer_rows(m0, z0, wts, m1, sat, ntr, 1, rows - 1)
    react_rows(dv, mix, m1, sat, ntr, 1, rows - 1)
    light_rows(m0, dv, m1, ntr, 1, rows - 1)
    derive_rows(m1, dv, ntr, 1, rows - 1)
    derive_columns(z1, zd, ntr)
    ocean_rows(m1, dv, z1, zd, wts, m0, coriolis_at, ntr, 2, rows - 2)
    tracer_rows(m1, z1, wts, m0, sat, ntr, 2, rows - 2)
    react_rows(dv, mix, m0, sat, ntr, 2, rows - 2)
    light_rows(m0, dv, m0, ntr, 2, rows - 2)
    write_out(m0, out, ntr)
    half = lat_blk // 2
    for f in range(3):
        keep[f] = m0[ntr + f, pl.ds(2 + place_half * half, half)]
        send[f] = m0[ntr + f, pl.ds(2 + (1 - place_half) * half, half)]


def unpack_kernel(keep, got, flow, temp):
    _, lat_dev, nz, lon = keep.shape
    first = place()[0] == 0
    for t in range(lat_dev):
        for f in range(3):
            a, b = (keep[f, t], got[f, t])
            low, high = (jnp.where(first, a, b), jnp.where(first, b, a))
            if f < 2:
                flow[f, :, t, :lon] = low
                flow[f, :, t, lon:] = high
            else:
                temp[:, t, :lon] = low
                temp[:, t, lon:] = high


def call(kernel, outs, *args, scratch=(), held=None):
    vmem = pl.BlockSpec(memory_space=pltpu.VMEM)
    held = held or [True] * len(args)
    return pl.pallas_call(
        kernel,
        out_shape=[jax.ShapeDtypeStruct(s, jnp.float32) for s in outs],
        in_specs=[vmem if h else pl.BlockSpec(memory_space=pl.ANY) for h in held],
        out_specs=[vmem] * len(outs),
        scratch_shapes=[pltpu.VMEM(s, jnp.float32) if isinstance(s, tuple) else s for s in scratch],
        compiler_params=pltpu.CompilerParams(vmem_limit_bytes=(40 if all(held) else 52) * 2**20),
    )(*args)


def both_ways(pairs):
    return sorted(pairs + [(b, a) for a, b in pairs])


def exchanges(n_row, n_col):
    chips = n_row // 2

    def dev(p, h, c):
        return (2 * p + h) * n_col + c

    partner = [(dev(p, 0, c), dev(p, 1, c)) for p in range(chips) for c in range(n_col)]
    outer = [(dev(p, 1, c), dev(p, 0, c + 1)) for p in range(chips) for c in range(n_col - 1)]
    for p in range(0, chips - 1, 2):
        outer += [(dev(p, 0, 0), dev(p + 1, 0, 0)), (dev(p, 1, n_col - 1), dev(p + 1, 1, n_col - 1))]
    lat_a = [(dev(p, h, c), dev(p + 1, h, c)) for p in range(0, chips - 1, 2) for h in (0, 1) for c in range(n_col)]
    lat_b = [(dev(p, h, c), dev(p + 1, h, c)) for p in range(1, chips - 1, 2) for h in (0, 1) for c in range(n_col)]
    if chips % 2 == 0 and chips > 2:
        lat_b += [(dev(0, h, c), dev(chips - 1, h, c)) for h in (0, 1) for c in range(n_col)]
    return [both_ways(x) for x in (partner, outer, lat_a, lat_b)]


def on_device(n_row, n_col, flow, temp, tracers, bottom, sunlight, rates):
    nz, lat_dev, lon_dev = temp.shape
    _, ntr, _, lat_blk, lon = tracers.shape
    nf = ntr + EXTRA
    partner, outer, lat_a, lat_b = exchanges(n_row, n_col)

    def swap(x, pairs):
        return lax.ppermute(x, ("row", "col"), pairs)

    block = tracers[0]
    parts = [flow.reshape(-1, lat_dev, lon_dev), temp, bottom[None], sunlight[None]]
    total = sum(part.shape[0] for part in parts)
    surface, start = (0.0, 0)
    for part in parts:
        count = part.shape[0]
        surface = surface + jnp.pad(part, ((start, total - start - count), (0, 0), (0, 0))).astype(jnp.float32)
        start += count
    mix = jnp.kron(rates, jnp.eye(nz, dtype=jnp.float32))
    half_shape = (EXTRA, lat_dev, nz, lon)
    mine, other, g_send, g_other, turned = call(
        pack_kernel,
        [half_shape, half_shape, (nf, nz, lon), (EXTRA, nz, lon), (ntr, lat_blk, nz, lon)],
        surface,
        block,
        scratch=[block.shape, pltpu.SemaphoreType.DMA((ntr // GROUP,))],
        held=[True, False],
    )
    got, g_partner = swap((other, g_send), partner)
    ocean, g_own = call(join_kernel, [(EXTRA, lat_blk, nz, lon), (nf, nz, lon)], mine, got, g_send)
    g_outer = swap(g_own, outer)
    edge_shape = (2 * nf + 1, nz, lon)
    z, to_a, to_b = call(
        edge_kernel, [(nf, nz, lon), edge_shape, edge_shape], turned, ocean, g_partner, g_other, g_outer
    )
    got_a, got_b = (swap(to_a, lat_a), swap(to_b, lat_b))
    rows = lat_blk + 4
    cols = (nf, nz, lon)
    third = (3, lat_dev, nz, lon)
    out, keep, send = call(
        steps_kernel,
        [(ntr, nz, lat_blk, lon), third, third],
        turned,
        ocean,
        z,
        g_own,
        got_a,
        got_b,
        mix,
        scratch=[
            (nf, rows, nz, lon),
            (nf, rows, nz, lon),
            (3, rows, nz, lon),
            (7, rows, nz, lon),
            pltpu.VMEM((rows, 2 * ntr * nz, lon), jnp.bfloat16),
            pltpu.VMEM((2 * ntr * nz, 2 * ntr * nz), jnp.bfloat16),
            cols,
            cols,
            cols,
            (3, nz, lon),
            (3, nz, lon),
        ],
    )
    flow_out, temp_out = call(
        unpack_kernel, [(2, nz, lat_dev, lon_dev), (nz, lat_dev, lon_dev)], keep, swap(send, partner)
    )
    return (flow_out, temp_out, out[None])


def solution(mesh):
    in_specs = (
        P(None, None, "row", "col"),
        P(None, "row", "col"),
        P("row", None, None, None, "col"),
        P("row", "col"),
        P("row", "col"),
        P(),
    )
    out_specs = (
        P(None, None, "row", "col"),
        P(None, "row", "col"),
        P("row", None, None, None, "col"),
    )
    return jax.shard_map(
        functools.partial(on_device, mesh.shape["row"], mesh.shape["col"]),
        mesh=mesh,
        in_specs=in_specs,
        out_specs=out_specs,
        check_vma=False,
    )
```

```python
import functools
import jax
import jax.numpy as jnp
from jax import lax
from jax.experimental import pallas as pl
from jax.experimental.pallas import tpu as pltpu
from jax.sharding import PartitionSpec as P

KL = 4
STEPS = 2

time_step = 0.2
viscosity = 0.2
expansion = 0.05
coriolis_base = 0.5
kappa_base = 0.05
kappa_shear = 0.2
react_step = 0.25
water_absorb = 0.1
pigment_absorb = 0.6
heat_gain = 1.0

EXTRA = 4
WIN = 4


def up(x):
    return pltpu.roll(x, 1, x.ndim - 2)


def down(x):
    return pltpu.roll(x, x.shape[-2] - 1, x.ndim - 2)


def lanes_of(shape):
    return lax.broadcasted_iota(jnp.int32, shape, len(shape) - 1)


def levels_of(shape):
    return lax.broadcasted_iota(jnp.int32, shape, len(shape) - 2)


def window(x, lat, into):
    lon = x.shape[1]
    lane = lanes_of(x.shape)
    base = WIN * (lat + 1)
    moved = pltpu.roll(x, (base + 2) % lon, 1)
    return jnp.where((lane >= base) & (lane < base + WIN), moved, into)


def place():
    row = lax.axis_index("row")
    return (row % 2, row // 2, lax.axis_index("col"))


def edge_starts(chip, lat_blk):
    odd = chip % 2
    return ((1 - odd) * (lat_blk - 2), odd * (lat_blk - 2))


def pack_ocean_kernel(surface, mine, to_partner, g_other):
    lat_dev, nz, lon = mine.shape[1:]
    lon_dev = surface.shape[2]
    half, _, _ = place()
    first = half == 0
    zero = jnp.zeros((nz, lon), jnp.float32)
    level = levels_of((nz, lon_dev))
    own = [zero] * EXTRA
    far = [zero] * EXTRA
    for t in range(lat_dev):
        depth = jnp.broadcast_to(surface[3 * nz, t : t + 1, :], (nz, lon_dev))
        light = jnp.broadcast_to(surface[3 * nz + 1, t : t + 1, :], (nz, lon_dev))
        wet = (level.astype(jnp.float32) < depth).astype(jnp.float32)
        aux = jnp.where(level == 0, depth, jnp.where(level == 1, light, 0.0))
        for f, tile in enumerate([surface[f * nz : (f + 1) * nz, t, :] * wet for f in range(3)] + [aux]):
            low, high = (tile[:, :lon], tile[:, lon:])
            a, b = (jnp.where(first, low, high), jnp.where(first, high, low))
            mine[f, t] = a
            to_partner[f * lat_dev + t] = b
            own[f] = window(a, t, own[f])
            far[f] = window(b, t, far[f])
    shift = half * (WIN * lat_dev)
    for f in range(EXTRA):
        to_partner[EXTRA * lat_dev + f] = pltpu.roll(own[f], shift, 1)
        g_other[f] = pltpu.roll(far[f], shift, 1)


def pack_tracers_kernel(tracers_in, turned, g_tracers, tracers, sem):
    ntr, nz, lat_blk, lon = tracers.shape
    copies = [
        pltpu.make_async_copy(tracers_in.at[pl.ds(n, GROUP)], tracers.at[pl.ds(n, GROUP)], sem.at[n // GROUP])
        for n in range(0, ntr, GROUP)
    ]
    for copy in copies:
        copy.start()
    for i, copy in enumerate(copies):
        copy.wait()
        g = [jnp.zeros((nz, lon), jnp.float32)] * GROUP
        for t in range(lat_blk):
            for k in range(GROUP):
                x = tracers[i * GROUP + k, :, t, :]
                turned[i * GROUP + k, t] = x
                g[k] = window(x, t, g[k])
        for k in range(GROUP):
            g_tracers[i * GROUP + k] = g[k]


def in_half(shape, half, lat_dev):
    lane = lanes_of(shape)
    base = WIN * (lat_dev * half + 1)
    return (lane >= base) & (lane < base + WIN * lat_dev)


def join_kernel(mine, got, to_partner, g_tracers, ocean, g_own, to_outer):
    _, lat_dev, nz, lon = mine.shape
    ntr = g_tracers.shape[0]
    nf = ntr + EXTRA
    half, _, _ = place()
    tile = (nz, lon)
    own_lanes = in_half(tile, half, lat_dev)
    shift = (1 - half) * (WIN * lat_dev)
    g_own[:ntr] = g_tracers[...]
    for f in range(EXTRA):
        g = jnp.zeros(tile, jnp.float32)
        for t in range(lat_dev):
            x = got[f * lat_dev + t]
            ocean[f, half * lat_dev + t] = mine[f, t]
            ocean[f, (1 - half) * lat_dev + t] = x
            g = window(x, t, g)
        g_own[ntr + f] = jnp.where(own_lanes, to_partner[EXTRA * lat_dev + f], pltpu.roll(g, shift, 1))
    lane = lanes_of(tile)
    front, near = (lane % WIN < 2, in_half(tile, 0, 2 * lat_dev))
    side = (1 - half) * (lon - 2)
    for i in range(nf // 4):
        a, b, c, d = [pltpu.roll(g_own[4 * i + k], side, 1) for k in range(4)]
        low = jnp.where(front, a, pltpu.roll(b, 2, 1))
        high = jnp.where(front, c, pltpu.roll(d, 2, 1))
        to_outer[i] = jnp.where(near, low, pltpu.roll(high, lon // 2, 1))


def edge_kernel(turned, ocean, g_partner, got, g_other, from_outer, z, to_a, to_b):
    ntr, lat_blk, nz, lon = turned.shape
    nf = ntr + EXTRA
    half, chip, column = place()
    tile = (nz, lon)
    lane = lanes_of(tile)
    own_lanes = in_half(tile, half, lat_blk // 2)
    outer_ok = jnp.where(half == 0, column > 0, column < lax.axis_size("col") - 1)
    from_partner = (lane % WIN < 2).astype(jnp.int32) == half
    outer_lanes = in_half(tile, 0, lat_blk) & outer_ok
    start_a, start_b = edge_starts(chip, lat_blk)
    corner_a = corner_b = jnp.zeros(tile, jnp.float32)
    for f in range(nf):
        if f < ntr:
            partner = g_partner[f]
        else:
            partner = jnp.where(own_lanes, g_other[f - ntr], got[EXTRA * (lat_blk // 2) + f - ntr])
        k = f % 4
        moved = pltpu.roll(from_outer[f // 4], lon + 2 * half - 2 * (k % 2) - lon // 2 * (k // 2), 1)
        cols = jnp.where(from_partner, partner, jnp.where(outer_lanes, moved, 0.0))
        z[f] = cols
        at = (lane >= WIN * f) & (lane < WIN * f + WIN)
        low = pltpu.roll(cols, (WIN * f - WIN) % lon, 1)
        high = pltpu.roll(cols, (WIN * f - WIN * lat_blk) % lon, 1)
        corner_a = jnp.where(at, jnp.where(start_a > 0, high, low), corner_a)
        corner_b = jnp.where(at, jnp.where(start_b > 0, high, low), corner_b)
    for out, start, corner in ((to_a, start_a, corner_a), (to_b, start_b, corner_b)):
        for n in range(ntr):
            out[2 * n : 2 * n + 2] = turned[n, pl.ds(start, 2)]
        for f in range(EXTRA):
            out[2 * (ntr + f) : 2 * (ntr + f) + 2] = ocean[f, pl.ds(start, 2)]
        out[2 * nf] = corner


def kappa_of(u, v):
    du, dv = (u - down(u), v - down(v))
    sq = jnp.where(levels_of(u.shape) < u.shape[-2] - 1, du * du + dv * dv, 0.0)
    return kappa_base + kappa_shear * sq / (1.0 + sq)


def sum_above(x):
    level = levels_of(x.shape)
    k = 1
    while k < x.shape[-2]:
        x = x + jnp.where(level >= k, pltpu.roll(x, k, x.ndim - 2), 0.0)
        k *= 2
    return x


def sum_below(x):
    level, nz = (levels_of(x.shape), x.shape[-2])
    k = 1
    while k < nz:
        x = x + jnp.where(level < nz - k, pltpu.roll(x, nz - k, x.ndim - 2), 0.0)
        k *= 2
    return x


def pressure_of(heat):
    return -expansion * sum_above(heat)


def wet_of(aux):
    depth = jnp.broadcast_to(aux[..., 0:1, :], aux.shape)
    return (levels_of(aux.shape).astype(jnp.float32) < depth).astype(jnp.float32)


def light_of(aux):
    return jnp.broadcast_to(aux[..., 1:2, :], aux.shape)


def dynamics(u, v, wet, kap, prs, coriolis):
    um, ue, uw, un, us = u
    vm, ve, vw, vn, vs = v
    wm, we, ww, wn, ws = wet
    km, ke, kw, kn, ks = kap
    _, pe, pw, pn, ps = prs
    level, nz = (levels_of(um.shape), um.shape[-2])
    oe, ow, on, os_ = (wm * we, wm * ww, wm * wn, wm * ws)
    fe, fw, fn, fs = (0.5 * (um + ue) * oe, 0.5 * (um + uw) * ow, 0.5 * (vm + vn) * on, 0.5 * (vm + vs) * os_)
    ce, cw, cn, cs = (0.5 * (km + ke) * oe, 0.5 * (km + kw) * ow, 0.5 * (km + kn) * on, 0.5 * (km + ks) * os_)
    div = fe - fw + fn - fs
    total = sum_below(div)
    w_top = jnp.where(level >= 1, -total, 0.0)
    w_bot = jnp.where(level < nz - 1, -down(total), 0.0)
    weights = (
        wm * (1.0 - time_step * (ce + cw + cn + cs + 0.5 * (div + w_top - w_bot))),
        time_step * (ce - 0.5 * fe),
        time_step * (cw + 0.5 * fw),
        time_step * (cn - 0.5 * fn),
        time_step * (cs + 0.5 * fs),
        (-0.5 * time_step) * wm * w_top,
        (0.5 * time_step) * wm * w_bot,
    )
    lap_u = oe * (ue - um) + ow * (uw - um) + on * (un - um) + os_ * (us - um)
    lap_v = oe * (ve - vm) + ow * (vw - vm) + on * (vn - vm) + os_ * (vs - vm)
    new_u = wm * (um + time_step * (coriolis * vm - 0.5 * (pe - pw) + viscosity * lap_u))
    new_v = wm * (vm + time_step * (-coriolis * um - 0.5 * (pn - ps) + viscosity * lap_v))
    return (new_u, new_v, weights)


def transport(weights, x, east, west, north, south):
    a0, ae, aw, an, as_, at, ab = weights
    return (a0 * x + ae * east) + (aw * west + an * north) + (as_ * south + at * up(x)) + ab * down(x)


def saturated(x):
    return x * lax.rsqrt(1.0 + x * x)


def absorbed(pigment):
    level = levels_of(pigment.shape)
    sq = pigment * pigment
    depth = water_absorb + pigment_absorb * (sq / (1.0 + sq))
    above = jnp.where(level >= 1, up(depth), 0.0)
    k = 1
    while k < KL:
        above = above + jnp.where(level >= k, pltpu.roll(above, k, above.ndim - 2), 0.0)
        k *= 2
    return jnp.where(level < KL, jnp.exp(-above) * (1.0 - jnp.exp(-depth)), 0.0)


def two_parts(x):
    high = x.astype(jnp.bfloat16)
    return (high, (x - high.astype(jnp.float32)).astype(jnp.bfloat16))


def mix_matrix(rates, nz):
    ntr = rates.shape[0]
    size = ntr * nz
    exact = dict(precision=lax.Precision.HIGHEST, preferred_element_type=jnp.float32)
    spread = lax.broadcasted_iota(jnp.int32, (size, ntr), 0) // nz == lax.broadcasted_iota(jnp.int32, (size, ntr), 1)
    spread = spread.astype(jnp.float32)
    wide = jnp.dot(spread, rates, **exact)
    full = lax.dot_general(wide, spread, (((1,), (1,)), ((), ())), **exact)
    same = lax.broadcasted_iota(jnp.int32, (size, size), 0) % nz == lax.broadcasted_iota(jnp.int32, (size, size), 1) % nz
    high, low = two_parts(jnp.where(same, full, 0.0))
    top = jnp.concatenate([high, high], axis=1)
    return jnp.concatenate([top, jnp.concatenate([low, jnp.zeros_like(low)], axis=1)], axis=0)


def beside(z, r, lon):
    return pltpu.roll(z, lon - 2 - WIN * (r - 1), z.ndim - 1)


def sides(x, edge):
    lane, lon = (lanes_of(x.shape), x.shape[-1])
    west = pltpu.roll(jnp.where(lane == lon - 1, edge, x), 1, x.ndim - 1)
    east = pltpu.roll(jnp.where(lane == 0, edge, x), lon - 1, x.ndim - 1)
    return (east, west)


def around_rows(m, f, z, r, count):
    x = m[f, pl.ds(r, count)]
    edge = jnp.stack([beside(z, r + i, x.shape[-1]) for i in range(count)])
    return (x, *sides(x, edge), m[f, pl.ds(r + 1, count)], m[f, pl.ds(r - 1, count)])


def around_columns(x, own):
    lane, lon = (lanes_of(x.shape), x.shape[-1])
    west = pltpu.roll(jnp.where(lane % WIN == 0, x, own), 1, x.ndim - 1)
    east = pltpu.roll(jnp.where(lane % WIN == WIN - 1, x, own), lon - 1, x.ndim - 1)
    return (x, east, west, pltpu.roll(x, lon - WIN, x.ndim - 1), pltpu.roll(x, WIN, x.ndim - 1))


def coriolis_at(lat, lat_blk):
    _, chip, _ = place()
    latitude = (lat + chip * lat_blk).astype(jnp.float32)
    return coriolis_base * (2.0 * (latitude + 0.5) / (lax.axis_size("row") // 2 * lat_blk) - 1.0)


KAP, PRS, WET = (0, 1, 2)
GROUP = 4


def span(start, stop):
    return (start, stop - start, 1, stop - start)


def chunks(rows, most, body):
    first, apart, times, size = rows
    count = max(k for k in range(1, min(most, size) + 1) if size % k == 0)
    if times == 1:
        apart, times = (count, size // count)
    elif count < size:
        raise ValueError(rows)

    def one(i, _):
        body(first + i * apart, count)
        return 0

    if times == 1:
        body(first, count)
    else:
        lax.fori_loop(0, times, one, 0)


def derive_rows(m, dv, ntr, rows):
    def body(r, count):
        at = pl.ds(r, count)
        dv[KAP, at] = kappa_of(m[ntr, at], m[ntr + 1, at])
        dv[PRS, at] = pressure_of(m[ntr + 2, at])

    chunks(rows, 10, body)


def derive_columns(z, zd, ntr):
    zd[KAP] = kappa_of(z[ntr], z[ntr + 1])
    zd[PRS] = pressure_of(z[ntr + 2])


def ocean_rows(m, dv, z, zd, wts, new, ntr, rows):
    def body(r, count):
        at = pl.ds(r, count)
        lat = lax.broadcasted_iota(jnp.int32, (count, *m.shape[2:]), 0) + (r - 2)
        new_u, new_v, weights = dynamics(
            around_rows(m, ntr, z[ntr], r, count),
            around_rows(m, ntr + 1, z[ntr + 1], r, count),
            around_rows(dv, WET, zd[WET], r, count),
            around_rows(dv, KAP, zd[KAP], r, count),
            around_rows(dv, PRS, zd[PRS], r, count),
            coriolis_at(lat, m.shape[1] - 4),
        )
        new[ntr, at] = new_u
        new[ntr + 1, at] = new_v
        for i, w in enumerate(weights):
            wts[i, at] = w

    chunks(rows, 9, body)


def tracer_rows(m, z, wts, new, sat, ntr, rows):
    nz, lon = m.shape[2:]
    half = ntr * nz

    def row(r):
        weights = [wts[i, r] for i in range(7)]
        for n in range(0, ntr, GROUP):
            x = m[n : n + GROUP, r]
            edge = beside(z[n : n + GROUP], r, lon)
            moved = transport(weights, x, *sides(x, edge), m[n : n + GROUP, r + 1], m[n : n + GROUP, r - 1])
            new[n : n + GROUP, r] = moved
            high, low = two_parts(saturated(moved).reshape(GROUP * nz, lon))
            sat[r, n * nz : (n + GROUP) * nz, :] = high
            sat[r, half + n * nz : half + (n + GROUP) * nz, :] = low
        h = ntr + 2
        x = m[h, r]
        new[h, r] = transport(weights, x, *sides(x, beside(z[h], r, lon)), m[h, r + 1], m[h, r - 1])

    def body(r, count):
        for i in range(count):
            row(r + i)

    chunks(rows, 3, body)


def react_rows(dv, mix, new, sat, ntr, rows):
    nz, lon = new.shape[2:]
    half = ntr * nz
    first, apart, times, size = rows
    every = [first + i * apart + k for i in range(times) for k in range(size)]
    both = jnp.concatenate([sat[r] for r in every], axis=1)
    res = jnp.dot(mix[...], both, preferred_element_type=jnp.float32)
    res = res[:half] + res[half:]
    for i, r in enumerate(every):
        gain = react_step * dv[WET, r]
        for n in range(ntr):
            new[n, r] = new[n, r] + gain * res[n * nz : (n + 1) * nz, i * lon : (i + 1) * lon]


def light_rows(m, dv, new, ntr, rows):
    def body(r, count):
        at = pl.ds(r, count)
        new[ntr + 2, at] += heat_gain * light_of(m[ntr + 3, at]) * dv[WET, at] * absorbed(new[0, at])

    chunks(rows, 9, body)


def column_step(z0, g0, zd, gd, z1, mix, ntr, lat_blk):
    nz, lon = z0.shape[1:]
    half = ntr * nz
    wet = zd[WET]
    new_u, new_v, weights = dynamics(
        around_columns(z0[ntr], g0[ntr]),
        around_columns(z0[ntr + 1], g0[ntr + 1]),
        around_columns(wet, gd[WET]),
        around_columns(zd[KAP], gd[KAP]),
        around_columns(zd[PRS], gd[PRS]),
        coriolis_at(lanes_of((nz, lon)) // WIN - 1, lat_blk),
    )
    moved = transport(weights, *around_columns(z0[:ntr], g0[:ntr]))
    high, low = two_parts(saturated(moved).reshape(half, lon))
    res = jnp.dot(mix[...], jnp.concatenate([high, low], axis=0), preferred_element_type=jnp.float32)
    done = moved + (react_step * wet) * (res[:half] + res[half:]).reshape(ntr, nz, lon)
    z1[:ntr] = done
    z1[ntr] = new_u
    z1[ntr + 1] = new_v
    heat = transport(weights, *around_columns(z0[ntr + 2], g0[ntr + 2]))
    z1[ntr + 2] = heat + heat_gain * light_of(z0[ntr + 3]) * wet * absorbed(done[0])


def fill_kernel(turned, ocean, g_own, rates, m0, dv, mix, g0, gd):
    ntr, lat_blk, nz, _ = turned.shape
    mix[...] = mix_matrix(rates[...], nz)
    own = span(2, lat_blk + 2)

    def wets(r, count):
        at = pl.ds(r, count)
        for f in range(EXTRA):
            m0[ntr + f, at] = ocean[f, pl.ds(r - 2, count)]
        dv[WET, at] = wet_of(ocean[EXTRA - 1, pl.ds(r - 2, count)])

    chunks(own, 8, wets)

    def some(r, count):
        wet = dv[WET, r]
        for n in range(ntr):
            m0[n, r] = turned[n, r - 2] * wet

    chunks(own, 1, some)
    derive_rows(m0, dv, ntr, own)
    mask_columns([g_own[f] for f in range(ntr + EXTRA)], g0, gd)


def mask_columns(fields, z, zd):
    ntr = len(fields) - EXTRA
    wet = wet_of(fields[-1])
    zd[WET] = wet
    for f, cols in enumerate(fields):
        z[f] = cols * wet if f < ntr else cols
    derive_columns(z, zd, ntr)


def inner_kernel(m0, dv, mix, g0, gd, z_in, m1, m2, dv1, wts, sat, z0, z1, zd):
    nf, rows, _, _ = m0.shape
    ntr = nf - EXTRA
    mask_columns([z_in[f] for f in range(nf)], z0, zd)
    column_step(z0, g0, zd, gd, z1, mix, ntr, rows - 4)
    now = span(3, rows - 3)
    ocean_rows(m0, dv, z0, zd, wts, m1, ntr, now)
    tracer_rows(m0, z0, wts, m1, sat, ntr, now)
    react_rows(dv, mix, m1, sat, ntr, now)
    light_rows(m0, dv, m1, ntr, now)
    dv1[WET, 3 : rows - 3] = dv[WET, 3 : rows - 3]
    derive_rows(m1, dv1, ntr, now)
    derive_columns(z1, zd, ntr)
    now = span(4, rows - 4)
    ocean_rows(m1, dv1, z1, zd, wts, m2, ntr, now)
    tracer_rows(m1, z1, wts, m2, sat, ntr, now)
    react_rows(dv1, mix, m2, sat, ntr, now)
    light_rows(m0, dv1, m2, ntr, now)


def outer_kernel(m_own, dv_own, mix, g0, gd, z_in, got_a, got_b, m1_in, m2_in, rim, keep, send, m0, m1, dv0, dv1, wts, sat, z0, z1, zd):
    nf, rows, nz, lon = m_own.shape
    ntr = nf - EXTRA
    lat_blk = rows - 4
    half, chip, _ = place()
    even = chip % 2 == 0
    south_ok, north_ok = (chip > 0, chip < lax.axis_size("row") // 2 - 1)

    def got(high, index):
        a, b = (got_a[index], got_b[index])
        picked = jnp.where(even, a, b) if high else jnp.where(even, b, a)
        return jnp.where(north_ok if high else south_ok, picked, 0.0)

    for high, start in ((False, 0), (True, rows - 2)):
        for f in range(EXTRA):
            m0[ntr + f, start : start + 2] = got(high, pl.ds(2 * (ntr + f), 2))
        wet = wet_of(m0[nf - 1, start : start + 2])
        dv0[WET, start : start + 2] = wet
        for n in range(ntr):
            m0[n, start : start + 2] = got(high, pl.ds(2 * n, 2)) * wet
        derive_rows(m0, dv0, ntr, span(start, start + 2))
    for start in (2, rows - 4):
        m0[:, start : start + 2] = m_own[:, start : start + 2]
        dv0[:, start : start + 2] = dv_own[:, start : start + 2]
    lane = lanes_of((nz, lon))
    low, high = (got(False, 2 * nf), got(True, 2 * nf))
    at_low, at_high = (lane < WIN, (lane >= WIN * (lat_blk + 1)) & (lane < WIN * (lat_blk + 2)))
    fields = []
    for f in range(nf):
        cols = jnp.where(at_low, pltpu.roll(low, (-WIN * f) % lon, 1), z_in[f])
        fields.append(jnp.where(at_high, pltpu.roll(high, (WIN * (lat_blk + 1) - WIN * f) % lon, 1), cols))
    mask_columns(fields, z0, zd)
    column_step(z0, g0, zd, gd, z1, mix, ntr, lat_blk)
    now = (1, lat_blk, 2, 2)
    ocean_rows(m0, dv0, z0, zd, wts, m1, ntr, now)
    tracer_rows(m0, z0, wts, m1, sat, ntr, now)
    react_rows(dv0, mix, m1, sat, ntr, now)
    light_rows(m0, dv0, m1, ntr, now)
    for start in (3, rows - 5):
        m1[:, start : start + 2] = m1_in[:, start : start + 2]
    for start in (1, rows - 3):
        dv1[WET, start : start + 2] = dv0[WET, start : start + 2]
    for start in (3, rows - 5):
        dv1[WET, start : start + 2] = dv_own[WET, start : start + 2]
    derive_rows(m1, dv1, ntr, (1, rows - 6, 2, 4))
    derive_columns(z1, zd, ntr)
    now = (2, rows - 6, 2, 2)
    ocean_rows(m1, dv1, z1, zd, wts, m0, ntr, now)
    tracer_rows(m1, z1, wts, m0, sat, ntr, now)
    react_rows(dv1, mix, m0, sat, ntr, now)
    light_rows(m0, dv1, m0, ntr, now)

    rim[:, 0:2] = m0[:ntr, 2:4]
    rim[:, 2:4] = m0[:ntr, rows - 4 : rows - 2]
    m0[ntr : ntr + 3, 4 : rows - 4] = m2_in[ntr : ntr + 3, 4 : rows - 4]
    count = lat_blk // 2
    for f in range(3):
        keep[f] = m0[ntr + f, pl.ds(2 + half * count, count)]
        send[f] = m0[ntr + f, pl.ds(2 + (1 - half) * count, count)]


def write_kernel(rim, m, out, block, sem):
    ntr, nz, lat_blk, lon = block.shape
    copies = []
    for n in range(0, ntr, GROUP):
        for k in range(n, n + GROUP):
            for t in range(lat_blk):
                edge = {0: 0, 1: 1, lat_blk - 2: 2, lat_blk - 1: 3}.get(t)
                block[k, :, t, :] = m[k, t + 2] if edge is None else rim[k, edge]
        copy = pltpu.make_async_copy(block.at[pl.ds(n, GROUP)], out.at[pl.ds(n, GROUP)], sem.at[n // GROUP])
        copy.start()
        copies.append(copy)
    for copy in copies:
        copy.wait()


def unpack_kernel(keep, got, flow, temp):
    _, lat_dev, nz, lon = keep.shape
    first = place()[0] == 0
    for t in range(lat_dev):
        for f in range(3):
            a, b = (keep[f, t], got[f, t])
            low, high = (jnp.where(first, a, b), jnp.where(first, b, a))
            if f < 2:
                flow[f, :, t, :lon] = low
                flow[f, :, t, lon:] = high
            else:
                temp[:, t, :lon] = low
                temp[:, t, lon:] = high


def call(kernel, outs, *args, scratch=(), held=True, away=False, limit=40):
    vmem = pl.BlockSpec(memory_space=pltpu.VMEM)
    return pl.pallas_call(
        kernel,
        out_shape=[jax.ShapeDtypeStruct(s, jnp.float32) if isinstance(s, tuple) else s for s in outs],
        in_specs=[vmem if held else pl.BlockSpec(memory_space=pl.ANY)] * len(args),
        out_specs=[pl.BlockSpec(memory_space=pl.ANY) if away else vmem] * len(outs),
        scratch_shapes=[pltpu.VMEM(s, jnp.float32) if isinstance(s, tuple) else s for s in scratch],
        compiler_params=pltpu.CompilerParams(vmem_limit_bytes=limit * 2**20),
    )(*args)


def both_ways(pairs):
    return sorted(pairs + [(b, a) for a, b in pairs])


def exchanges(n_row, n_col):
    chips = n_row // 2

    def dev(p, h, c):
        return (2 * p + h) * n_col + c

    partner = [(dev(p, 0, c), dev(p, 1, c)) for p in range(chips) for c in range(n_col)]
    outer = [(dev(p, 1, c), dev(p, 0, c + 1)) for p in range(chips) for c in range(n_col - 1)]
    outer += [(dev(p, 0, 0), dev(p, 1, n_col - 1)) for p in range(chips)]
    lat_a = [(dev(p, h, c), dev(p + 1, h, c)) for p in range(0, chips - 1, 2) for h in (0, 1) for c in range(n_col)]
    lat_b = [(dev(p, h, c), dev(p + 1, h, c)) for p in range(1, chips - 1, 2) for h in (0, 1) for c in range(n_col)]
    if chips % 2 == 0 and chips > 2:
        lat_b += [(dev(0, h, c), dev(chips - 1, h, c)) for h in (0, 1) for c in range(n_col)]
    return [both_ways(x) for x in (partner, outer, lat_a, lat_b)]


def on_device(n_row, n_col, flow, temp, tracers, bottom, sunlight, rates):
    nz, lat_dev, lon_dev = temp.shape
    _, ntr, _, lat_blk, lon = tracers.shape
    nf = ntr + EXTRA
    partner, outer, lat_a, lat_b = exchanges(n_row, n_col)

    def swap(x, pairs):
        return lax.ppermute(x, ("row", "col"), pairs)

    block = tracers[0]
    parts = [flow.reshape(-1, lat_dev, lon_dev), temp, bottom[None], sunlight[None]]
    total = sum(part.shape[0] for part in parts)
    surface, start = (0.0, 0)
    for part in parts:
        count = part.shape[0]
        surface = surface + jnp.pad(part, ((start, total - start - count), (0, 0), (0, 0))).astype(jnp.float32)
        start += count
    rows = lat_blk + 4
    cols, extra, some = ((nf, nz, lon), (EXTRA, nz, lon), (3, nz, lon))
    copies = pltpu.SemaphoreType.DMA((ntr // GROUP,))
    sent = (EXTRA * (lat_dev + 1), nz, lon)
    mine, to_partner, g_other = call(pack_ocean_kernel, [(EXTRA, lat_dev, nz, lon), sent, extra], surface)
    got = swap(to_partner, partner)
    turned, g_tracers = call(
        pack_tracers_kernel,
        [(ntr, lat_blk, nz, lon), (ntr, nz, lon)],
        block,
        scratch=[block.shape, copies],
        held=False,
        limit=52,
    )
    ocean, g_own, to_outer = call(
        join_kernel, [(EXTRA, lat_blk, nz, lon), cols, (nf // 4, nz, lon)], mine, got, to_partner, g_tracers
    )
    from_outer = swap(to_outer, outer)
    g_partner = swap(g_tracers, partner)
    full, derived = ((nf, rows, nz, lon), (3, rows, nz, lon))
    m0, dv, mix, g0, gd = call(
        fill_kernel,
        [full, derived, jax.ShapeDtypeStruct((2 * ntr * nz, 2 * ntr * nz), jnp.bfloat16), cols, some],
        turned,
        ocean,
        g_own,
        rates,
    )
    edge = (2 * nf + 1, nz, lon)
    z, to_a, to_b = call(edge_kernel, [cols, edge, edge], turned, ocean, g_partner, got, g_other, from_outer)
    got_a, got_b = (swap(to_a, lat_a), swap(to_b, lat_b))
    work = [(7, rows, nz, lon), pltpu.VMEM((rows, 2 * ntr * nz, lon), jnp.bfloat16), cols, cols, some]
    m1, m2 = call(inner_kernel, [full, full], m0, dv, mix, g0, gd, z, scratch=[derived] + work)
    third = (3, lat_dev, nz, lon)
    rim, keep, send = call(
        outer_kernel,
        [(ntr, 4, nz, lon), third, third],
        m0,
        dv,
        mix,
        g0,
        gd,
        z,
        got_a,
        got_b,
        m1,
        m2,
        scratch=[full, full, derived, derived] + work,
    )
    returned = swap(send, partner)
    (out,) = call(write_kernel, [(ntr, nz, lat_blk, lon)], rim, m2, scratch=[(ntr, nz, lat_blk, lon), copies], away=True)
    flow_out, temp_out = call(
        unpack_kernel, [(2, nz, lat_dev, lon_dev), (nz, lat_dev, lon_dev)], keep, returned
    )
    return (flow_out, temp_out, out[None])


def solution(mesh):
    in_specs = (
        P(None, None, "row", "col"),
        P(None, "row", "col"),
        P("row", None, None, None, "col"),
        P("row", "col"),
        P("row", "col"),
        P(),
    )
    out_specs = (
        P(None, None, "row", "col"),
        P(None, "row", "col"),
        P("row", None, None, None, "col"),
    )
    return jax.shard_map(
        functools.partial(on_device, mesh.shape["row"], mesh.shape["col"]),
        mesh=mesh,
        in_specs=in_specs,
        out_specs=out_specs,
        check_vma=False,
    )
```

```python
import functools
import jax
import jax.numpy as jnp
from jax import lax
from jax.experimental import pallas as pl
from jax.experimental.pallas import tpu as pltpu
from jax.sharding import PartitionSpec as P

KL = 4
STEPS = 2

time_step = 0.2
viscosity = 0.2
expansion = 0.05
coriolis_base = 0.5
kappa_base = 0.05
kappa_shear = 0.2
react_step = 0.25
water_absorb = 0.1
pigment_absorb = 0.6
heat_gain = 1.0

EXTRA = 4
WIN = 4


def up(x):
    return pltpu.roll(x, 1, x.ndim - 2)


def down(x):
    return pltpu.roll(x, x.shape[-2] - 1, x.ndim - 2)


def lanes_of(shape):
    return lax.broadcasted_iota(jnp.int32, shape, len(shape) - 1)


def levels_of(shape):
    return lax.broadcasted_iota(jnp.int32, shape, len(shape) - 2)


def window(x, lat, into):
    lon = x.shape[1]
    lane = lanes_of(x.shape)
    base = WIN * (lat + 1)
    moved = pltpu.roll(x, (base + 2) % lon, 1)
    return jnp.where((lane >= base) & (lane < base + WIN), moved, into)


def place():
    row = lax.axis_index("row")
    return (row % 2, row // 2, lax.axis_index("col"))


def edge_starts(chip, lat_blk):
    odd = chip % 2
    return ((1 - odd) * (lat_blk - 2), odd * (lat_blk - 2))


def pack_ocean_kernel(surface, mine, to_partner, g_other):
    lat_dev, nz, lon = mine.shape[1:]
    lon_dev = surface.shape[2]
    half, _, _ = place()
    first = half == 0
    zero = jnp.zeros((nz, lon), jnp.float32)
    level = levels_of((nz, lon_dev))
    own = [zero] * EXTRA
    far = [zero] * EXTRA
    for t in range(lat_dev):
        depth = jnp.broadcast_to(surface[3 * nz, t : t + 1, :], (nz, lon_dev))
        light = jnp.broadcast_to(surface[3 * nz + 1, t : t + 1, :], (nz, lon_dev))
        wet = (level.astype(jnp.float32) < depth).astype(jnp.float32)
        aux = jnp.where(level == 0, depth, jnp.where(level == 1, light, 0.0))
        for f, tile in enumerate([surface[f * nz : (f + 1) * nz, t, :] * wet for f in range(3)] + [aux]):
            low, high = (tile[:, :lon], tile[:, lon:])
            a, b = (jnp.where(first, low, high), jnp.where(first, high, low))
            mine[f, t] = a
            to_partner[f * lat_dev + t] = b
            own[f] = window(a, t, own[f])
            far[f] = window(b, t, far[f])
    shift = half * (WIN * lat_dev)
    for f in range(EXTRA):
        to_partner[EXTRA * lat_dev + f] = pltpu.roll(own[f], shift, 1)
        g_other[f] = pltpu.roll(far[f], shift, 1)


def pack_tracers_kernel(tracers_in, turned, g_tracers, tracers, sem):
    ntr, nz, lat_blk, lon = tracers.shape
    copies = [
        pltpu.make_async_copy(tracers_in.at[pl.ds(n, GROUP)], tracers.at[pl.ds(n, GROUP)], sem.at[n // GROUP])
        for n in range(0, ntr, GROUP)
    ]
    for copy in copies:
        copy.start()
    for i, copy in enumerate(copies):
        copy.wait()
        g = [jnp.zeros((nz, lon), jnp.float32)] * GROUP
        for t in range(lat_blk):
            for k in range(GROUP):
                x = tracers[i * GROUP + k, :, t, :]
                turned[i * GROUP + k, t] = x
                g[k] = window(x, t, g[k])
        for k in range(GROUP):
            g_tracers[i * GROUP + k] = g[k]


def in_half(shape, half, lat_dev):
    lane = lanes_of(shape)
    base = WIN * (lat_dev * half + 1)
    return (lane >= base) & (lane < base + WIN * lat_dev)


def join_kernel(mine, got, to_partner, g_tracers, ocean, g_own, to_outer):
    _, lat_dev, nz, lon = mine.shape
    ntr = g_tracers.shape[0]
    nf = ntr + EXTRA
    half, _, _ = place()
    tile = (nz, lon)
    own_lanes = in_half(tile, half, lat_dev)
    shift = (1 - half) * (WIN * lat_dev)
    g_own[:ntr] = g_tracers[...]
    for f in range(EXTRA):
        g = jnp.zeros(tile, jnp.float32)
        for t in range(lat_dev):
            x = got[f * lat_dev + t]
            ocean[f, half * lat_dev + t] = mine[f, t]
            ocean[f, (1 - half) * lat_dev + t] = x
            g = window(x, t, g)
        g_own[ntr + f] = jnp.where(own_lanes, to_partner[EXTRA * lat_dev + f], pltpu.roll(g, shift, 1))
    lane = lanes_of(tile)
    front, near = (lane % WIN < 2, in_half(tile, 0, 2 * lat_dev))
    side = (1 - half) * (lon - 2)
    for i in range(nf // 4):
        a, b, c, d = [pltpu.roll(g_own[4 * i + k], side, 1) for k in range(4)]
        low = jnp.where(front, a, pltpu.roll(b, 2, 1))
        high = jnp.where(front, c, pltpu.roll(d, 2, 1))
        to_outer[i] = jnp.where(near, low, pltpu.roll(high, lon // 2, 1))


def edge_kernel(lat_blk, inner, from_outer, z, to_a, to_b):
    nf, nz, lon = z.shape

    half, chip, column = place()
    tile = (nz, lon)
    lane = lanes_of(tile)
    outer_ok = jnp.where(half == 0, column > 0, column < lax.axis_size("col") - 1)
    from_partner = (lane % WIN < 2).astype(jnp.int32) == half
    outer_lanes = in_half(tile, 0, lat_blk) & outer_ok
    start_a, start_b = edge_starts(chip, lat_blk)
    corner_a = corner_b = jnp.zeros(tile, jnp.float32)
    for f in range(nf):
        k = f % 4
        moved = pltpu.roll(from_outer[f // 4], lon + 2 * half - 2 * (k % 2) - lon // 2 * (k // 2), 1)
        cols = jnp.where(from_partner, inner[f], jnp.where(outer_lanes, moved, 0.0))
        z[f] = cols
        at = (lane >= WIN * f) & (lane < WIN * f + WIN)
        low = pltpu.roll(cols, (WIN * f - WIN) % lon, 1)
        high = pltpu.roll(cols, (WIN * f - WIN * lat_blk) % lon, 1)
        corner_a = jnp.where(at, jnp.where(start_a > 0, high, low), corner_a)
        corner_b = jnp.where(at, jnp.where(start_b > 0, high, low), corner_b)
    to_a[...] = corner_a
    to_b[...] = corner_b


def kappa_of(u, v):
    du, dv = (u - down(u), v - down(v))
    sq = jnp.where(levels_of(u.shape) < u.shape[-2] - 1, du * du + dv * dv, 0.0)
    return kappa_base + kappa_shear * sq / (1.0 + sq)


def sum_above(x):
    level = levels_of(x.shape)
    k = 1
    while k < x.shape[-2]:
        x = x + jnp.where(level >= k, pltpu.roll(x, k, x.ndim - 2), 0.0)
        k *= 2
    return x


def sum_below(x):
    level, nz = (levels_of(x.shape), x.shape[-2])
    k = 1
    while k < nz:
        x = x + jnp.where(level < nz - k, pltpu.roll(x, nz - k, x.ndim - 2), 0.0)
        k *= 2
    return x


def pressure_of(heat):
    return -expansion * sum_above(heat)


def wet_of(aux):
    depth = jnp.broadcast_to(aux[..., 0:1, :], aux.shape)
    return (levels_of(aux.shape).astype(jnp.float32) < depth).astype(jnp.float32)


def light_of(aux):
    return jnp.broadcast_to(aux[..., 1:2, :], aux.shape)


def dynamics(u, v, wet, kap, prs, coriolis):
    um, ue, uw, un, us = u
    vm, ve, vw, vn, vs = v
    wm, we, ww, wn, ws = wet
    km, ke, kw, kn, ks = kap
    _, pe, pw, pn, ps = prs
    level, nz = (levels_of(um.shape), um.shape[-2])
    oe, ow, on, os_ = (wm * we, wm * ww, wm * wn, wm * ws)
    fe, fw, fn, fs = (0.5 * (um + ue) * oe, 0.5 * (um + uw) * ow, 0.5 * (vm + vn) * on, 0.5 * (vm + vs) * os_)
    ce, cw, cn, cs = (0.5 * (km + ke) * oe, 0.5 * (km + kw) * ow, 0.5 * (km + kn) * on, 0.5 * (km + ks) * os_)
    div = fe - fw + fn - fs
    total = sum_below(div)
    w_top = jnp.where(level >= 1, -total, 0.0)
    w_bot = jnp.where(level < nz - 1, -down(total), 0.0)
    weights = (
        wm * (1.0 - time_step * (ce + cw + cn + cs + 0.5 * (div + w_top - w_bot))),
        time_step * (ce - 0.5 * fe),
        time_step * (cw + 0.5 * fw),
        time_step * (cn - 0.5 * fn),
        time_step * (cs + 0.5 * fs),
        (-0.5 * time_step) * wm * w_top,
        (0.5 * time_step) * wm * w_bot,
    )
    lap_u = oe * (ue - um) + ow * (uw - um) + on * (un - um) + os_ * (us - um)
    lap_v = oe * (ve - vm) + ow * (vw - vm) + on * (vn - vm) + os_ * (vs - vm)
    new_u = wm * (um + time_step * (coriolis * vm - 0.5 * (pe - pw) + viscosity * lap_u))
    new_v = wm * (vm + time_step * (-coriolis * um - 0.5 * (pn - ps) + viscosity * lap_v))
    return (new_u, new_v, weights)


def transport(weights, x, east, west, north, south):
    a0, ae, aw, an, as_, at, ab = weights
    return (a0 * x + ae * east) + (aw * west + an * north) + (as_ * south + at * up(x)) + ab * down(x)


def saturated(x):
    return x * lax.rsqrt(1.0 + x * x)


def absorbed(pigment):
    level = levels_of(pigment.shape)
    sq = pigment * pigment
    depth = water_absorb + pigment_absorb * (sq / (1.0 + sq))
    above = jnp.where(level >= 1, up(depth), 0.0)
    k = 1
    while k < KL:
        above = above + jnp.where(level >= k, pltpu.roll(above, k, above.ndim - 2), 0.0)
        k *= 2
    return jnp.where(level < KL, jnp.exp(-above) * (1.0 - jnp.exp(-depth)), 0.0)


def two_parts(x):
    high = x.astype(jnp.bfloat16)
    return (high, (x - high.astype(jnp.float32)).astype(jnp.bfloat16))


def mix_matrix(rates, nz):
    ntr = rates.shape[0]
    size = ntr * nz
    exact = dict(precision=lax.Precision.HIGHEST, preferred_element_type=jnp.float32)
    spread = lax.broadcasted_iota(jnp.int32, (size, ntr), 0) // nz == lax.broadcasted_iota(jnp.int32, (size, ntr), 1)
    spread = spread.astype(jnp.float32)
    wide = jnp.dot(spread, rates, **exact)
    full = lax.dot_general(wide, spread, (((1,), (1,)), ((), ())), **exact)
    same = lax.broadcasted_iota(jnp.int32, (size, size), 0) % nz == lax.broadcasted_iota(jnp.int32, (size, size), 1) % nz
    high, low = two_parts(jnp.where(same, full, 0.0))
    top = jnp.concatenate([high, high], axis=1)
    return jnp.concatenate([top, jnp.concatenate([low, jnp.zeros_like(low)], axis=1)], axis=0)


def beside(z, r, lon):
    return pltpu.roll(z, lon - 2 - WIN * (r - 1), z.ndim - 1)


def sides(x, edge):
    lane, lon = (lanes_of(x.shape), x.shape[-1])
    west = pltpu.roll(jnp.where(lane == lon - 1, edge, x), 1, x.ndim - 1)
    east = pltpu.roll(jnp.where(lane == 0, edge, x), lon - 1, x.ndim - 1)
    return (east, west)


def around_rows(m, f, z, r, count):
    x = m[f, pl.ds(r, count)]
    edge = jnp.stack([beside(z, r + i, x.shape[-1]) for i in range(count)])
    return (x, *sides(x, edge), m[f, pl.ds(r + 1, count)], m[f, pl.ds(r - 1, count)])


def around_columns(x, own):
    lane, lon = (lanes_of(x.shape), x.shape[-1])
    west = pltpu.roll(jnp.where(lane % WIN == 0, x, own), 1, x.ndim - 1)
    east = pltpu.roll(jnp.where(lane % WIN == WIN - 1, x, own), lon - 1, x.ndim - 1)
    return (x, east, west, pltpu.roll(x, lon - WIN, x.ndim - 1), pltpu.roll(x, WIN, x.ndim - 1))


def coriolis_at(lat, lat_blk):
    _, chip, _ = place()
    latitude = (lat + chip * lat_blk).astype(jnp.float32)
    return coriolis_base * (2.0 * (latitude + 0.5) / (lax.axis_size("row") // 2 * lat_blk) - 1.0)


KAP, PRS, WET = (0, 1, 2)
GROUP = 4


def span(start, stop):
    return (start, stop - start, 1, stop - start)


def chunks(rows, most, body):
    first, apart, times, size = rows
    count = max(k for k in range(1, min(most, size) + 1) if size % k == 0)
    if times == 1:
        apart, times = (count, size // count)
    elif count < size:
        raise ValueError(rows)

    def one(i, _):
        body(first + i * apart, count)
        return 0

    if times == 1:
        body(first, count)
    else:
        lax.fori_loop(0, times, one, 0)


def derive_rows(m, dv, ntr, rows):
    def body(r, count):
        at = pl.ds(r, count)
        dv[KAP, at] = kappa_of(m[ntr, at], m[ntr + 1, at])
        dv[PRS, at] = pressure_of(m[ntr + 2, at])

    chunks(rows, 10, body)


def derive_columns(z, zd, ntr):
    zd[KAP] = kappa_of(z[ntr], z[ntr + 1])
    zd[PRS] = pressure_of(z[ntr + 2])


def ocean_rows(m, dv, z, zd, wts, new, ntr, rows):
    def body(r, count):
        at = pl.ds(r, count)
        lat = lax.broadcasted_iota(jnp.int32, (count, *m.shape[2:]), 0) + (r - 2)
        new_u, new_v, weights = dynamics(
            around_rows(m, ntr, z[ntr], r, count),
            around_rows(m, ntr + 1, z[ntr + 1], r, count),
            around_rows(dv, WET, zd[WET], r, count),
            around_rows(dv, KAP, zd[KAP], r, count),
            around_rows(dv, PRS, zd[PRS], r, count),
            coriolis_at(lat, m.shape[1] - 4),
        )
        new[ntr, at] = new_u
        new[ntr + 1, at] = new_v
        for i, w in enumerate(weights):
            wts[i, at] = w

    chunks(rows, 9, body)


def tracer_rows(m, z, wts, new, sat, ntr, rows):
    nz, lon = m.shape[2:]
    half = ntr * nz

    def row(r):
        weights = [wts[i, r] for i in range(7)]
        for n in range(0, ntr, GROUP):
            x = m[n : n + GROUP, r]
            edge = beside(z[n : n + GROUP], r, lon)
            moved = transport(weights, x, *sides(x, edge), m[n : n + GROUP, r + 1], m[n : n + GROUP, r - 1])
            new[n : n + GROUP, r] = moved
            high, low = two_parts(saturated(moved).reshape(GROUP * nz, lon))
            sat[r, n * nz : (n + GROUP) * nz, :] = high
            sat[r, half + n * nz : half + (n + GROUP) * nz, :] = low
        h = ntr + 2
        x = m[h, r]
        new[h, r] = transport(weights, x, *sides(x, beside(z[h], r, lon)), m[h, r + 1], m[h, r - 1])

    def body(r, count):
        for i in range(count):
            row(r + i)

    chunks(rows, 3, body)


def react_rows(dv, mix, new, sat, ntr, rows):
    nz, lon = new.shape[2:]
    half = ntr * nz
    first, apart, times, size = rows
    every = [first + i * apart + k for i in range(times) for k in range(size)]
    both = jnp.concatenate([sat[r] for r in every], axis=1)
    res = jnp.dot(mix[...], both, preferred_element_type=jnp.float32)
    res = res[:half] + res[half:]
    for i, r in enumerate(every):
        gain = react_step * dv[WET, r]
        for n in range(ntr):
            new[n, r] = new[n, r] + gain * res[n * nz : (n + 1) * nz, i * lon : (i + 1) * lon]


def light_rows(m, dv, new, ntr, rows):
    def body(r, count):
        at = pl.ds(r, count)
        new[ntr + 2, at] += heat_gain * light_of(m[ntr + 3, at]) * dv[WET, at] * absorbed(new[0, at])

    chunks(rows, 9, body)


def column_step(z0, g0, zd, gd, z1, mix, ntr, lat_blk):
    nz, lon = z0.shape[1:]
    half = ntr * nz
    wet = zd[WET]
    new_u, new_v, weights = dynamics(
        around_columns(z0[ntr], g0[ntr]),
        around_columns(z0[ntr + 1], g0[ntr + 1]),
        around_columns(wet, gd[WET]),
        around_columns(zd[KAP], gd[KAP]),
        around_columns(zd[PRS], gd[PRS]),
        coriolis_at(lanes_of((nz, lon)) // WIN - 1, lat_blk),
    )
    moved = transport(weights, *around_columns(z0[:ntr], g0[:ntr]))
    high, low = two_parts(saturated(moved).reshape(half, lon))
    res = jnp.dot(mix[...], jnp.concatenate([high, low], axis=0), preferred_element_type=jnp.float32)
    done = moved + (react_step * wet) * (res[:half] + res[half:]).reshape(ntr, nz, lon)
    z1[:ntr] = done
    z1[ntr] = new_u
    z1[ntr + 1] = new_v
    heat = transport(weights, *around_columns(z0[ntr + 2], g0[ntr + 2]))
    z1[ntr + 2] = heat + heat_gain * light_of(z0[ntr + 3]) * wet * absorbed(done[0])


def fill_kernel(turned, ocean, g_own, g_partner, got, g_other, rates, rows_a, rows_b, m0, dv, mix, g0, gd, inner):
    ntr, lat_blk, nz, lon = turned.shape
    half, chip, _ = place()
    inner[:ntr] = g_partner[...]
    for f in range(EXTRA):
        theirs = got[EXTRA * (lat_blk // 2) + f]
        inner[ntr + f] = jnp.where(in_half((nz, lon), half, lat_blk // 2), g_other[f], theirs)
    for out, start in zip((rows_a, rows_b), edge_starts(chip, lat_blk)):
        for n in range(ntr):
            out[2 * n : 2 * n + 2] = turned[n, pl.ds(start, 2)]
        for f in range(EXTRA):
            out[2 * (ntr + f) : 2 * (ntr + f) + 2] = ocean[f, pl.ds(start, 2)]
    mix[...] = mix_matrix(rates[...], nz)
    own = span(2, lat_blk + 2)

    def wets(r, count):
        at = pl.ds(r, count)
        for f in range(EXTRA):
            m0[ntr + f, at] = ocean[f, pl.ds(r - 2, count)]
        dv[WET, at] = wet_of(ocean[EXTRA - 1, pl.ds(r - 2, count)])

    chunks(own, 8, wets)

    def some(r, count):
        wet = dv[WET, r]
        for n in range(ntr):
            m0[n, r] = turned[n, r - 2] * wet

    chunks(own, 1, some)
    derive_rows(m0, dv, ntr, own)
    mask_columns([g_own[f] for f in range(ntr + EXTRA)], g0, gd)


def mask_columns(fields, z, zd):
    ntr = len(fields) - EXTRA
    wet = wet_of(fields[-1])
    zd[WET] = wet
    for f, cols in enumerate(fields):
        z[f] = cols * wet if f < ntr else cols
    derive_columns(z, zd, ntr)


def inner_kernel(m0, dv, mix, g0, gd, z_in, m1, m2, dv1, wts, sat, z0, z1, zd):
    nf, rows, _, _ = m0.shape
    ntr = nf - EXTRA
    mask_columns([z_in[f] for f in range(nf)], z0, zd)
    column_step(z0, g0, zd, gd, z1, mix, ntr, rows - 4)
    now = span(3, rows - 3)
    ocean_rows(m0, dv, z0, zd, wts, m1, ntr, now)
    tracer_rows(m0, z0, wts, m1, sat, ntr, now)
    react_rows(dv, mix, m1, sat, ntr, now)
    light_rows(m0, dv, m1, ntr, now)
    dv1[WET, 3 : rows - 3] = dv[WET, 3 : rows - 3]
    derive_rows(m1, dv1, ntr, now)
    derive_columns(z1, zd, ntr)
    now = span(4, rows - 4)
    ocean_rows(m1, dv1, z1, zd, wts, m2, ntr, now)
    tracer_rows(m1, z1, wts, m2, sat, ntr, now)
    react_rows(dv1, mix, m2, sat, ntr, now)
    light_rows(m0, dv1, m2, ntr, now)


def outer_kernel(m_own, dv_own, mix, g0, gd, z_in, rows_a, rows_b, edge_a, edge_b, m1_in, m2_in, rim, keep, send, m0, m1, dv0, dv1, wts, sat, z0, z1, zd):
    nf, rows, nz, lon = m_own.shape
    ntr = nf - EXTRA
    lat_blk = rows - 4
    half, chip, _ = place()
    even = chip % 2 == 0
    south_ok, north_ok = (chip > 0, chip < lax.axis_size("row") // 2 - 1)

    def got(high, a, b, index):
        a, b = (a[index], b[index])
        picked = jnp.where(even, a, b) if high else jnp.where(even, b, a)
        return jnp.where(north_ok if high else south_ok, picked, 0.0)

    for high, start in ((False, 0), (True, rows - 2)):
        for f in range(EXTRA):
            m0[ntr + f, start : start + 2] = got(high, rows_a, rows_b, pl.ds(2 * (ntr + f), 2))
        wet = wet_of(m0[nf - 1, start : start + 2])
        dv0[WET, start : start + 2] = wet
        for n in range(ntr):
            m0[n, start : start + 2] = got(high, rows_a, rows_b, pl.ds(2 * n, 2)) * wet
        derive_rows(m0, dv0, ntr, span(start, start + 2))
    for start in (2, rows - 4):
        m0[:, start : start + 2] = m_own[:, start : start + 2]
        dv0[:, start : start + 2] = dv_own[:, start : start + 2]
    lane = lanes_of((nz, lon))
    low, high = (got(False, edge_a, edge_b, ...), got(True, edge_a, edge_b, ...))
    at_low, at_high = (lane < WIN, (lane >= WIN * (lat_blk + 1)) & (lane < WIN * (lat_blk + 2)))
    fields = []
    for f in range(nf):
        cols = jnp.where(at_low, pltpu.roll(low, (-WIN * f) % lon, 1), z_in[f])
        fields.append(jnp.where(at_high, pltpu.roll(high, (WIN * (lat_blk + 1) - WIN * f) % lon, 1), cols))
    mask_columns(fields, z0, zd)
    column_step(z0, g0, zd, gd, z1, mix, ntr, lat_blk)
    now = (1, lat_blk, 2, 2)
    ocean_rows(m0, dv0, z0, zd, wts, m1, ntr, now)
    tracer_rows(m0, z0, wts, m1, sat, ntr, now)
    react_rows(dv0, mix, m1, sat, ntr, now)
    light_rows(m0, dv0, m1, ntr, now)
    for start in (3, rows - 5):
        m1[:, start : start + 2] = m1_in[:, start : start + 2]
    for start in (1, rows - 3):
        dv1[WET, start : start + 2] = dv0[WET, start : start + 2]
    for start in (3, rows - 5):
        dv1[WET, start : start + 2] = dv_own[WET, start : start + 2]
    derive_rows(m1, dv1, ntr, (1, rows - 6, 2, 4))
    derive_columns(z1, zd, ntr)
    now = (2, rows - 6, 2, 2)
    ocean_rows(m1, dv1, z1, zd, wts, m0, ntr, now)
    tracer_rows(m1, z1, wts, m0, sat, ntr, now)
    react_rows(dv1, mix, m0, sat, ntr, now)
    light_rows(m0, dv1, m0, ntr, now)

    rim[:, 0:2] = m0[:ntr, 2:4]
    rim[:, 2:4] = m0[:ntr, rows - 4 : rows - 2]
    m0[ntr : ntr + 3, 4 : rows - 4] = m2_in[ntr : ntr + 3, 4 : rows - 4]
    count = lat_blk // 2
    for f in range(3):
        keep[f] = m0[ntr + f, pl.ds(2 + half * count, count)]
        send[f] = m0[ntr + f, pl.ds(2 + (1 - half) * count, count)]


def write_kernel(rim, m, out, block, sem):
    ntr, nz, lat_blk, lon = block.shape
    copies = []
    for n in range(0, ntr, GROUP):
        for k in range(n, n + GROUP):
            for t in range(lat_blk):
                edge = {0: 0, 1: 1, lat_blk - 2: 2, lat_blk - 1: 3}.get(t)
                block[k, :, t, :] = m[k, t + 2] if edge is None else rim[k, edge]
        copy = pltpu.make_async_copy(block.at[pl.ds(n, GROUP)], out.at[pl.ds(n, GROUP)], sem.at[n // GROUP])
        copy.start()
        copies.append(copy)
    for copy in copies:
        copy.wait()


def unpack_kernel(keep, got, flow, temp):
    _, lat_dev, nz, lon = keep.shape
    first = place()[0] == 0
    for t in range(lat_dev):
        for f in range(3):
            a, b = (keep[f, t], got[f, t])
            low, high = (jnp.where(first, a, b), jnp.where(first, b, a))
            if f < 2:
                flow[f, :, t, :lon] = low
                flow[f, :, t, lon:] = high
            else:
                temp[:, t, :lon] = low
                temp[:, t, lon:] = high


def call(kernel, outs, *args, scratch=(), held=True, away=False, limit=40, cost=1):
    vmem = pl.BlockSpec(memory_space=pltpu.VMEM)
    return pl.pallas_call(
        kernel,
        out_shape=[jax.ShapeDtypeStruct(s, jnp.float32) if isinstance(s, tuple) else s for s in outs],
        in_specs=[vmem if held else pl.BlockSpec(memory_space=pl.ANY)] * len(args),
        out_specs=[pl.BlockSpec(memory_space=pl.ANY) if away else vmem] * len(outs),
        scratch_shapes=[pltpu.VMEM(s, jnp.float32) if isinstance(s, tuple) else s for s in scratch],
        compiler_params=pltpu.CompilerParams(vmem_limit_bytes=limit * 2**20),
        cost_estimate=pl.CostEstimate(flops=int(cost * 10**9), transcendentals=0, bytes_accessed=int(cost * 4 * 2**20)),
    )(*args)


def both_ways(pairs):
    return sorted(pairs + [(b, a) for a, b in pairs])


def exchanges(n_row, n_col):
    chips = n_row // 2

    def dev(p, h, c):
        return (2 * p + h) * n_col + c

    partner = [(dev(p, 0, c), dev(p, 1, c)) for p in range(chips) for c in range(n_col)]
    outer = [(dev(p, 1, c), dev(p, 0, c + 1)) for p in range(chips) for c in range(n_col - 1)]
    for p in range(0, chips - 1, 2):
        outer += [(dev(p, 0, 0), dev(p + 1, 0, 0)), (dev(p, 1, n_col - 1), dev(p + 1, 1, n_col - 1))]
    lat_a = [(dev(p, h, c), dev(p + 1, h, c)) for p in range(0, chips - 1, 2) for h in (0, 1) for c in range(n_col)]
    lat_b = [(dev(p, h, c), dev(p + 1, h, c)) for p in range(1, chips - 1, 2) for h in (0, 1) for c in range(n_col)]
    if chips % 2 == 0 and chips > 2:
        lat_b += [(dev(0, h, c), dev(chips - 1, h, c)) for h in (0, 1) for c in range(n_col)]
    return [both_ways(x) for x in (partner, outer, lat_a, lat_b)]


def on_device(n_row, n_col, flow, temp, tracers, bottom, sunlight, rates):
    nz, lat_dev, lon_dev = temp.shape
    _, ntr, _, lat_blk, lon = tracers.shape
    nf = ntr + EXTRA
    partner, outer, lat_a, lat_b = exchanges(n_row, n_col)

    def swap(x, pairs):
        return lax.ppermute(x, ("row", "col"), pairs)

    block = tracers[0]
    parts = [flow.reshape(-1, lat_dev, lon_dev), temp, bottom[None], sunlight[None]]
    total = sum(part.shape[0] for part in parts)
    surface, start = (0.0, 0)
    for part in parts:
        count = part.shape[0]
        surface = surface + jnp.pad(part, ((start, total - start - count), (0, 0), (0, 0))).astype(jnp.float32)
        start += count
    rows = lat_blk + 4
    cols, extra, some = ((nf, nz, lon), (EXTRA, nz, lon), (3, nz, lon))
    copies = pltpu.SemaphoreType.DMA((ntr // GROUP,))
    sent = (EXTRA * (lat_dev + 1), nz, lon)
    mine, to_partner, g_other = call(pack_ocean_kernel, [(EXTRA, lat_dev, nz, lon), sent, extra], surface)
    got = swap(to_partner, partner)
    turned, g_tracers = call(
        pack_tracers_kernel,
        [(ntr, lat_blk, nz, lon), (ntr, nz, lon)],
        block,
        scratch=[block.shape, copies],
        held=False,
        limit=52,
    )
    ocean, g_own, to_outer = call(
        join_kernel, [(EXTRA, lat_blk, nz, lon), cols, (nf // 4, nz, lon)], mine, got, to_partner, g_tracers
    )
    from_outer = swap(to_outer, outer)
    g_partner = swap(g_tracers, partner)
    full, derived = ((nf, rows, nz, lon), (3, rows, nz, lon))
    rim = (2 * nf, nz, lon)
    rows_a, rows_b, m0, dv, mix, g0, gd, inner = call(
        fill_kernel,
        [rim, rim, full, derived, jax.ShapeDtypeStruct((2 * ntr * nz, 2 * ntr * nz), jnp.bfloat16), cols, some, cols],
        turned,
        ocean,
        g_own,
        g_partner,
        got,
        g_other,
        rates,
    )
    rows_a, rows_b = (swap(rows_a, lat_a), swap(rows_b, lat_b))
    z, edge_a, edge_b = call(
        functools.partial(edge_kernel, lat_blk), [cols, (nz, lon), (nz, lon)], inner, from_outer
    )
    edge_a, edge_b = (swap(edge_a, lat_a), swap(edge_b, lat_b))
    work = [(7, rows, nz, lon), pltpu.VMEM((rows, 2 * ntr * nz, lon), jnp.bfloat16), cols, cols, some]
    m1, m2 = call(inner_kernel, [full, full], m0, dv, mix, g0, gd, z, scratch=[derived] + work, cost=20)
    third = (3, lat_dev, nz, lon)
    rim, keep, send = call(
        outer_kernel,
        [(ntr, 4, nz, lon), third, third],
        m0,
        dv,
        mix,
        g0,
        gd,
        z,
        rows_a,
        rows_b,
        edge_a,
        edge_b,
        m1,
        m2,
        scratch=[full, full, derived, derived] + work,
    )
    returned = swap(send, partner)
    (out,) = call(write_kernel, [(ntr, nz, lat_blk, lon)], rim, m2, scratch=[(ntr, nz, lat_blk, lon), copies], away=True)
    flow_out, temp_out = call(
        unpack_kernel, [(2, nz, lat_dev, lon_dev), (nz, lat_dev, lon_dev)], keep, returned
    )
    return (flow_out, temp_out, out[None])


def solution(mesh):
    in_specs = (
        P(None, None, "row", "col"),
        P(None, "row", "col"),
        P("row", None, None, None, "col"),
        P("row", "col"),
        P("row", "col"),
        P(),
    )
    out_specs = (
        P(None, None, "row", "col"),
        P(None, "row", "col"),
        P("row", None, None, None, "col"),
    )
    return jax.shard_map(
        functools.partial(on_device, mesh.shape["row"], mesh.shape["col"]),
        mesh=mesh,
        in_specs=in_specs,
        out_specs=out_specs,
        check_vma=False,
    )
```

```python
import functools
import jax
import jax.numpy as jnp
from jax import lax
from jax.experimental import pallas as pl
from jax.experimental.pallas import tpu as pltpu
from jax.sharding import PartitionSpec as P

KL = 4
STEPS = 2

time_step = 0.2
viscosity = 0.2
expansion = 0.05
coriolis_base = 0.5
kappa_base = 0.05
kappa_shear = 0.2
react_step = 0.25
water_absorb = 0.1
pigment_absorb = 0.6
heat_gain = 1.0

EXTRA = 4
WIN = 4


def up(x):
    return pltpu.roll(x, 1, x.ndim - 2)


def down(x):
    return pltpu.roll(x, x.shape[-2] - 1, x.ndim - 2)


def lanes_of(shape):
    return lax.broadcasted_iota(jnp.int32, shape, len(shape) - 1)


def levels_of(shape):
    return lax.broadcasted_iota(jnp.int32, shape, len(shape) - 2)


def window(x, lat, into):
    lon = x.shape[1]
    lane = lanes_of(x.shape)
    base = WIN * (lat + 1)
    moved = pltpu.roll(x, (base + 2) % lon, 1)
    return jnp.where((lane >= base) & (lane < base + WIN), moved, into)


def place():
    row = lax.axis_index("row")
    return (row % 2, row // 2, lax.axis_index("col"))


def edge_starts(chip, lat_blk):
    odd = chip % 2
    return ((1 - odd) * (lat_blk - 2), odd * (lat_blk - 2))


def pack_ocean_kernel(flow_in, temp_in, bottom_in, sunlight_in, tracers_in, mine, to_partner, g_other, tracers, flow, temp, bottom, sunlight, sem):
    copies = [
        pltpu.make_async_copy(src, dst, sem.at[i])
        for i, (src, dst) in enumerate(
            ((flow_in, flow), (temp_in, temp), (bottom_in, bottom), (sunlight_in, sunlight), (tracers_in, tracers))
        )
    ]
    for copy in copies:
        copy.start()
    for copy in copies[:-1]:
        copy.wait()
    lat_dev, nz, lon = mine.shape[1:]
    lon_dev = temp.shape[2]
    half, _, _ = place()
    first = half == 0
    zero = jnp.zeros((nz, lon), jnp.float32)
    level = levels_of((nz, lon_dev))
    own = [zero] * EXTRA
    far = [zero] * EXTRA
    for t in range(lat_dev):
        depth = jnp.broadcast_to(bottom[t : t + 1, :], (nz, lon_dev))
        light = jnp.broadcast_to(sunlight[t : t + 1, :], (nz, lon_dev))
        wet = (level < depth).astype(jnp.float32)
        aux = jnp.where(level == 0, depth.astype(jnp.float32), jnp.where(level == 1, light, 0.0))
        for f, tile in enumerate((flow[0, :, t, :] * wet, flow[1, :, t, :] * wet, temp[:, t, :] * wet, aux)):
            low, high = (tile[:, :lon], tile[:, lon:])
            a, b = (jnp.where(first, low, high), jnp.where(first, high, low))
            mine[f, t] = a
            to_partner[f * lat_dev + t] = b
            own[f] = window(a, t, own[f])
            far[f] = window(b, t, far[f])
    shift = half * (WIN * lat_dev)
    for f in range(EXTRA):
        to_partner[EXTRA * lat_dev + f] = pltpu.roll(own[f], shift, 1)
        g_other[f] = pltpu.roll(far[f], shift, 1)
    copies[-1].wait()


def pack_tracers_kernel(tracers, turned, g_tracers):
    ntr, nz, lat_blk, lon = tracers.shape

    def some(i, _):
        g = [jnp.zeros((nz, lon), jnp.float32)] * GROUP
        for t in range(lat_blk):
            for k in range(GROUP):
                x = tracers[i * GROUP + k, :, t, :]
                turned[i * GROUP + k, t] = x
                g[k] = window(x, t, g[k])
        for k in range(GROUP):
            g_tracers[i * GROUP + k] = g[k]
        return 0

    lax.fori_loop(0, ntr // GROUP, some, 0)


def in_half(shape, half, lat_dev):
    lane = lanes_of(shape)
    base = WIN * (lat_dev * half + 1)
    return (lane >= base) & (lane < base + WIN * lat_dev)


def join_kernel(mine, got, to_partner, g_tracers, ocean, g_own, to_outer):
    _, lat_dev, nz, lon = mine.shape
    ntr = g_tracers.shape[0]
    nf = ntr + EXTRA
    half, _, _ = place()
    tile = (nz, lon)
    own_lanes = in_half(tile, half, lat_dev)
    shift = (1 - half) * (WIN * lat_dev)
    g_own[:ntr] = g_tracers[...]
    for f in range(EXTRA):
        g = jnp.zeros(tile, jnp.float32)
        for t in range(lat_dev):
            x = got[f * lat_dev + t]
            ocean[f, half * lat_dev + t] = mine[f, t]
            ocean[f, (1 - half) * lat_dev + t] = x
            g = window(x, t, g)
        g_own[ntr + f] = jnp.where(own_lanes, to_partner[EXTRA * lat_dev + f], pltpu.roll(g, shift, 1))
    lane = lanes_of(tile)
    front, near = (lane % WIN < 2, in_half(tile, 0, 2 * lat_dev))
    side = (1 - half) * (lon - 2)
    for i in range(nf // 4):
        a, b, c, d = [pltpu.roll(g_own[4 * i + k], side, 1) for k in range(4)]
        low = jnp.where(front, a, pltpu.roll(b, 2, 1))
        high = jnp.where(front, c, pltpu.roll(d, 2, 1))
        to_outer[i] = jnp.where(near, low, pltpu.roll(high, lon // 2, 1))


def edge_kernel(lat_blk, inner, from_outer, z, to_a, to_b):
    nf, nz, lon = z.shape

    half, chip, column = place()
    tile = (nz, lon)
    lane = lanes_of(tile)
    outer_ok = jnp.where(half == 0, column > 0, column < lax.axis_size("col") - 1)
    from_partner = (lane % WIN < 2).astype(jnp.int32) == half
    outer_lanes = in_half(tile, 0, lat_blk) & outer_ok
    start_a, start_b = edge_starts(chip, lat_blk)
    corner_a = corner_b = jnp.zeros(tile, jnp.float32)
    for f in range(nf):
        k = f % 4
        moved = pltpu.roll(from_outer[f // 4], lon + 2 * half - 2 * (k % 2) - lon // 2 * (k // 2), 1)
        cols = jnp.where(from_partner, inner[f], jnp.where(outer_lanes, moved, 0.0))
        z[f] = cols
        at = (lane >= WIN * f) & (lane < WIN * f + WIN)
        low = pltpu.roll(cols, (WIN * f - WIN) % lon, 1)
        high = pltpu.roll(cols, (WIN * f - WIN * lat_blk) % lon, 1)
        corner_a = jnp.where(at, jnp.where(start_a > 0, high, low), corner_a)
        corner_b = jnp.where(at, jnp.where(start_b > 0, high, low), corner_b)
    to_a[...] = corner_a
    to_b[...] = corner_b


def kappa_of(u, v):
    du, dv = (u - down(u), v - down(v))
    sq = jnp.where(levels_of(u.shape) < u.shape[-2] - 1, du * du + dv * dv, 0.0)
    return kappa_base + kappa_shear * sq / (1.0 + sq)


def sum_above(x):
    level = levels_of(x.shape)
    k = 1
    while k < x.shape[-2]:
        x = x + jnp.where(level >= k, pltpu.roll(x, k, x.ndim - 2), 0.0)
        k *= 2
    return x


def sum_below(x):
    level, nz = (levels_of(x.shape), x.shape[-2])
    k = 1
    while k < nz:
        x = x + jnp.where(level < nz - k, pltpu.roll(x, nz - k, x.ndim - 2), 0.0)
        k *= 2
    return x


def pressure_of(heat):
    return -expansion * sum_above(heat)


def wet_of(aux):
    depth = jnp.broadcast_to(aux[..., 0:1, :], aux.shape)
    return (levels_of(aux.shape).astype(jnp.float32) < depth).astype(jnp.float32)


def light_of(aux):
    return jnp.broadcast_to(aux[..., 1:2, :], aux.shape)


def dynamics(u, v, wet, kap, prs, coriolis):
    um, ue, uw, un, us = u
    vm, ve, vw, vn, vs = v
    wm, we, ww, wn, ws = wet
    km, ke, kw, kn, ks = kap
    _, pe, pw, pn, ps = prs
    level, nz = (levels_of(um.shape), um.shape[-2])
    oe, ow, on, os_ = (wm * we, wm * ww, wm * wn, wm * ws)
    fe, fw, fn, fs = (0.5 * (um + ue) * oe, 0.5 * (um + uw) * ow, 0.5 * (vm + vn) * on, 0.5 * (vm + vs) * os_)
    ce, cw, cn, cs = (0.5 * (km + ke) * oe, 0.5 * (km + kw) * ow, 0.5 * (km + kn) * on, 0.5 * (km + ks) * os_)
    div = fe - fw + fn - fs
    total = sum_below(div)
    w_top = jnp.where(level >= 1, -total, 0.0)
    w_bot = jnp.where(level < nz - 1, -down(total), 0.0)
    weights = (
        wm * (1.0 - time_step * (ce + cw + cn + cs + 0.5 * (div + w_top - w_bot))),
        time_step * (ce - 0.5 * fe),
        time_step * (cw + 0.5 * fw),
        time_step * (cn - 0.5 * fn),
        time_step * (cs + 0.5 * fs),
        (-0.5 * time_step) * wm * w_top,
        (0.5 * time_step) * wm * w_bot,
    )
    lap_u = oe * (ue - um) + ow * (uw - um) + on * (un - um) + os_ * (us - um)
    lap_v = oe * (ve - vm) + ow * (vw - vm) + on * (vn - vm) + os_ * (vs - vm)
    new_u = wm * (um + time_step * (coriolis * vm - 0.5 * (pe - pw) + viscosity * lap_u))
    new_v = wm * (vm + time_step * (-coriolis * um - 0.5 * (pn - ps) + viscosity * lap_v))
    return (new_u, new_v, weights)


def transport(weights, x, east, west, north, south):
    a0, ae, aw, an, as_, at, ab = weights
    return (a0 * x + ae * east) + (aw * west + an * north) + (as_ * south + at * up(x)) + ab * down(x)


def saturated(x):
    return x * lax.rsqrt(1.0 + x * x)


def absorbed(pigment):
    level = levels_of(pigment.shape)
    sq = pigment * pigment
    depth = water_absorb + pigment_absorb * (sq / (1.0 + sq))
    above = jnp.where(level >= 1, up(depth), 0.0)
    k = 1
    while k < KL:
        above = above + jnp.where(level >= k, pltpu.roll(above, k, above.ndim - 2), 0.0)
        k *= 2
    return jnp.where(level < KL, jnp.exp(-above) * (1.0 - jnp.exp(-depth)), 0.0)


def two_parts(x):
    high = x.astype(jnp.bfloat16)
    return (high, (x - high.astype(jnp.float32)).astype(jnp.bfloat16))


def mix_matrix(rates, nz):
    ntr = rates.shape[0]
    size = ntr * nz
    exact = dict(precision=lax.Precision.HIGHEST, preferred_element_type=jnp.float32)
    spread = lax.broadcasted_iota(jnp.int32, (size, ntr), 0) // nz == lax.broadcasted_iota(jnp.int32, (size, ntr), 1)
    spread = spread.astype(jnp.float32)
    wide = jnp.dot(spread, rates, **exact)
    full = lax.dot_general(wide, spread, (((1,), (1,)), ((), ())), **exact)
    same = lax.broadcasted_iota(jnp.int32, (size, size), 0) % nz == lax.broadcasted_iota(jnp.int32, (size, size), 1) % nz
    high, low = two_parts(jnp.where(same, full, 0.0))
    top = jnp.concatenate([high, high], axis=1)
    return jnp.concatenate([top, jnp.concatenate([low, jnp.zeros_like(low)], axis=1)], axis=0)


def beside(z, r, lon):
    return pltpu.roll(z, lon - 2 - WIN * (r - 1), z.ndim - 1)


def sides(x, edge):
    lane, lon = (lanes_of(x.shape), x.shape[-1])
    west = pltpu.roll(jnp.where(lane == lon - 1, edge, x), 1, x.ndim - 1)
    east = pltpu.roll(jnp.where(lane == 0, edge, x), lon - 1, x.ndim - 1)
    return (east, west)


def around_rows(m, f, z, r, count):
    x = m[f, pl.ds(r, count)]
    edge = jnp.stack([beside(z, r + i, x.shape[-1]) for i in range(count)])
    return (x, *sides(x, edge), m[f, pl.ds(r + 1, count)], m[f, pl.ds(r - 1, count)])


def around_columns(x, own):
    lane, lon = (lanes_of(x.shape), x.shape[-1])
    west = pltpu.roll(jnp.where(lane % WIN == 0, x, own), 1, x.ndim - 1)
    east = pltpu.roll(jnp.where(lane % WIN == WIN - 1, x, own), lon - 1, x.ndim - 1)
    return (x, east, west, pltpu.roll(x, lon - WIN, x.ndim - 1), pltpu.roll(x, WIN, x.ndim - 1))


def coriolis_at(lat, lat_blk):
    _, chip, _ = place()
    latitude = (lat + chip * lat_blk).astype(jnp.float32)
    return coriolis_base * (2.0 * (latitude + 0.5) / (lax.axis_size("row") // 2 * lat_blk) - 1.0)


KAP, PRS, WET = (0, 1, 2)
GROUP = 4
PIECE = 3


def span(start, stop):
    return (start, stop - start, 1, stop - start)


def chunks(rows, most, body):
    first, apart, times, size = rows
    count = max(k for k in range(1, min(most, size) + 1) if size % k == 0)
    if times > 1 or count == size:
        for i in range(times):
            body(first + i * apart, size)
    else:

        def one(i, _):
            body(first + i * count, count)
            return 0

        lax.fori_loop(0, size // count, one, 0)


def derive_rows(m, dv, ntr, rows):
    def body(r, count):
        at = pl.ds(r, count)
        dv[KAP, at] = kappa_of(m[ntr, at], m[ntr + 1, at])
        dv[PRS, at] = pressure_of(m[ntr + 2, at])

    chunks(rows, 10, body)


def derive_columns(z, zd, ntr):
    zd[KAP] = kappa_of(z[ntr], z[ntr + 1])
    zd[PRS] = pressure_of(z[ntr + 2])


def ocean_rows(m, dv, z, zd, wts, new, ntr, rows):
    def body(r, count):
        at = pl.ds(r, count)
        lat = lax.broadcasted_iota(jnp.int32, (count, *m.shape[2:]), 0) + (r - 2)
        new_u, new_v, weights = dynamics(
            around_rows(m, ntr, z[ntr], r, count),
            around_rows(m, ntr + 1, z[ntr + 1], r, count),
            around_rows(dv, WET, zd[WET], r, count),
            around_rows(dv, KAP, zd[KAP], r, count),
            around_rows(dv, PRS, zd[PRS], r, count),
            coriolis_at(lat, m.shape[1] - 4),
        )
        new[ntr, at] = new_u
        new[ntr + 1, at] = new_v
        for i, w in enumerate(weights):
            wts[i, at] = w

    chunks(rows, 9, body)


def tracer_rows(m, z, wts, dv, mix, moved, sat, new, ntr, rows):
    nz, lon = m.shape[2:]
    half = ntr * nz
    first, apart, times, count = rows
    if times == 1:
        count = max(k for k in range(1, PIECE + 1) if rows[3] % k == 0)
        apart, times = (count, rows[3] // count)

    def move(r):
        weights = [wts[i, r] for i in range(7)]
        for n in range(0, ntr, GROUP):
            x = m[n : n + GROUP, r]
            edge = beside(z[n : n + GROUP], r, lon)
            done = transport(weights, x, *sides(x, edge), m[n : n + GROUP, r + 1], m[n : n + GROUP, r - 1])
            moved[n : n + GROUP, r] = done
            high, low = two_parts(saturated(done).reshape(GROUP * nz, lon))
            sat[r, n * nz : (n + GROUP) * nz, :] = high
            sat[r, half + n * nz : half + (n + GROUP) * nz, :] = low
        h = ntr + 2
        x = m[h, r]
        moved[ntr, r] = transport(weights, x, *sides(x, beside(z[h], r, lon)), m[h, r + 1], m[h, r - 1])

    def react(r):
        both = jnp.concatenate([sat[r + i] for i in range(count)], axis=1)
        res = jnp.dot(mix[...], both, preferred_element_type=jnp.float32)
        res = res[:half] + res[half:]
        for i in range(count):
            gain = react_step * dv[WET, r + i]
            for n in range(ntr):
                new[n, r + i] = moved[n, r + i] + gain * res[n * nz : (n + 1) * nz, i * lon : (i + 1) * lon]

    def move_all(r):
        for i in range(count):
            move(r + i)

    def both_parts(i, _):
        react(first + (i - 1) * apart)
        move_all(first + i * apart)
        return 0

    move_all(first)
    if rows[2] > 1:
        for i in range(1, times):
            both_parts(i, 0)
    else:
        lax.fori_loop(1, times, both_parts, 0)
    react(first + (times - 1) * apart)


def light_rows(m, dv, moved, new, ntr, rows):
    def body(r, count):
        at = pl.ds(r, count)
        light = light_of(m[ntr + 3, at]) * dv[WET, at] * absorbed(new[0, at])
        new[ntr + 2, at] = moved[ntr, at] + heat_gain * light

    chunks(rows, 9, body)


def column_step(z0, g0, zd, gd, z1, mix, ntr, lat_blk):
    nz, lon = z0.shape[1:]
    half = ntr * nz
    wet = zd[WET]
    new_u, new_v, weights = dynamics(
        around_columns(z0[ntr], g0[ntr]),
        around_columns(z0[ntr + 1], g0[ntr + 1]),
        around_columns(wet, gd[WET]),
        around_columns(zd[KAP], gd[KAP]),
        around_columns(zd[PRS], gd[PRS]),
        coriolis_at(lanes_of((nz, lon)) // WIN - 1, lat_blk),
    )
    moved = transport(weights, *around_columns(z0[:ntr], g0[:ntr]))
    high, low = two_parts(saturated(moved).reshape(half, lon))
    res = jnp.dot(mix[...], jnp.concatenate([high, low], axis=0), preferred_element_type=jnp.float32)
    done = moved + (react_step * wet) * (res[:half] + res[half:]).reshape(ntr, nz, lon)
    z1[:ntr] = done
    z1[ntr] = new_u
    z1[ntr + 1] = new_v
    heat = transport(weights, *around_columns(z0[ntr + 2], g0[ntr + 2]))
    z1[ntr + 2] = heat + heat_gain * light_of(z0[ntr + 3]) * wet * absorbed(done[0])


def fill_kernel(turned, ocean, g_own, g_partner, got, g_other, rates, rows_a, rows_b, m0, dv, mix, g0, gd, inner):
    ntr, lat_blk, nz, lon = turned.shape
    half, chip, _ = place()
    inner[:ntr] = g_partner[...]
    for f in range(EXTRA):
        theirs = got[EXTRA * (lat_blk // 2) + f]
        inner[ntr + f] = jnp.where(in_half((nz, lon), half, lat_blk // 2), g_other[f], theirs)
    for out, start in zip((rows_a, rows_b), edge_starts(chip, lat_blk)):
        for n in range(ntr):
            out[2 * n : 2 * n + 2] = turned[n, pl.ds(start, 2)]
        for f in range(EXTRA):
            out[2 * (ntr + f) : 2 * (ntr + f) + 2] = ocean[f, pl.ds(start, 2)]
    mix[...] = mix_matrix(rates[...], nz)
    own = span(2, lat_blk + 2)

    def wets(r, count):
        at = pl.ds(r, count)
        for f in range(EXTRA):
            m0[ntr + f, at] = ocean[f, pl.ds(r - 2, count)]
        dv[WET, at] = wet_of(ocean[EXTRA - 1, pl.ds(r - 2, count)])

    chunks(own, 8, wets)

    def some(r, count):
        wet = dv[WET, r]
        for n in range(ntr):
            m0[n, r] = turned[n, r - 2] * wet

    chunks(own, 1, some)
    derive_rows(m0, dv, ntr, own)
    mask_columns([g_own[f] for f in range(ntr + EXTRA)], g0, gd)


def mask_columns(fields, z, zd):
    ntr = len(fields) - EXTRA
    wet = wet_of(fields[-1])
    zd[WET] = wet
    for f, cols in enumerate(fields):
        z[f] = cols * wet if f < ntr else cols
    derive_columns(z, zd, ntr)


def inner_kernel(m0, dv, mix, g0, gd, z_in, m1, m2, dv1, wts, sat, moved, z0, z1, zd):
    nf, rows, _, _ = m0.shape
    ntr = nf - EXTRA
    mask_columns([z_in[f] for f in range(nf)], z0, zd)
    column_step(z0, g0, zd, gd, z1, mix, ntr, rows - 4)
    now = span(3, rows - 3)
    ocean_rows(m0, dv, z0, zd, wts, m1, ntr, now)
    tracer_rows(m0, z0, wts, dv, mix, moved, sat, m1, ntr, now)
    light_rows(m0, dv, moved, m1, ntr, now)
    dv1[WET, 3 : rows - 3] = dv[WET, 3 : rows - 3]
    derive_rows(m1, dv1, ntr, now)
    derive_columns(z1, zd, ntr)
    now = span(4, rows - 4)
    ocean_rows(m1, dv1, z1, zd, wts, m2, ntr, now)
    tracer_rows(m1, z1, wts, dv1, mix, moved, sat, m2, ntr, now)
    light_rows(m0, dv1, moved, m2, ntr, now)


def outer_kernel(m_own, dv_own, mix, g0, gd, z_in, rows_a, rows_b, edge_a, edge_b, m1_in, m2_in, rim, keep, send, m0, m1, dv0, dv1, wts, sat, moved, z0, z1, zd):
    nf, rows, nz, lon = m_own.shape
    ntr = nf - EXTRA
    lat_blk = rows - 4
    half, chip, _ = place()
    even = chip % 2 == 0
    south_ok, north_ok = (chip > 0, chip < lax.axis_size("row") // 2 - 1)

    def got(high, a, b, index):
        a, b = (a[index], b[index])
        picked = jnp.where(even, a, b) if high else jnp.where(even, b, a)
        return jnp.where(north_ok if high else south_ok, picked, 0.0)

    for high, start in ((False, 0), (True, rows - 2)):
        for f in range(EXTRA):
            m0[ntr + f, start : start + 2] = got(high, rows_a, rows_b, pl.ds(2 * (ntr + f), 2))
        wet = wet_of(m0[nf - 1, start : start + 2])
        dv0[WET, start : start + 2] = wet
        for n in range(ntr):
            m0[n, start : start + 2] = got(high, rows_a, rows_b, pl.ds(2 * n, 2)) * wet
        derive_rows(m0, dv0, ntr, span(start, start + 2))
    for start in (2, rows - 4):
        m0[:, start : start + 2] = m_own[:, start : start + 2]
        dv0[:, start : start + 2] = dv_own[:, start : start + 2]
    lane = lanes_of((nz, lon))
    low, high = (got(False, edge_a, edge_b, ...), got(True, edge_a, edge_b, ...))
    at_low, at_high = (lane < WIN, (lane >= WIN * (lat_blk + 1)) & (lane < WIN * (lat_blk + 2)))
    fields = []
    for f in range(nf):
        cols = jnp.where(at_low, pltpu.roll(low, (-WIN * f) % lon, 1), z_in[f])
        fields.append(jnp.where(at_high, pltpu.roll(high, (WIN * (lat_blk + 1) - WIN * f) % lon, 1), cols))
    mask_columns(fields, z0, zd)
    column_step(z0, g0, zd, gd, z1, mix, ntr, lat_blk)
    now = (1, lat_blk, 2, 2)
    ocean_rows(m0, dv0, z0, zd, wts, m1, ntr, now)
    tracer_rows(m0, z0, wts, dv0, mix, moved, sat, m1, ntr, now)
    light_rows(m0, dv0, moved, m1, ntr, now)
    for start in (3, rows - 5):
        m1[:, start : start + 2] = m1_in[:, start : start + 2]
    for start in (1, rows - 3):
        dv1[WET, start : start + 2] = dv0[WET, start : start + 2]
    for start in (3, rows - 5):
        dv1[WET, start : start + 2] = dv_own[WET, start : start + 2]
    derive_rows(m1, dv1, ntr, (1, rows - 6, 2, 4))
    derive_columns(z1, zd, ntr)
    now = (2, rows - 6, 2, 2)
    ocean_rows(m1, dv1, z1, zd, wts, m0, ntr, now)
    tracer_rows(m1, z1, wts, dv1, mix, moved, sat, m0, ntr, now)
    light_rows(m0, dv1, moved, m0, ntr, now)

    rim[:, 0:2] = m0[:ntr, 2:4]
    rim[:, 2:4] = m0[:ntr, rows - 4 : rows - 2]
    m0[ntr : ntr + 3, 4 : rows - 4] = m2_in[ntr : ntr + 3, 4 : rows - 4]
    count = lat_blk // 2
    for f in range(3):
        keep[f] = m0[ntr + f, pl.ds(2 + half * count, count)]
        send[f] = m0[ntr + f, pl.ds(2 + (1 - half) * count, count)]


def write_kernel(rim, m, out, block, sem):
    ntr, nz, lat_blk, lon = block.shape
    copies = []
    for n in range(0, ntr, GROUP):
        for k in range(n, n + GROUP):
            for t in range(lat_blk):
                edge = {0: 0, 1: 1, lat_blk - 2: 2, lat_blk - 1: 3}.get(t)
                block[k, :, t, :] = m[k, t + 2] if edge is None else rim[k, edge]
        copy = pltpu.make_async_copy(block.at[pl.ds(n, GROUP)], out.at[pl.ds(n, GROUP)], sem.at[n // GROUP])
        copy.start()
        copies.append(copy)
    for copy in copies:
        copy.wait()


def unpack_kernel(keep, got, flow, temp):
    _, lat_dev, nz, lon = keep.shape
    first = place()[0] == 0
    for t in range(lat_dev):
        for f in range(3):
            a, b = (keep[f, t], got[f, t])
            low, high = (jnp.where(first, a, b), jnp.where(first, b, a))
            if f < 2:
                flow[f, :, t, :lon] = low
                flow[f, :, t, lon:] = high
            else:
                temp[:, t, :lon] = low
                temp[:, t, lon:] = high


def call(kernel, outs, *args, scratch=(), held=True, away=False, limit=40, cost=1):
    vmem = pl.BlockSpec(memory_space=pltpu.VMEM)
    return pl.pallas_call(
        kernel,
        out_shape=[jax.ShapeDtypeStruct(s, jnp.float32) if isinstance(s, tuple) else s for s in outs],
        in_specs=[vmem if held else pl.BlockSpec(memory_space=pl.ANY)] * len(args),
        out_specs=[pl.BlockSpec(memory_space=pl.ANY) if away else vmem] * len(outs),
        scratch_shapes=[pltpu.VMEM(s, jnp.float32) if isinstance(s, tuple) else s for s in scratch],
        compiler_params=pltpu.CompilerParams(vmem_limit_bytes=limit * 2**20),
        cost_estimate=pl.CostEstimate(flops=int(cost * 10**9), transcendentals=0, bytes_accessed=int(cost * 4 * 2**20)),
    )(*args)


def both_ways(pairs):
    return sorted(pairs + [(b, a) for a, b in pairs])


def exchanges(n_row, n_col):
    chips = n_row // 2

    def dev(p, h, c):
        return (2 * p + h) * n_col + c

    partner = [(dev(p, 0, c), dev(p, 1, c)) for p in range(chips) for c in range(n_col)]
    outer = [(dev(p, 1, c), dev(p, 0, c + 1)) for p in range(chips) for c in range(n_col - 1)]
    for p in range(0, chips - 1, 2):
        outer += [(dev(p, 0, 0), dev(p + 1, 0, 0)), (dev(p, 1, n_col - 1), dev(p + 1, 1, n_col - 1))]
    lat_a = [(dev(p, h, c), dev(p + 1, h, c)) for p in range(0, chips - 1, 2) for h in (0, 1) for c in range(n_col)]
    lat_b = [(dev(p, h, c), dev(p + 1, h, c)) for p in range(1, chips - 1, 2) for h in (0, 1) for c in range(n_col)]
    ends = [0] if chips % 2 else [0, chips - 1]
    lat_b += [(dev(p, 0, c), dev(p, 1, c)) for p in ends for c in range(n_col)]
    return [both_ways(x) for x in (partner, outer, lat_a, lat_b)]


def on_device(n_row, n_col, flow, temp, tracers, bottom, sunlight, rates):
    nz, lat_dev, lon_dev = temp.shape
    _, ntr, _, lat_blk, lon = tracers.shape
    nf = ntr + EXTRA
    partner, outer, lat_a, lat_b = exchanges(n_row, n_col)

    def swap(x, pairs):
        return lax.ppermute(x, ("row", "col"), pairs)

    block = tracers[0]
    rows = lat_blk + 4
    cols, extra, some = ((nf, nz, lon), (EXTRA, nz, lon), (3, nz, lon))
    copies = pltpu.SemaphoreType.DMA((ntr // GROUP,))
    sent = (EXTRA * (lat_dev + 1), nz, lon)
    given = (flow, temp, bottom, sunlight, block)
    mine, to_partner, g_other, block = call(
        pack_ocean_kernel,
        [(EXTRA, lat_dev, nz, lon), sent, extra, block.shape],
        *[pltpu.with_memory_space_constraint(x, pltpu.HBM) for x in given],
        scratch=[
            flow.shape,
            temp.shape,
            pltpu.VMEM(bottom.shape, jnp.int32),
            sunlight.shape,
            pltpu.SemaphoreType.DMA((len(given),)),
        ],
        held=False,
    )
    got = swap(to_partner, partner)
    turned, g_tracers = call(pack_tracers_kernel, [(ntr, lat_blk, nz, lon), (ntr, nz, lon)], block)
    ocean, g_own, to_outer = call(
        join_kernel, [(EXTRA, lat_blk, nz, lon), cols, (nf // 4, nz, lon)], mine, got, to_partner, g_tracers
    )
    from_outer = swap(to_outer, outer)
    g_partner = swap(g_tracers, partner)
    full, derived = ((nf, rows, nz, lon), (3, rows, nz, lon))
    rim = (2 * nf, nz, lon)
    rows_a, rows_b, m0, dv, mix, g0, gd, inner = call(
        fill_kernel,
        [rim, rim, full, derived, jax.ShapeDtypeStruct((2 * ntr * nz, 2 * ntr * nz), jnp.bfloat16), cols, some, cols],
        turned,
        ocean,
        g_own,
        g_partner,
        got,
        g_other,
        rates,
    )
    rows_a, rows_b = (swap(rows_a, lat_a), swap(rows_b, lat_b))
    z, edge_a, edge_b = call(
        functools.partial(edge_kernel, lat_blk), [cols, (nz, lon), (nz, lon)], inner, from_outer
    )
    edge_a, edge_b = (swap(edge_a, lat_a), swap(edge_b, lat_b))
    work = [(7, rows, nz, lon), pltpu.VMEM((rows, 2 * ntr * nz, lon), jnp.bfloat16)]
    work += [(ntr + 1, rows, nz, lon), cols, cols, some]
    m1, m2 = call(inner_kernel, [full, full], m0, dv, mix, g0, gd, z, scratch=[derived] + work, cost=20)
    third = (3, lat_dev, nz, lon)
    rim, keep, send = call(
        outer_kernel,
        [(ntr, 4, nz, lon), third, third],
        m0,
        dv,
        mix,
        g0,
        gd,
        z,
        rows_a,
        rows_b,
        edge_a,
        edge_b,
        m1,
        m2,
        scratch=[full, full, derived, derived] + work,
    )
    returned = swap(send, partner)
    (out,) = call(write_kernel, [(ntr, nz, lat_blk, lon)], rim, m2, scratch=[(ntr, nz, lat_blk, lon), copies], away=True)
    flow_out, temp_out = call(
        unpack_kernel, [(2, nz, lat_dev, lon_dev), (nz, lat_dev, lon_dev)], keep, returned
    )
    return (flow_out, temp_out, out[None])


def solution(mesh):
    in_specs = (
        P(None, None, "row", "col"),
        P(None, "row", "col"),
        P("row", None, None, None, "col"),
        P("row", "col"),
        P("row", "col"),
        P(),
    )
    out_specs = (
        P(None, None, "row", "col"),
        P(None, "row", "col"),
        P("row", None, None, None, "col"),
    )
    return jax.shard_map(
        functools.partial(on_device, mesh.shape["row"], mesh.shape["col"]),
        mesh=mesh,
        in_specs=in_specs,
        out_specs=out_specs,
        check_vma=False,
    )
```

```python
import functools
import jax
import jax.numpy as jnp
from jax import lax
from jax.experimental import pallas as pl
from jax.experimental.pallas import tpu as pltpu
from jax.sharding import PartitionSpec as P

KL = 4
STEPS = 2

time_step = 0.2
viscosity = 0.2
expansion = 0.05
coriolis_base = 0.5
kappa_base = 0.05
kappa_shear = 0.2
react_step = 0.25
water_absorb = 0.1
pigment_absorb = 0.6
heat_gain = 1.0

EXTRA = 4
WIN = 4


def up(x):
    return pltpu.roll(x, 1, x.ndim - 2)


def down(x):
    return pltpu.roll(x, x.shape[-2] - 1, x.ndim - 2)


def lanes_of(shape):
    return lax.broadcasted_iota(jnp.int32, shape, len(shape) - 1)


def levels_of(shape):
    return lax.broadcasted_iota(jnp.int32, shape, len(shape) - 2)


def window(x, lat, into):
    lon = x.shape[1]
    lane = lanes_of(x.shape)
    base = WIN * (lat + 1)
    moved = pltpu.roll(x, (base + 2) % lon, 1)
    return jnp.where((lane >= base) & (lane < base + WIN), moved, into)


def place():
    row = lax.axis_index("row")
    return (row % 2, row // 2, lax.axis_index("col"))


def edge_starts(chip, lat_blk):
    odd = chip % 2
    return ((1 - odd) * (lat_blk - 2), odd * (lat_blk - 2))


def pack_ocean_kernel(flow_in, temp_in, bottom_in, sunlight_in, tracers_in, mine, to_partner, g_other, tracers, flow, temp, bottom, sunlight, sem):
    copies = [
        pltpu.make_async_copy(src, dst, sem.at[i])
        for i, (src, dst) in enumerate(
            ((flow_in, flow), (temp_in, temp), (bottom_in, bottom), (sunlight_in, sunlight), (tracers_in, tracers))
        )
    ]
    for copy in copies:
        copy.start()
    for copy in copies[:-1]:
        copy.wait()
    lat_dev, nz, lon = mine.shape[1:]
    lon_dev = temp.shape[2]
    half, _, _ = place()
    first = half == 0
    zero = jnp.zeros((nz, lon), jnp.float32)
    level = levels_of((nz, lon_dev))
    own = [zero] * EXTRA
    far = [zero] * EXTRA
    for t in range(lat_dev):
        depth = jnp.broadcast_to(bottom[t : t + 1, :], (nz, lon_dev))
        light = jnp.broadcast_to(sunlight[t : t + 1, :], (nz, lon_dev))
        wet = (level < depth).astype(jnp.float32)
        aux = jnp.where(level == 0, depth.astype(jnp.float32), jnp.where(level == 1, light, 0.0))
        for f, tile in enumerate((flow[0, :, t, :] * wet, flow[1, :, t, :] * wet, temp[:, t, :] * wet, aux)):
            low, high = (tile[:, :lon], tile[:, lon:])
            a, b = (jnp.where(first, low, high), jnp.where(first, high, low))
            mine[f, t] = a
            to_partner[f * lat_dev + t] = b
            own[f] = window(a, t, own[f])
            far[f] = window(b, t, far[f])
    shift = half * (WIN * lat_dev)
    for f in range(EXTRA):
        to_partner[EXTRA * lat_dev + f] = pltpu.roll(own[f], shift, 1)
        g_other[f] = pltpu.roll(far[f], shift, 1)
    copies[-1].wait()


def pack_tracers_kernel(tracers, turned, g_tracers):
    ntr, nz, lat_blk, lon = tracers.shape

    def some(i, _):
        g = [jnp.zeros((nz, lon), jnp.float32)] * GROUP
        for t in range(lat_blk):
            for k in range(GROUP):
                x = tracers[i * GROUP + k, :, t, :]
                turned[i * GROUP + k, t] = x
                g[k] = window(x, t, g[k])
        for k in range(GROUP):
            g_tracers[i * GROUP + k] = g[k]
        return 0

    lax.fori_loop(0, ntr // GROUP, some, 0)


def in_half(shape, half, lat_dev):
    lane = lanes_of(shape)
    base = WIN * (lat_dev * half + 1)
    return (lane >= base) & (lane < base + WIN * lat_dev)


def edge_rows(turned, ocean, start, out):
    ntr = turned.shape[0]
    for n in range(ntr):
        out[2 * n : 2 * n + 2] = turned[n, pl.ds(start, 2)]
    for f in range(EXTRA):
        out[2 * (ntr + f) : 2 * (ntr + f) + 2] = ocean[f, pl.ds(start, 2)]


def join_kernel(mine, got, to_partner, g_tracers, turned, ocean, g_own, to_outer, rows_a):
    _, lat_dev, nz, lon = mine.shape
    ntr = g_tracers.shape[0]
    nf = ntr + EXTRA
    half, chip, _ = place()
    tile = (nz, lon)
    own_lanes = in_half(tile, half, lat_dev)
    shift = (1 - half) * (WIN * lat_dev)
    g_own[:ntr] = g_tracers[...]
    for f in range(EXTRA):
        g = jnp.zeros(tile, jnp.float32)
        for t in range(lat_dev):
            x = got[f * lat_dev + t]
            ocean[f, half * lat_dev + t] = mine[f, t]
            ocean[f, (1 - half) * lat_dev + t] = x
            g = window(x, t, g)
        g_own[ntr + f] = jnp.where(own_lanes, to_partner[EXTRA * lat_dev + f], pltpu.roll(g, shift, 1))
    edge_rows(turned, ocean, edge_starts(chip, 2 * lat_dev)[0], rows_a)
    lane = lanes_of(tile)
    front, near = (lane % WIN < 2, in_half(tile, 0, 2 * lat_dev))
    side = (1 - half) * (lon - 2)
    for i in range(nf // 4):
        a, b, c, d = [pltpu.roll(g_own[4 * i + k], side, 1) for k in range(4)]
        low = jnp.where(front, a, pltpu.roll(b, 2, 1))
        high = jnp.where(front, c, pltpu.roll(d, 2, 1))
        to_outer[i] = jnp.where(near, low, pltpu.roll(high, lon // 2, 1))


def edge_kernel(turned, ocean, inner, from_outer, z, to_a, to_b):
    nf, nz, lon = z.shape
    lat_blk = turned.shape[1]

    half, chip, column = place()
    tile = (nz, lon)
    lane = lanes_of(tile)
    outer_ok = jnp.where(half == 0, column > 0, column < lax.axis_size("col") - 1)
    from_partner = (lane % WIN < 2).astype(jnp.int32) == half
    outer_lanes = in_half(tile, 0, lat_blk) & outer_ok
    start_a, start_b = edge_starts(chip, lat_blk)
    corner_a = corner_b = jnp.zeros(tile, jnp.float32)
    for f in range(nf):
        k = f % 4
        moved = pltpu.roll(from_outer[f // 4], lon + 2 * half - 2 * (k % 2) - lon // 2 * (k // 2), 1)
        cols = jnp.where(from_partner, inner[f], jnp.where(outer_lanes, moved, 0.0))
        z[f] = cols
        at = (lane >= WIN * f) & (lane < WIN * f + WIN)
        low = pltpu.roll(cols, (WIN * f - WIN) % lon, 1)
        high = pltpu.roll(cols, (WIN * f - WIN * lat_blk) % lon, 1)
        corner_a = jnp.where(at, jnp.where(start_a > 0, high, low), corner_a)
        corner_b = jnp.where(at, jnp.where(start_b > 0, high, low), corner_b)
    to_a[...] = corner_a
    edge_rows(turned, ocean, start_b, to_b)
    to_b[2 * nf] = corner_b


def kappa_of(u, v):
    du, dv = (u - down(u), v - down(v))
    sq = jnp.where(levels_of(u.shape) < u.shape[-2] - 1, du * du + dv * dv, 0.0)
    return kappa_base + kappa_shear * sq / (1.0 + sq)


def sum_above(x):
    level = levels_of(x.shape)
    k = 1
    while k < x.shape[-2]:
        x = x + jnp.where(level >= k, pltpu.roll(x, k, x.ndim - 2), 0.0)
        k *= 2
    return x


def sum_below(x):
    level, nz = (levels_of(x.shape), x.shape[-2])
    k = 1
    while k < nz:
        x = x + jnp.where(level < nz - k, pltpu.roll(x, nz - k, x.ndim - 2), 0.0)
        k *= 2
    return x


def pressure_of(heat):
    return -expansion * sum_above(heat)


def wet_of(aux):
    depth = jnp.broadcast_to(aux[..., 0:1, :], aux.shape)
    return (levels_of(aux.shape).astype(jnp.float32) < depth).astype(jnp.float32)


def light_of(aux):
    return jnp.broadcast_to(aux[..., 1:2, :], aux.shape)


def dynamics(u, v, wet, kap, prs, coriolis):
    um, ue, uw, un, us = u
    vm, ve, vw, vn, vs = v
    wm, we, ww, wn, ws = wet
    km, ke, kw, kn, ks = kap
    _, pe, pw, pn, ps = prs
    level, nz = (levels_of(um.shape), um.shape[-2])
    oe, ow, on, os_ = (wm * we, wm * ww, wm * wn, wm * ws)
    fe, fw, fn, fs = (0.5 * (um + ue) * oe, 0.5 * (um + uw) * ow, 0.5 * (vm + vn) * on, 0.5 * (vm + vs) * os_)
    ce, cw, cn, cs = (0.5 * (km + ke) * oe, 0.5 * (km + kw) * ow, 0.5 * (km + kn) * on, 0.5 * (km + ks) * os_)
    div = fe - fw + fn - fs
    total = sum_below(div)
    w_top = jnp.where(level >= 1, -total, 0.0)
    w_bot = jnp.where(level < nz - 1, -down(total), 0.0)
    weights = (
        wm * (1.0 - time_step * (ce + cw + cn + cs + 0.5 * (div + w_top - w_bot))),
        time_step * (ce - 0.5 * fe),
        time_step * (cw + 0.5 * fw),
        time_step * (cn - 0.5 * fn),
        time_step * (cs + 0.5 * fs),
        (-0.5 * time_step) * wm * w_top,
        (0.5 * time_step) * wm * w_bot,
    )
    lap_u = oe * (ue - um) + ow * (uw - um) + on * (un - um) + os_ * (us - um)
    lap_v = oe * (ve - vm) + ow * (vw - vm) + on * (vn - vm) + os_ * (vs - vm)
    new_u = wm * (um + time_step * (coriolis * vm - 0.5 * (pe - pw) + viscosity * lap_u))
    new_v = wm * (vm + time_step * (-coriolis * um - 0.5 * (pn - ps) + viscosity * lap_v))
    return (new_u, new_v, weights)


def transport(weights, x, east, west, north, south):
    a0, ae, aw, an, as_, at, ab = weights
    return (a0 * x + ae * east) + (aw * west + an * north) + (as_ * south + at * up(x)) + ab * down(x)


def saturated(x):
    return x * lax.rsqrt(1.0 + x * x)


def absorbed(pigment):
    level = levels_of(pigment.shape)
    sq = pigment * pigment
    depth = water_absorb + pigment_absorb * (sq / (1.0 + sq))
    above = jnp.where(level >= 1, up(depth), 0.0)
    k = 1
    while k < KL:
        above = above + jnp.where(level >= k, pltpu.roll(above, k, above.ndim - 2), 0.0)
        k *= 2
    return jnp.where(level < KL, jnp.exp(-above) * (1.0 - jnp.exp(-depth)), 0.0)


def two_parts(x):
    high = x.astype(jnp.bfloat16)
    return (high, (x - high.astype(jnp.float32)).astype(jnp.bfloat16))


def mix_matrix(rates, nz):
    ntr = rates.shape[0]
    size = ntr * nz
    exact = dict(precision=lax.Precision.HIGHEST, preferred_element_type=jnp.float32)
    spread = lax.broadcasted_iota(jnp.int32, (size, ntr), 0) // nz == lax.broadcasted_iota(jnp.int32, (size, ntr), 1)
    spread = spread.astype(jnp.float32)
    wide = jnp.dot(spread, rates, **exact)
    full = lax.dot_general(wide, spread, (((1,), (1,)), ((), ())), **exact)
    same = lax.broadcasted_iota(jnp.int32, (size, size), 0) % nz == lax.broadcasted_iota(jnp.int32, (size, size), 1) % nz
    high, low = two_parts(jnp.where(same, full, 0.0))
    top = jnp.concatenate([high, high], axis=1)
    return jnp.concatenate([top, jnp.concatenate([low, jnp.zeros_like(low)], axis=1)], axis=0)


def beside(z, r, lon):
    return pltpu.roll(z, lon - 2 - WIN * (r - 1), z.ndim - 1)


def sides(x, edge):
    lane, lon = (lanes_of(x.shape), x.shape[-1])
    west = pltpu.roll(jnp.where(lane == lon - 1, edge, x), 1, x.ndim - 1)
    east = pltpu.roll(jnp.where(lane == 0, edge, x), lon - 1, x.ndim - 1)
    return (east, west)


def around_rows(m, f, z, r, count):
    x = m[f, pl.ds(r, count)]
    edge = jnp.stack([beside(z, r + i, x.shape[-1]) for i in range(count)])
    return (x, *sides(x, edge), m[f, pl.ds(r + 1, count)], m[f, pl.ds(r - 1, count)])


def around_columns(x, own):
    lane, lon = (lanes_of(x.shape), x.shape[-1])
    west = pltpu.roll(jnp.where(lane % WIN == 0, x, own), 1, x.ndim - 1)
    east = pltpu.roll(jnp.where(lane % WIN == WIN - 1, x, own), lon - 1, x.ndim - 1)
    return (x, east, west, pltpu.roll(x, lon - WIN, x.ndim - 1), pltpu.roll(x, WIN, x.ndim - 1))


def coriolis_at(lat, lat_blk):
    _, chip, _ = place()
    latitude = (lat + chip * lat_blk).astype(jnp.float32)
    return coriolis_base * (2.0 * (latitude + 0.5) / (lax.axis_size("row") // 2 * lat_blk) - 1.0)


KAP, PRS, WET = (0, 1, 2)
GROUP = 4
PIECE = 3


def span(start, stop):
    return (start, stop - start, 1, stop - start)


def chunks(rows, most, body):
    first, apart, times, size = rows
    count = max(k for k in range(1, min(most, size) + 1) if size % k == 0)
    if times > 1 or count == size:
        for i in range(times):
            body(first + i * apart, size)
    else:

        def one(i, _):
            body(first + i * count, count)
            return 0

        lax.fori_loop(0, size // count, one, 0)


def derive_rows(m, dv, ntr, rows):
    def body(r, count):
        at = pl.ds(r, count)
        dv[KAP, at] = kappa_of(m[ntr, at], m[ntr + 1, at])
        dv[PRS, at] = pressure_of(m[ntr + 2, at])

    chunks(rows, 10, body)


def derive_columns(z, zd, ntr):
    zd[KAP] = kappa_of(z[ntr], z[ntr + 1])
    zd[PRS] = pressure_of(z[ntr + 2])


def ocean_rows(m, dv, z, zd, wts, new, ntr, rows):
    def body(r, count):
        at = pl.ds(r, count)
        lat = lax.broadcasted_iota(jnp.int32, (count, *m.shape[2:]), 0) + (r - 2)
        new_u, new_v, weights = dynamics(
            around_rows(m, ntr, z[ntr], r, count),
            around_rows(m, ntr + 1, z[ntr + 1], r, count),
            around_rows(dv, WET, zd[WET], r, count),
            around_rows(dv, KAP, zd[KAP], r, count),
            around_rows(dv, PRS, zd[PRS], r, count),
            coriolis_at(lat, m.shape[1] - 4),
        )
        new[ntr, at] = new_u
        new[ntr + 1, at] = new_v
        for i, w in enumerate(weights):
            wts[i, at] = w

    chunks(rows, 9, body)


def tracer_rows(m, z, wts, dv, mix, moved, sat, new, ntr, rows):
    nz, lon = m.shape[2:]
    half = ntr * nz
    first, apart, times, count = rows
    if times == 1:
        count = max(k for k in range(1, PIECE + 1) if rows[3] % k == 0)
        apart, times = (count, rows[3] // count)

    def move(r):
        weights = [wts[i, r] for i in range(7)]
        for n in range(0, ntr, GROUP):
            x = m[n : n + GROUP, r]
            edge = beside(z[n : n + GROUP], r, lon)
            done = transport(weights, x, *sides(x, edge), m[n : n + GROUP, r + 1], m[n : n + GROUP, r - 1])
            moved[n : n + GROUP, r] = done
            high, low = two_parts(saturated(done).reshape(GROUP * nz, lon))
            sat[r, n * nz : (n + GROUP) * nz, :] = high
            sat[r, half + n * nz : half + (n + GROUP) * nz, :] = low
        h = ntr + 2
        x = m[h, r]
        moved[ntr, r] = transport(weights, x, *sides(x, beside(z[h], r, lon)), m[h, r + 1], m[h, r - 1])

    def react(r):
        both = jnp.concatenate([sat[r + i] for i in range(count)], axis=1)
        res = jnp.dot(mix[...], both, preferred_element_type=jnp.float32)
        res = res[:half] + res[half:]
        for i in range(count):
            gain = react_step * dv[WET, r + i]
            for n in range(ntr):
                new[n, r + i] = moved[n, r + i] + gain * res[n * nz : (n + 1) * nz, i * lon : (i + 1) * lon]

    def move_all(r):
        for i in range(count):
            move(r + i)

    def both_parts(i, _):
        react(first + (i - 1) * apart)
        move_all(first + i * apart)
        return 0

    move_all(first)
    if rows[2] > 1:
        for i in range(1, times):
            both_parts(i, 0)
    else:
        lax.fori_loop(1, times, both_parts, 0)
    react(first + (times - 1) * apart)


def light_rows(m, dv, moved, new, ntr, rows):
    def body(r, count):
        at = pl.ds(r, count)
        light = light_of(m[ntr + 3, at]) * dv[WET, at] * absorbed(new[0, at])
        new[ntr + 2, at] = moved[ntr, at] + heat_gain * light

    chunks(rows, 9, body)


def column_step(z0, g0, zd, gd, z1, mix, ntr, lat_blk):
    nz, lon = z0.shape[1:]
    half = ntr * nz
    wet = zd[WET]
    new_u, new_v, weights = dynamics(
        around_columns(z0[ntr], g0[ntr]),
        around_columns(z0[ntr + 1], g0[ntr + 1]),
        around_columns(wet, gd[WET]),
        around_columns(zd[KAP], gd[KAP]),
        around_columns(zd[PRS], gd[PRS]),
        coriolis_at(lanes_of((nz, lon)) // WIN - 1, lat_blk),
    )
    moved = transport(weights, *around_columns(z0[:ntr], g0[:ntr]))
    high, low = two_parts(saturated(moved).reshape(half, lon))
    res = jnp.dot(mix[...], jnp.concatenate([high, low], axis=0), preferred_element_type=jnp.float32)
    done = moved + (react_step * wet) * (res[:half] + res[half:]).reshape(ntr, nz, lon)
    z1[:ntr] = done
    z1[ntr] = new_u
    z1[ntr + 1] = new_v
    heat = transport(weights, *around_columns(z0[ntr + 2], g0[ntr + 2]))
    z1[ntr + 2] = heat + heat_gain * light_of(z0[ntr + 3]) * wet * absorbed(done[0])


def fill_kernel(turned, ocean, g_own, g_partner, got, g_other, rates, m0, dv, mix, g0, gd, inner):
    ntr, lat_blk, nz, lon = turned.shape
    half, _, _ = place()
    inner[:ntr] = g_partner[...]
    for f in range(EXTRA):
        theirs = got[EXTRA * (lat_blk // 2) + f]
        inner[ntr + f] = jnp.where(in_half((nz, lon), half, lat_blk // 2), g_other[f], theirs)
    mix[...] = mix_matrix(rates[...], nz)
    own = span(2, lat_blk + 2)

    def wets(r, count):
        at = pl.ds(r, count)
        for f in range(EXTRA):
            m0[ntr + f, at] = ocean[f, pl.ds(r - 2, count)]
        dv[WET, at] = wet_of(ocean[EXTRA - 1, pl.ds(r - 2, count)])

    chunks(own, 8, wets)

    def some(r, count):
        wet = dv[WET, r]
        for n in range(ntr):
            m0[n, r] = turned[n, r - 2] * wet

    chunks(own, 1, some)
    derive_rows(m0, dv, ntr, own)
    mask_columns([g_own[f] for f in range(ntr + EXTRA)], g0, gd)


def mask_columns(fields, z, zd):
    ntr = len(fields) - EXTRA
    wet = wet_of(fields[-1])
    zd[WET] = wet
    for f, cols in enumerate(fields):
        z[f] = cols * wet if f < ntr else cols
    derive_columns(z, zd, ntr)


def inner_kernel(m0, dv, mix, g0, gd, z_in, m1, m2, dv1, wts, sat, moved, z0, z1, zd):
    nf, rows, _, _ = m0.shape
    ntr = nf - EXTRA
    mask_columns([z_in[f] for f in range(nf)], z0, zd)
    column_step(z0, g0, zd, gd, z1, mix, ntr, rows - 4)
    now = span(3, rows - 3)
    ocean_rows(m0, dv, z0, zd, wts, m1, ntr, now)
    tracer_rows(m0, z0, wts, dv, mix, moved, sat, m1, ntr, now)
    light_rows(m0, dv, moved, m1, ntr, now)
    dv1[WET, 3 : rows - 3] = dv[WET, 3 : rows - 3]
    derive_rows(m1, dv1, ntr, now)
    derive_columns(z1, zd, ntr)
    now = span(4, rows - 4)
    ocean_rows(m1, dv1, z1, zd, wts, m2, ntr, now)
    tracer_rows(m1, z1, wts, dv1, mix, moved, sat, m2, ntr, now)
    light_rows(m0, dv1, moved, m2, ntr, now)


def outer_kernel(m_own, dv_own, mix, g0, gd, z_in, rows_a, rows_b, edge_a, m1_in, m2_in, rim, keep, send, m0, m1, dv0, dv1, wts, sat, moved, z0, z1, zd):
    nf, rows, nz, lon = m_own.shape
    ntr = nf - EXTRA
    lat_blk = rows - 4
    half, chip, _ = place()
    even = chip % 2 == 0
    south_ok, north_ok = (chip > 0, chip < lax.axis_size("row") // 2 - 1)

    def got(high, a, b):
        picked = jnp.where(even, a, b) if high else jnp.where(even, b, a)
        return jnp.where(north_ok if high else south_ok, picked, 0.0)

    for high, start in ((False, 0), (True, rows - 2)):
        for f in range(EXTRA):
            m0[ntr + f, start : start + 2] = got(high, *(x[pl.ds(2 * (ntr + f), 2)] for x in (rows_a, rows_b)))
        wet = wet_of(m0[nf - 1, start : start + 2])
        dv0[WET, start : start + 2] = wet
        for n in range(ntr):
            m0[n, start : start + 2] = got(high, *(x[pl.ds(2 * n, 2)] for x in (rows_a, rows_b))) * wet
        derive_rows(m0, dv0, ntr, span(start, start + 2))
    for start in (2, rows - 4):
        m0[:, start : start + 2] = m_own[:, start : start + 2]
        dv0[:, start : start + 2] = dv_own[:, start : start + 2]
    lane = lanes_of((nz, lon))
    low, high = (got(side, edge_a[...], rows_b[2 * nf]) for side in (False, True))
    at_low, at_high = (lane < WIN, (lane >= WIN * (lat_blk + 1)) & (lane < WIN * (lat_blk + 2)))
    fields = []
    for f in range(nf):
        cols = jnp.where(at_low, pltpu.roll(low, (-WIN * f) % lon, 1), z_in[f])
        fields.append(jnp.where(at_high, pltpu.roll(high, (WIN * (lat_blk + 1) - WIN * f) % lon, 1), cols))
    mask_columns(fields, z0, zd)
    column_step(z0, g0, zd, gd, z1, mix, ntr, lat_blk)
    now = (1, lat_blk, 2, 2)
    ocean_rows(m0, dv0, z0, zd, wts, m1, ntr, now)
    tracer_rows(m0, z0, wts, dv0, mix, moved, sat, m1, ntr, now)
    light_rows(m0, dv0, moved, m1, ntr, now)
    for start in (3, rows - 5):
        m1[:, start : start + 2] = m1_in[:, start : start + 2]
    for start in (1, rows - 3):
        dv1[WET, start : start + 2] = dv0[WET, start : start + 2]
    for start in (3, rows - 5):
        dv1[WET, start : start + 2] = dv_own[WET, start : start + 2]
    derive_rows(m1, dv1, ntr, (1, rows - 6, 2, 4))
    derive_columns(z1, zd, ntr)
    now = (2, rows - 6, 2, 2)
    ocean_rows(m1, dv1, z1, zd, wts, m0, ntr, now)
    tracer_rows(m1, z1, wts, dv1, mix, moved, sat, m0, ntr, now)
    light_rows(m0, dv1, moved, m0, ntr, now)

    rim[:, 0:2] = m0[:ntr, 2:4]
    rim[:, 2:4] = m0[:ntr, rows - 4 : rows - 2]
    m0[ntr : ntr + 3, 4 : rows - 4] = m2_in[ntr : ntr + 3, 4 : rows - 4]
    count = lat_blk // 2
    for f in range(3):
        keep[f] = m0[ntr + f, pl.ds(2 + half * count, count)]
        send[f] = m0[ntr + f, pl.ds(2 + (1 - half) * count, count)]


def write_kernel(rim, m, out, block, sem):
    ntr, nz, lat_blk, lon = block.shape
    copies = []
    for n in range(0, ntr, GROUP):
        for k in range(n, n + GROUP):
            for t in range(lat_blk):
                edge = {0: 0, 1: 1, lat_blk - 2: 2, lat_blk - 1: 3}.get(t)
                block[k, :, t, :] = m[k, t + 2] if edge is None else rim[k, edge]
        copy = pltpu.make_async_copy(block.at[pl.ds(n, GROUP)], out.at[pl.ds(n, GROUP)], sem.at[n // GROUP])
        copy.start()
        copies.append(copy)
    for copy in copies:
        copy.wait()


def unpack_kernel(keep, got, flow, temp):
    _, lat_dev, nz, lon = keep.shape
    first = place()[0] == 0
    for t in range(lat_dev):
        for f in range(3):
            a, b = (keep[f, t], got[f, t])
            low, high = (jnp.where(first, a, b), jnp.where(first, b, a))
            if f < 2:
                flow[f, :, t, :lon] = low
                flow[f, :, t, lon:] = high
            else:
                temp[:, t, :lon] = low
                temp[:, t, lon:] = high


def call(kernel, outs, *args, scratch=(), held=True, away=False, limit=40, cost=1):
    vmem = pl.BlockSpec(memory_space=pltpu.VMEM)
    return pl.pallas_call(
        kernel,
        out_shape=[jax.ShapeDtypeStruct(s, jnp.float32) if isinstance(s, tuple) else s for s in outs],
        in_specs=[vmem if held else pl.BlockSpec(memory_space=pl.ANY)] * len(args),
        out_specs=[pl.BlockSpec(memory_space=pl.ANY) if away else vmem] * len(outs),
        scratch_shapes=[pltpu.VMEM(s, jnp.float32) if isinstance(s, tuple) else s for s in scratch],
        compiler_params=pltpu.CompilerParams(vmem_limit_bytes=limit * 2**20),
        cost_estimate=pl.CostEstimate(flops=int(cost * 10**9), transcendentals=0, bytes_accessed=int(cost * 4 * 2**20)),
    )(*args)


def both_ways(pairs):
    return sorted(pairs + [(b, a) for a, b in pairs])


def exchanges(n_row, n_col):
    chips = n_row // 2

    def dev(p, h, c):
        return (2 * p + h) * n_col + c

    partner = [(dev(p, 0, c), dev(p, 1, c)) for p in range(chips) for c in range(n_col)]
    outer = [(dev(p, 1, c), dev(p, 0, c + 1)) for p in range(chips) for c in range(n_col - 1)]
    for p in range(0, chips - 1, 2):
        outer += [(dev(p, 0, 0), dev(p + 1, 0, 0)), (dev(p, 1, n_col - 1), dev(p + 1, 1, n_col - 1))]
    lat_a = [(dev(p, h, c), dev(p + 1, h, c)) for p in range(0, chips - 1, 2) for h in (0, 1) for c in range(n_col)]
    lat_b = [(dev(p, h, c), dev(p + 1, h, c)) for p in range(1, chips - 1, 2) for h in (0, 1) for c in range(n_col)]
    ends = [0] if chips % 2 else [0, chips - 1]
    lat_b += [(dev(p, 0, c), dev(p, 1, c)) for p in ends for c in range(n_col)]
    return [both_ways(x) for x in (partner, outer, lat_a, lat_b)]


def on_device(n_row, n_col, flow, temp, tracers, bottom, sunlight, rates):
    nz, lat_dev, lon_dev = temp.shape
    _, ntr, _, lat_blk, lon = tracers.shape
    nf = ntr + EXTRA
    partner, outer, lat_a, lat_b = exchanges(n_row, n_col)

    def swap(x, pairs):
        return lax.ppermute(x, ("row", "col"), pairs)

    block = tracers[0]
    rows = lat_blk + 4
    cols, extra, some = ((nf, nz, lon), (EXTRA, nz, lon), (3, nz, lon))
    copies = pltpu.SemaphoreType.DMA((ntr // GROUP,))
    sent = (EXTRA * (lat_dev + 1), nz, lon)
    given = (flow, temp, bottom, sunlight, block)
    mine, to_partner, g_other, block = call(
        pack_ocean_kernel,
        [(EXTRA, lat_dev, nz, lon), sent, extra, block.shape],
        *[pltpu.with_memory_space_constraint(x, pltpu.HBM) for x in given],
        scratch=[
            flow.shape,
            temp.shape,
            pltpu.VMEM(bottom.shape, jnp.int32),
            sunlight.shape,
            pltpu.SemaphoreType.DMA((len(given),)),
        ],
        held=False,
    )
    got = swap(to_partner, partner)
    turned, g_tracers = call(pack_tracers_kernel, [(ntr, lat_blk, nz, lon), (ntr, nz, lon)], block)
    rim = (2 * nf, nz, lon)
    ocean, g_own, to_outer, rows_a = call(
        join_kernel,
        [(EXTRA, lat_blk, nz, lon), cols, (nf // 4, nz, lon), rim],
        mine,
        got,
        to_partner,
        g_tracers,
        turned,
    )
    rows_a = swap(rows_a, lat_a)
    from_outer = swap(to_outer, outer)
    g_partner = swap(g_tracers, partner)
    full, derived = ((nf, rows, nz, lon), (3, rows, nz, lon))
    m0, dv, mix, g0, gd, inner = call(
        fill_kernel,
        [full, derived, jax.ShapeDtypeStruct((2 * ntr * nz, 2 * ntr * nz), jnp.bfloat16), cols, some, cols],
        turned,
        ocean,
        g_own,
        g_partner,
        got,
        g_other,
        rates,
    )
    z, edge_a, rows_b = call(
        edge_kernel, [cols, (nz, lon), (2 * nf + 1, nz, lon)], turned, ocean, inner, from_outer
    )
    rows_b, edge_a = (swap(rows_b, lat_b), swap(edge_a, lat_a))
    work = [(7, rows, nz, lon), pltpu.VMEM((rows, 2 * ntr * nz, lon), jnp.bfloat16)]
    work += [(ntr + 1, rows, nz, lon), cols, cols, some]
    m1, m2 = call(inner_kernel, [full, full], m0, dv, mix, g0, gd, z, scratch=[derived] + work, cost=20)
    third = (3, lat_dev, nz, lon)
    rim, keep, send = call(
        outer_kernel,
        [(ntr, 4, nz, lon), third, third],
        m0,
        dv,
        mix,
        g0,
        gd,
        z,
        rows_a,
        rows_b,
        edge_a,
        m1,
        m2,
        scratch=[full, full, derived, derived] + work,
    )
    returned = swap(send, partner)
    (out,) = call(write_kernel, [(ntr, nz, lat_blk, lon)], rim, m2, scratch=[(ntr, nz, lat_blk, lon), copies], away=True)
    flow_out, temp_out = call(
        unpack_kernel, [(2, nz, lat_dev, lon_dev), (nz, lat_dev, lon_dev)], keep, returned
    )
    return (flow_out, temp_out, out[None])


def solution(mesh):
    in_specs = (
        P(None, None, "row", "col"),
        P(None, "row", "col"),
        P("row", None, None, None, "col"),
        P("row", "col"),
        P("row", "col"),
        P(),
    )
    out_specs = (
        P(None, None, "row", "col"),
        P(None, "row", "col"),
        P("row", None, None, None, "col"),
    )
    return jax.shard_map(
        functools.partial(on_device, mesh.shape["row"], mesh.shape["col"]),
        mesh=mesh,
        in_specs=in_specs,
        out_specs=out_specs,
        check_vma=False,
    )
```

```python
import functools
import jax
import jax.numpy as jnp
from jax import lax
from jax.experimental import pallas as pl
from jax.experimental.pallas import tpu as pltpu
from jax.sharding import PartitionSpec as P

KL = 4
STEPS = 2

time_step = 0.2
viscosity = 0.2
expansion = 0.05
coriolis_base = 0.5
kappa_base = 0.05
kappa_shear = 0.2
react_step = 0.25
water_absorb = 0.1
pigment_absorb = 0.6
heat_gain = 1.0

EXTRA = 4
WIN = 4


def up(x):
    return pltpu.roll(x, 1, x.ndim - 2)


def down(x):
    return pltpu.roll(x, x.shape[-2] - 1, x.ndim - 2)


def lanes_of(shape):
    return lax.broadcasted_iota(jnp.int32, shape, len(shape) - 1)


def levels_of(shape):
    return lax.broadcasted_iota(jnp.int32, shape, len(shape) - 2)


def window(x, lat, into):
    lon = x.shape[1]
    lane = lanes_of(x.shape)
    base = WIN * (lat + 1)
    moved = pltpu.roll(x, (base + 2) % lon, 1)
    return jnp.where((lane >= base) & (lane < base + WIN), moved, into)


def place():
    row = lax.axis_index("row")
    return (row % 2, row // 2, lax.axis_index("col"))


def edge_starts(chip, lat_blk):
    odd = chip % 2
    return ((1 - odd) * (lat_blk - 2), odd * (lat_blk - 2))


def pack_ocean_kernel(flow_in, temp_in, bottom_in, sunlight_in, tracers_in, mine, to_partner, g_other, tracers, flow, temp, bottom, sunlight, sem):
    copies = [
        pltpu.make_async_copy(src, dst, sem.at[i])
        for i, (src, dst) in enumerate(
            ((flow_in, flow), (temp_in, temp), (bottom_in, bottom), (sunlight_in, sunlight), (tracers_in, tracers))
        )
    ]
    for copy in copies:
        copy.start()
    for copy in copies[:-1]:
        copy.wait()
    lat_dev, nz, lon = mine.shape[1:]
    lon_dev = temp.shape[2]
    half, _, _ = place()
    first = half == 0
    zero = jnp.zeros((nz, lon), jnp.float32)
    level = levels_of((nz, lon_dev))
    own = [zero] * EXTRA
    far = [zero] * EXTRA
    for t in range(lat_dev):
        depth = jnp.broadcast_to(bottom[t : t + 1, :], (nz, lon_dev))
        light = jnp.broadcast_to(sunlight[t : t + 1, :], (nz, lon_dev))
        wet = (level < depth).astype(jnp.float32)
        aux = jnp.where(level == 0, depth.astype(jnp.float32), jnp.where(level == 1, light, 0.0))
        for f, tile in enumerate((flow[0, :, t, :] * wet, flow[1, :, t, :] * wet, temp[:, t, :] * wet, aux)):
            low, high = (tile[:, :lon], tile[:, lon:])
            a, b = (jnp.where(first, low, high), jnp.where(first, high, low))
            mine[f, t] = a
            to_partner[f * lat_dev + t] = b
            own[f] = window(a, t, own[f])
            far[f] = window(b, t, far[f])
    shift = half * (WIN * lat_dev)
    for f in range(EXTRA):
        to_partner[EXTRA * lat_dev + f] = pltpu.roll(own[f], shift, 1)
        g_other[f] = pltpu.roll(far[f], shift, 1)
    copies[-1].wait()


def pack_tracers_kernel(tracers, turned, g_tracers):
    ntr, nz, lat_blk, lon = tracers.shape

    def some(i, _):
        g = [jnp.zeros((nz, lon), jnp.float32)] * GROUP
        for t in range(lat_blk):
            for k in range(GROUP):
                x = tracers[i * GROUP + k, :, t, :]
                turned[i * GROUP + k, t] = x
                g[k] = window(x, t, g[k])
        for k in range(GROUP):
            g_tracers[i * GROUP + k] = g[k]
        return 0

    lax.fori_loop(0, ntr // GROUP, some, 0)


def in_half(shape, half, lat_dev):
    lane = lanes_of(shape)
    base = WIN * (lat_dev * half + 1)
    return (lane >= base) & (lane < base + WIN * lat_dev)


def edge_rows(turned, ocean, start, out):
    ntr = turned.shape[0]
    for n in range(ntr):
        out[2 * n : 2 * n + 2] = turned[n, pl.ds(start, 2)]
    for f in range(EXTRA):
        out[2 * (ntr + f) : 2 * (ntr + f) + 2] = ocean[f, pl.ds(start, 2)]


def join_kernel(mine, got, to_partner, g_tracers, turned, ocean, g_own, to_outer, rows_a):
    _, lat_dev, nz, lon = mine.shape
    ntr = g_tracers.shape[0]
    nf = ntr + EXTRA
    half, chip, _ = place()
    tile = (nz, lon)
    own_lanes = in_half(tile, half, lat_dev)
    shift = (1 - half) * (WIN * lat_dev)
    g_own[:ntr] = g_tracers[...]
    for f in range(EXTRA):
        g = jnp.zeros(tile, jnp.float32)
        for t in range(lat_dev):
            x = got[f * lat_dev + t]
            ocean[f, half * lat_dev + t] = mine[f, t]
            ocean[f, (1 - half) * lat_dev + t] = x
            g = window(x, t, g)
        g_own[ntr + f] = jnp.where(own_lanes, to_partner[EXTRA * lat_dev + f], pltpu.roll(g, shift, 1))
    edge_rows(turned, ocean, edge_starts(chip, 2 * lat_dev)[0], rows_a)
    lane = lanes_of(tile)
    front, near = (lane % WIN < 2, in_half(tile, 0, 2 * lat_dev))
    side = (1 - half) * (lon - 2)
    for i in range(nf // 4):
        a, b, c, d = [pltpu.roll(g_own[4 * i + k], side, 1) for k in range(4)]
        low = jnp.where(front, a, pltpu.roll(b, 2, 1))
        high = jnp.where(front, c, pltpu.roll(d, 2, 1))
        to_outer[i] = jnp.where(near, low, pltpu.roll(high, lon // 2, 1))


def edge_kernel(turned, ocean, inner, from_outer, z, to_a, to_b):
    nf, nz, lon = z.shape
    lat_blk = turned.shape[1]

    half, chip, column = place()
    tile = (nz, lon)
    lane = lanes_of(tile)
    outer_ok = jnp.where(half == 0, column > 0, column < lax.axis_size("col") - 1)
    from_partner = (lane % WIN < 2).astype(jnp.int32) == half
    outer_lanes = in_half(tile, 0, lat_blk) & outer_ok
    start_a, start_b = edge_starts(chip, lat_blk)
    corner_a = corner_b = jnp.zeros(tile, jnp.float32)
    for f in range(nf):
        k = f % 4
        moved = pltpu.roll(from_outer[f // 4], lon + 2 * half - 2 * (k % 2) - lon // 2 * (k // 2), 1)
        cols = jnp.where(from_partner, inner[f], jnp.where(outer_lanes, moved, 0.0))
        z[f] = cols
        at = (lane >= WIN * f) & (lane < WIN * f + WIN)
        low = pltpu.roll(cols, (WIN * f - WIN) % lon, 1)
        high = pltpu.roll(cols, (WIN * f - WIN * lat_blk) % lon, 1)
        corner_a = jnp.where(at, jnp.where(start_a > 0, high, low), corner_a)
        corner_b = jnp.where(at, jnp.where(start_b > 0, high, low), corner_b)
    to_a[...] = corner_a
    edge_rows(turned, ocean, start_b, to_b)
    to_b[2 * nf] = corner_b


def kappa_of(u, v):
    du, dv = (u - down(u), v - down(v))
    sq = jnp.where(levels_of(u.shape) < u.shape[-2] - 1, du * du + dv * dv, 0.0)
    return kappa_base + kappa_shear * sq / (1.0 + sq)


def sum_above(x):
    level = levels_of(x.shape)
    k = 1
    while k < x.shape[-2]:
        x = x + jnp.where(level >= k, pltpu.roll(x, k, x.ndim - 2), 0.0)
        k *= 2
    return x


def sum_below(x):
    level, nz = (levels_of(x.shape), x.shape[-2])
    k = 1
    while k < nz:
        x = x + jnp.where(level < nz - k, pltpu.roll(x, nz - k, x.ndim - 2), 0.0)
        k *= 2
    return x


def pressure_of(heat):
    return -expansion * sum_above(heat)


def wet_of(aux):
    depth = jnp.broadcast_to(aux[..., 0:1, :], aux.shape)
    return (levels_of(aux.shape).astype(jnp.float32) < depth).astype(jnp.float32)


def light_of(aux):
    return jnp.broadcast_to(aux[..., 1:2, :], aux.shape)


def dynamics(u, v, wet, kap, prs, coriolis):
    um, ue, uw, un, us = u
    vm, ve, vw, vn, vs = v
    wm, we, ww, wn, ws = wet
    km, ke, kw, kn, ks = kap
    _, pe, pw, pn, ps = prs
    level, nz = (levels_of(um.shape), um.shape[-2])
    oe, ow, on, os_ = (wm * we, wm * ww, wm * wn, wm * ws)
    fe, fw, fn, fs = (0.5 * (um + ue) * oe, 0.5 * (um + uw) * ow, 0.5 * (vm + vn) * on, 0.5 * (vm + vs) * os_)
    ce, cw, cn, cs = (0.5 * (km + ke) * oe, 0.5 * (km + kw) * ow, 0.5 * (km + kn) * on, 0.5 * (km + ks) * os_)
    div = fe - fw + fn - fs
    total = sum_below(div)
    w_top = jnp.where(level >= 1, -total, 0.0)
    w_bot = jnp.where(level < nz - 1, -down(total), 0.0)
    weights = (
        wm * (1.0 - time_step * (ce + cw + cn + cs + 0.5 * (div + w_top - w_bot))),
        time_step * (ce - 0.5 * fe),
        time_step * (cw + 0.5 * fw),
        time_step * (cn - 0.5 * fn),
        time_step * (cs + 0.5 * fs),
        (-0.5 * time_step) * wm * w_top,
        (0.5 * time_step) * wm * w_bot,
    )
    lap_u = oe * (ue - um) + ow * (uw - um) + on * (un - um) + os_ * (us - um)
    lap_v = oe * (ve - vm) + ow * (vw - vm) + on * (vn - vm) + os_ * (vs - vm)
    new_u = wm * (um + time_step * (coriolis * vm - 0.5 * (pe - pw) + viscosity * lap_u))
    new_v = wm * (vm + time_step * (-coriolis * um - 0.5 * (pn - ps) + viscosity * lap_v))
    return (new_u, new_v, weights)


def transport(weights, x, east, west, north, south):
    a0, ae, aw, an, as_, at, ab = weights
    return (a0 * x + ae * east) + (aw * west + an * north) + (as_ * south + at * up(x)) + ab * down(x)


def saturated(x):
    return x * lax.rsqrt(1.0 + x * x)


def absorbed(pigment):
    level = levels_of(pigment.shape)
    sq = pigment * pigment
    depth = water_absorb + pigment_absorb * (sq / (1.0 + sq))
    above = jnp.where(level >= 1, up(depth), 0.0)
    k = 1
    while k < KL:
        above = above + jnp.where(level >= k, pltpu.roll(above, k, above.ndim - 2), 0.0)
        k *= 2
    return jnp.where(level < KL, jnp.exp(-above) * (1.0 - jnp.exp(-depth)), 0.0)


def two_parts(x):
    high = x.astype(jnp.bfloat16)
    return (high, (x - high.astype(jnp.float32)).astype(jnp.bfloat16))


def mix_matrix(rates, nz):
    ntr = rates.shape[0]
    size = ntr * nz
    exact = dict(precision=lax.Precision.HIGHEST, preferred_element_type=jnp.float32)
    spread = lax.broadcasted_iota(jnp.int32, (size, ntr), 0) // nz == lax.broadcasted_iota(jnp.int32, (size, ntr), 1)
    spread = spread.astype(jnp.float32)
    wide = jnp.dot(spread, rates, **exact)
    full = lax.dot_general(wide, spread, (((1,), (1,)), ((), ())), **exact)
    same = lax.broadcasted_iota(jnp.int32, (size, size), 0) % nz == lax.broadcasted_iota(jnp.int32, (size, size), 1) % nz
    high, low = two_parts(jnp.where(same, full, 0.0))
    top = jnp.concatenate([high, high], axis=1)
    return jnp.concatenate([top, jnp.concatenate([low, jnp.zeros_like(low)], axis=1)], axis=0)


def beside(z, r, lon):
    return pltpu.roll(z, lon - 2 - WIN * (r - 1), z.ndim - 1)


def sides(x, edge):
    lane, lon = (lanes_of(x.shape), x.shape[-1])
    west = pltpu.roll(jnp.where(lane == lon - 1, edge, x), 1, x.ndim - 1)
    east = pltpu.roll(jnp.where(lane == 0, edge, x), lon - 1, x.ndim - 1)
    return (east, west)


def around_rows(m, f, z, r, count):
    x = m[f, pl.ds(r, count)]
    edge = jnp.stack([beside(z, r + i, x.shape[-1]) for i in range(count)])
    return (x, *sides(x, edge), m[f, pl.ds(r + 1, count)], m[f, pl.ds(r - 1, count)])


def around_columns(x, own):
    lane, lon = (lanes_of(x.shape), x.shape[-1])
    west = pltpu.roll(jnp.where(lane % WIN == 0, x, own), 1, x.ndim - 1)
    east = pltpu.roll(jnp.where(lane % WIN == WIN - 1, x, own), lon - 1, x.ndim - 1)
    return (x, east, west, pltpu.roll(x, lon - WIN, x.ndim - 1), pltpu.roll(x, WIN, x.ndim - 1))


def coriolis_at(lat, lat_blk):
    _, chip, _ = place()
    latitude = (lat + chip * lat_blk).astype(jnp.float32)
    return coriolis_base * (2.0 * (latitude + 0.5) / (lax.axis_size("row") // 2 * lat_blk) - 1.0)


KAP, PRS, WET = (0, 1, 2)
GROUP = 4
PIECE = 3


def span(start, stop):
    return (start, stop - start, 1, stop - start)


def chunks(rows, most, body):
    first, apart, times, size = rows
    count = max(k for k in range(1, min(most, size) + 1) if size % k == 0)
    if times > 1 or count == size:
        for i in range(times):
            body(first + i * apart, size)
    else:

        def one(i, _):
            body(first + i * count, count)
            return 0

        lax.fori_loop(0, size // count, one, 0)


def derive_rows(m, dv, ntr, rows):
    def body(r, count):
        at = pl.ds(r, count)
        dv[KAP, at] = kappa_of(m[ntr, at], m[ntr + 1, at])
        dv[PRS, at] = pressure_of(m[ntr + 2, at])

    chunks(rows, 10, body)


def derive_columns(z, zd, ntr):
    zd[KAP] = kappa_of(z[ntr], z[ntr + 1])
    zd[PRS] = pressure_of(z[ntr + 2])


def ocean_rows(m, dv, z, zd, wts, new, ntr, rows):
    def body(r, count):
        at = pl.ds(r, count)
        lat = lax.broadcasted_iota(jnp.int32, (count, *m.shape[2:]), 0) + (r - 2)
        new_u, new_v, weights = dynamics(
            around_rows(m, ntr, z[ntr], r, count),
            around_rows(m, ntr + 1, z[ntr + 1], r, count),
            around_rows(dv, WET, zd[WET], r, count),
            around_rows(dv, KAP, zd[KAP], r, count),
            around_rows(dv, PRS, zd[PRS], r, count),
            coriolis_at(lat, m.shape[1] - 4),
        )
        new[ntr, at] = new_u
        new[ntr + 1, at] = new_v
        for i, w in enumerate(weights):
            wts[i, at] = w

    chunks(rows, 9, body)


def tracer_rows(m, z, wts, dv, mix, moved, sat, new, ntr, rows):
    nz, lon = m.shape[2:]
    half = ntr * nz
    first, apart, times, count = rows
    if times == 1:
        count = max(k for k in range(1, PIECE + 1) if rows[3] % k == 0)
        apart, times = (count, rows[3] // count)

    def move(r):
        weights = [wts[i, r] for i in range(7)]
        for n in range(0, ntr, GROUP):
            x = m[n : n + GROUP, r]
            edge = beside(z[n : n + GROUP], r, lon)
            done = transport(weights, x, *sides(x, edge), m[n : n + GROUP, r + 1], m[n : n + GROUP, r - 1])
            moved[n : n + GROUP, r] = done
            high, low = two_parts(saturated(done).reshape(GROUP * nz, lon))
            sat[r, n * nz : (n + GROUP) * nz, :] = high
            sat[r, half + n * nz : half + (n + GROUP) * nz, :] = low
        h = ntr + 2
        x = m[h, r]
        moved[ntr, r] = transport(weights, x, *sides(x, beside(z[h], r, lon)), m[h, r + 1], m[h, r - 1])

    def react(r):
        both = jnp.concatenate([sat[r + i] for i in range(count)], axis=1)
        res = jnp.dot(mix[...], both, preferred_element_type=jnp.float32)
        res = res[:half] + res[half:]
        for i in range(count):
            gain = react_step * dv[WET, r + i]
            for n in range(ntr):
                new[n, r + i] = moved[n, r + i] + gain * res[n * nz : (n + 1) * nz, i * lon : (i + 1) * lon]

    def move_all(r):
        for i in range(count):
            move(r + i)

    def both_parts(i, _):
        react(first + (i - 1) * apart)
        move_all(first + i * apart)
        return 0

    move_all(first)
    if rows[2] > 1:
        for i in range(1, times):
            both_parts(i, 0)
    else:
        lax.fori_loop(1, times, both_parts, 0)
    react(first + (times - 1) * apart)


def light_rows(m, dv, moved, new, ntr, rows):
    def body(r, count):
        at = pl.ds(r, count)
        light = light_of(m[ntr + 3, at]) * dv[WET, at] * absorbed(new[0, at])
        new[ntr + 2, at] = moved[ntr, at] + heat_gain * light

    chunks(rows, 9, body)


def column_step(z0, g0, zd, gd, z1, mix, ntr, lat_blk):
    nz, lon = z0.shape[1:]
    half = ntr * nz
    wet = zd[WET]
    new_u, new_v, weights = dynamics(
        around_columns(z0[ntr], g0[ntr]),
        around_columns(z0[ntr + 1], g0[ntr + 1]),
        around_columns(wet, gd[WET]),
        around_columns(zd[KAP], gd[KAP]),
        around_columns(zd[PRS], gd[PRS]),
        coriolis_at(lanes_of((nz, lon)) // WIN - 1, lat_blk),
    )
    moved = transport(weights, *around_columns(z0[:ntr], g0[:ntr]))
    high, low = two_parts(saturated(moved).reshape(half, lon))
    res = jnp.dot(mix[...], jnp.concatenate([high, low], axis=0), preferred_element_type=jnp.float32)
    done = moved + (react_step * wet) * (res[:half] + res[half:]).reshape(ntr, nz, lon)
    z1[:ntr] = done
    z1[ntr] = new_u
    z1[ntr + 1] = new_v
    heat = transport(weights, *around_columns(z0[ntr + 2], g0[ntr + 2]))
    z1[ntr + 2] = heat + heat_gain * light_of(z0[ntr + 3]) * wet * absorbed(done[0])


def fill_kernel(turned, ocean, g_own, g_partner, got, g_other, rates, m0, dv, mix, g0, gd, inner):
    ntr, lat_blk, nz, lon = turned.shape
    half, _, _ = place()
    inner[:ntr] = g_partner[...]
    for f in range(EXTRA):
        theirs = got[EXTRA * (lat_blk // 2) + f]
        inner[ntr + f] = jnp.where(in_half((nz, lon), half, lat_blk // 2), g_other[f], theirs)
    mix[...] = mix_matrix(rates[...], nz)
    own = span(2, lat_blk + 2)

    def wets(r, count):
        at = pl.ds(r, count)
        for f in range(EXTRA):
            m0[ntr + f, at] = ocean[f, pl.ds(r - 2, count)]
        dv[WET, at] = wet_of(ocean[EXTRA - 1, pl.ds(r - 2, count)])

    chunks(own, 8, wets)

    def some(r, count):
        wet = dv[WET, r]
        for n in range(ntr):
            m0[n, r] = turned[n, r - 2] * wet

    chunks(own, 1, some)
    derive_rows(m0, dv, ntr, own)
    mask_columns([g_own[f] for f in range(ntr + EXTRA)], g0, gd)


def mask_columns(fields, z, zd):
    ntr = len(fields) - EXTRA
    wet = wet_of(fields[-1])
    zd[WET] = wet
    for f, cols in enumerate(fields):
        z[f] = cols * wet if f < ntr else cols
    derive_columns(z, zd, ntr)


def inner_kernel(m0, dv, mix, g0, gd, z_in, m1, m2, dv1, wts, sat, moved, z0, z1, zd):
    nf, rows, _, _ = m0.shape
    ntr = nf - EXTRA
    mask_columns([z_in[f] for f in range(nf)], z0, zd)
    column_step(z0, g0, zd, gd, z1, mix, ntr, rows - 4)
    now = span(3, rows - 3)
    ocean_rows(m0, dv, z0, zd, wts, m1, ntr, now)
    tracer_rows(m0, z0, wts, dv, mix, moved, sat, m1, ntr, now)
    light_rows(m0, dv, moved, m1, ntr, now)
    dv1[WET, 3 : rows - 3] = dv[WET, 3 : rows - 3]
    derive_rows(m1, dv1, ntr, now)
    derive_columns(z1, zd, ntr)
    now = span(4, rows - 4)
    ocean_rows(m1, dv1, z1, zd, wts, m2, ntr, now)
    tracer_rows(m1, z1, wts, dv1, mix, moved, sat, m2, ntr, now)
    light_rows(m0, dv1, moved, m2, ntr, now)


def outer_kernel(m_own, dv_own, mix, g0, gd, z_in, rows_a, rows_b, edge_a, m1_in, m2_in, out, rim, keep, send, m0, m1, dv0, dv1, wts, sat, moved, z0, z1, zd, sem):
    nf, rows, nz, lon = m_own.shape
    ntr = nf - EXTRA
    lat_blk = rows - 4
    half, chip, _ = place()
    even = chip % 2 == 0
    south_ok, north_ok = (chip > 0, chip < lax.axis_size("row") // 2 - 1)
    copies = [
        pltpu.make_async_copy(m2_in.at[pl.ds(0, ntr), r], out.at[:, :, r - 2, :], sem.at[r - 4]) for r in range(4, rows - 4)
    ]
    for copy in copies:
        copy.start()

    def got(high, a, b):
        picked = jnp.where(even, a, b) if high else jnp.where(even, b, a)
        return jnp.where(north_ok if high else south_ok, picked, 0.0)

    for high, start in ((False, 0), (True, rows - 2)):
        for f in range(EXTRA):
            m0[ntr + f, start : start + 2] = got(high, *(x[pl.ds(2 * (ntr + f), 2)] for x in (rows_a, rows_b)))
        wet = wet_of(m0[nf - 1, start : start + 2])
        dv0[WET, start : start + 2] = wet
        for n in range(ntr):
            m0[n, start : start + 2] = got(high, *(x[pl.ds(2 * n, 2)] for x in (rows_a, rows_b))) * wet
        derive_rows(m0, dv0, ntr, span(start, start + 2))
    for start in (2, rows - 4):
        m0[:, start : start + 2] = m_own[:, start : start + 2]
        dv0[:, start : start + 2] = dv_own[:, start : start + 2]
    lane = lanes_of((nz, lon))
    low, high = (got(side, edge_a[...], rows_b[2 * nf]) for side in (False, True))
    at_low, at_high = (lane < WIN, (lane >= WIN * (lat_blk + 1)) & (lane < WIN * (lat_blk + 2)))
    fields = []
    for f in range(nf):
        cols = jnp.where(at_low, pltpu.roll(low, (-WIN * f) % lon, 1), z_in[f])
        fields.append(jnp.where(at_high, pltpu.roll(high, (WIN * (lat_blk + 1) - WIN * f) % lon, 1), cols))
    mask_columns(fields, z0, zd)
    column_step(z0, g0, zd, gd, z1, mix, ntr, lat_blk)
    now = (1, lat_blk, 2, 2)
    ocean_rows(m0, dv0, z0, zd, wts, m1, ntr, now)
    tracer_rows(m0, z0, wts, dv0, mix, moved, sat, m1, ntr, now)
    light_rows(m0, dv0, moved, m1, ntr, now)
    for start in (3, rows - 5):
        m1[:, start : start + 2] = m1_in[:, start : start + 2]
    for start in (1, rows - 3):
        dv1[WET, start : start + 2] = dv0[WET, start : start + 2]
    for start in (3, rows - 5):
        dv1[WET, start : start + 2] = dv_own[WET, start : start + 2]
    derive_rows(m1, dv1, ntr, (1, rows - 6, 2, 4))
    derive_columns(z1, zd, ntr)
    now = (2, rows - 6, 2, 2)
    ocean_rows(m1, dv1, z1, zd, wts, m0, ntr, now)
    tracer_rows(m1, z1, wts, dv1, mix, moved, sat, m0, ntr, now)
    light_rows(m0, dv1, moved, m0, ntr, now)

    rim[:, 0:2] = m0[:ntr, 2:4]
    rim[:, 2:4] = m0[:ntr, rows - 4 : rows - 2]
    m0[ntr : ntr + 3, 4 : rows - 4] = m2_in[ntr : ntr + 3, 4 : rows - 4]
    count = lat_blk // 2
    for f in range(3):
        keep[f] = m0[ntr + f, pl.ds(2 + half * count, count)]
        send[f] = m0[ntr + f, pl.ds(2 + (1 - half) * count, count)]
    for copy in copies:
        copy.wait()


def finish_kernel(keep, got, rim, out_in, flow_out, temp_out, out, flow, temp, sem):
    _, lat_dev, nz, lon = keep.shape
    lat_blk = 2 * lat_dev
    copies = [
        pltpu.make_async_copy(rim.at[:, i], out.at[:, :, t, :], sem.at[i])
        for i, t in enumerate((0, 1, lat_blk - 2, lat_blk - 1))
    ]
    for copy in copies:
        copy.start()
    first = place()[0] == 0
    for f in range(3):
        for t in range(lat_dev):
            a, b = (keep[f, t], got[f, t])
            low, high = (jnp.where(first, a, b), jnp.where(first, b, a))
            if f < 2:
                flow[f, :, t, :lon] = low
                flow[f, :, t, lon:] = high
            else:
                temp[:, t, :lon] = low
                temp[:, t, lon:] = high
        if f == 1:
            copies.append(pltpu.make_async_copy(flow, flow_out, sem.at[4]))
            copies[-1].start()
    copies.append(pltpu.make_async_copy(temp, temp_out, sem.at[5]))
    copies[-1].start()
    for copy in copies:
        copy.wait()


def call(kernel, outs, *args, scratch=(), far=(), away=(), aliases=None, cost=1):
    vmem, anywhere = (pl.BlockSpec(memory_space=pltpu.VMEM), pl.BlockSpec(memory_space=pl.ANY))
    return pl.pallas_call(
        kernel,
        out_shape=[jax.ShapeDtypeStruct(s, jnp.float32) if isinstance(s, tuple) else s for s in outs],
        in_specs=[anywhere if i in far else vmem for i in range(len(args))],
        out_specs=[anywhere if i in away else vmem for i in range(len(outs))],
        scratch_shapes=[pltpu.VMEM(s, jnp.float32) if isinstance(s, tuple) else s for s in scratch],
        input_output_aliases=aliases or {},
        compiler_params=pltpu.CompilerParams(vmem_limit_bytes=40 * 2**20),
        cost_estimate=pl.CostEstimate(
            flops=int(cost * 10**9), transcendentals=0, bytes_accessed=int(cost * 4 * 2**20)
        ),
    )(*args)


def both_ways(pairs):
    return sorted(pairs + [(b, a) for a, b in pairs])


def exchanges(n_row, n_col):
    chips = n_row // 2

    def dev(p, h, c):
        return (2 * p + h) * n_col + c

    partner = [(dev(p, 0, c), dev(p, 1, c)) for p in range(chips) for c in range(n_col)]
    outer = [(dev(p, 1, c), dev(p, 0, c + 1)) for p in range(chips) for c in range(n_col - 1)]
    for p in range(0, chips - 1, 2):
        outer += [(dev(p, 0, 0), dev(p + 1, 0, 0)), (dev(p, 1, n_col - 1), dev(p + 1, 1, n_col - 1))]
    lat_a = [(dev(p, h, c), dev(p + 1, h, c)) for p in range(0, chips - 1, 2) for h in (0, 1) for c in range(n_col)]
    lat_b = [(dev(p, h, c), dev(p + 1, h, c)) for p in range(1, chips - 1, 2) for h in (0, 1) for c in range(n_col)]
    ends = [0] if chips % 2 else [0, chips - 1]
    lat_b += [(dev(p, 0, c), dev(p, 1, c)) for p in ends for c in range(n_col)]
    return [both_ways(x) for x in (partner, outer, lat_a, lat_b)]


def on_device(n_row, n_col, flow, temp, tracers, bottom, sunlight, rates):
    nz, lat_dev, lon_dev = temp.shape
    _, ntr, _, lat_blk, lon = tracers.shape
    nf = ntr + EXTRA
    partner, outer, lat_a, lat_b = exchanges(n_row, n_col)

    def swap(x, pairs):
        return lax.ppermute(x, ("row", "col"), pairs)

    block = tracers[0]
    rows = lat_blk + 4
    cols, extra, some = ((nf, nz, lon), (EXTRA, nz, lon), (3, nz, lon))
    sent = (EXTRA * (lat_dev + 1), nz, lon)
    given = (flow, temp, bottom, sunlight, block)
    mine, to_partner, g_other, block = call(
        pack_ocean_kernel,
        [(EXTRA, lat_dev, nz, lon), sent, extra, block.shape],
        *[pltpu.with_memory_space_constraint(x, pltpu.HBM) for x in given],
        scratch=[
            flow.shape,
            temp.shape,
            pltpu.VMEM(bottom.shape, jnp.int32),
            sunlight.shape,
            pltpu.SemaphoreType.DMA((len(given),)),
        ],
        far=range(len(given)),
    )
    got = swap(to_partner, partner)
    turned, g_tracers = call(pack_tracers_kernel, [(ntr, lat_blk, nz, lon), (ntr, nz, lon)], block)
    rim = (2 * nf, nz, lon)
    ocean, g_own, to_outer, rows_a = call(
        join_kernel,
        [(EXTRA, lat_blk, nz, lon), cols, (nf // 4, nz, lon), rim],
        mine,
        got,
        to_partner,
        g_tracers,
        turned,
    )
    rows_a = swap(rows_a, lat_a)
    from_outer = swap(to_outer, outer)
    g_partner = swap(g_tracers, partner)
    full, derived = ((nf, rows, nz, lon), (3, rows, nz, lon))
    m0, dv, mix, g0, gd, inner = call(
        fill_kernel,
        [full, derived, jax.ShapeDtypeStruct((2 * ntr * nz, 2 * ntr * nz), jnp.bfloat16), cols, some, cols],
        turned,
        ocean,
        g_own,
        g_partner,
        got,
        g_other,
        rates,
    )
    z, edge_a, rows_b = call(
        edge_kernel, [cols, (nz, lon), (2 * nf + 1, nz, lon)], turned, ocean, inner, from_outer
    )
    rows_b, edge_a = (swap(rows_b, lat_b), swap(edge_a, lat_a))
    work = [(7, rows, nz, lon), pltpu.VMEM((rows, 2 * ntr * nz, lon), jnp.bfloat16)]
    work += [(ntr + 1, rows, nz, lon), cols, cols, some]
    m1, m2 = call(inner_kernel, [full, full], m0, dv, mix, g0, gd, z, scratch=[derived] + work, cost=20)
    third = (3, lat_dev, nz, lon)
    out, rim, keep, send = call(
        outer_kernel,
        [(ntr, nz, lat_blk, lon), (ntr, 4, nz, lon), third, third],
        m0,
        dv,
        mix,
        g0,
        gd,
        z,
        rows_a,
        rows_b,
        edge_a,
        m1,
        m2,
        scratch=[full, full, derived, derived] + work + [pltpu.SemaphoreType.DMA((lat_blk - 4,))],
        away=(0,),
    )
    flow_out, temp_out, out = call(
        finish_kernel,
        [flow.shape, temp.shape, out.shape],
        keep,
        swap(send, partner),
        rim,
        out,
        scratch=[flow.shape, temp.shape, pltpu.SemaphoreType.DMA((6,))],
        far=(3,),
        away=(0, 1, 2),
        aliases={3: 2},
    )
    return (flow_out, temp_out, out[None])


def solution(mesh):
    in_specs = (
        P(None, None, "row", "col"),
        P(None, "row", "col"),
        P("row", None, None, None, "col"),
        P("row", "col"),
        P("row", "col"),
        P(),
    )
    out_specs = (
        P(None, None, "row", "col"),
        P(None, "row", "col"),
        P("row", None, None, None, "col"),
    )
    return jax.shard_map(
        functools.partial(on_device, mesh.shape["row"], mesh.shape["col"]),
        mesh=mesh,
        in_specs=in_specs,
        out_specs=out_specs,
        check_vma=False,
    )
```

```python
import functools
import jax
import jax.numpy as jnp
from jax import lax
from jax.experimental import pallas as pl
from jax.experimental.pallas import tpu as pltpu
from jax.sharding import PartitionSpec as P

KL = 4
STEPS = 2

time_step = 0.2
viscosity = 0.2
expansion = 0.05
coriolis_base = 0.5
kappa_base = 0.05
kappa_shear = 0.2
react_step = 0.25
water_absorb = 0.1
pigment_absorb = 0.6
heat_gain = 1.0

EXTRA = 4
WIN = 4


def up(x):
    return pltpu.roll(x, 1, x.ndim - 2)


def down(x):
    return pltpu.roll(x, x.shape[-2] - 1, x.ndim - 2)


def lanes_of(shape):
    return lax.broadcasted_iota(jnp.int32, shape, len(shape) - 1)


def levels_of(shape):
    return lax.broadcasted_iota(jnp.int32, shape, len(shape) - 2)


def window(x, lat, into):
    lon = x.shape[1]
    lane = lanes_of(x.shape)
    base = WIN * (lat + 1)
    moved = pltpu.roll(x, (base + 2) % lon, 1)
    return jnp.where((lane >= base) & (lane < base + WIN), moved, into)


def place():
    row = lax.axis_index("row")
    return (row % 2, row // 2, lax.axis_index("col"))


def edge_starts(chip, lat_blk):
    odd = chip % 2
    return ((1 - odd) * (lat_blk - 2), odd * (lat_blk - 2))


def pack_ocean_kernel(flow_in, temp_in, bottom_in, sunlight_in, tracers_in, mine, to_partner, g_other, tracers, flow, temp, bottom, sunlight, sem):
    copies = [
        pltpu.make_async_copy(src, dst, sem.at[i])
        for i, (src, dst) in enumerate(
            ((flow_in, flow), (temp_in, temp), (bottom_in, bottom), (sunlight_in, sunlight), (tracers_in, tracers))
        )
    ]
    for copy in copies:
        copy.start()
    for copy in copies[:-1]:
        copy.wait()
    lat_dev, nz, lon = mine.shape[1:]
    lon_dev = temp.shape[2]
    half, _, _ = place()
    first = half == 0
    zero = jnp.zeros((nz, lon), jnp.float32)
    level = levels_of((nz, lon_dev))
    own = [zero] * EXTRA
    far = [zero] * EXTRA
    for t in range(lat_dev):
        depth = jnp.broadcast_to(bottom[t : t + 1, :], (nz, lon_dev))
        light = jnp.broadcast_to(sunlight[t : t + 1, :], (nz, lon_dev))
        wet = (level < depth).astype(jnp.float32)
        aux = jnp.where(level == 0, depth.astype(jnp.float32), jnp.where(level == 1, light, 0.0))
        for f, tile in enumerate((flow[0, :, t, :] * wet, flow[1, :, t, :] * wet, temp[:, t, :] * wet, aux)):
            low, high = (tile[:, :lon], tile[:, lon:])
            a, b = (jnp.where(first, low, high), jnp.where(first, high, low))
            mine[f, t] = a
            if f < EXTRA - 1:
                to_partner[f * lat_dev + t] = b
            own[f] = window(a, t, own[f])
            far[f] = window(b, t, far[f])
    flat = (EXTRA - 1) * lat_dev
    for i, both in enumerate((bottom[...].astype(jnp.float32), sunlight[...])):
        to_partner[flat + i, :lat_dev, :] = jnp.where(first, both[:, lon:], both[:, :lon])
    shift = half * (WIN * lat_dev)
    for f in range(EXTRA):
        to_partner[flat + 2 + f] = pltpu.roll(own[f], shift, 1)
        g_other[f] = pltpu.roll(far[f], shift, 1)
    copies[-1].wait()


def pack_tracers_kernel(tracers, turned, g_tracers):
    ntr, nz, lat_blk, lon = tracers.shape

    def some(i, _):
        g = [jnp.zeros((nz, lon), jnp.float32)] * PACK
        for t in range(lat_blk):
            for k in range(PACK):
                x = tracers[i * PACK + k, :, t, :]
                turned[i * PACK + k, t] = x
                g[k] = window(x, t, g[k])
        for k in range(PACK):
            g_tracers[i * PACK + k] = g[k]
        return 0

    lax.fori_loop(0, ntr // PACK, some, 0)


def in_half(shape, half, lat_dev):
    lane = lanes_of(shape)
    base = WIN * (lat_dev * half + 1)
    return (lane >= base) & (lane < base + WIN * lat_dev)


def edge_rows(turned, ocean, start, out):
    ntr = turned.shape[0]
    for n in range(ntr):
        out[2 * n : 2 * n + 2] = turned[n, pl.ds(start, 2)]
    for f in range(EXTRA):
        out[2 * (ntr + f) : 2 * (ntr + f) + 2] = ocean[f, pl.ds(start, 2)]


def join_kernel(mine, got, to_partner, g_tracers, turned, ocean, g_own, to_outer, rows_a):
    _, lat_dev, nz, lon = mine.shape
    ntr = g_tracers.shape[0]
    nf = ntr + EXTRA
    half, chip, _ = place()
    tile = (nz, lon)
    own_lanes = in_half(tile, half, lat_dev)
    shift = (1 - half) * (WIN * lat_dev)
    flat, level = ((EXTRA - 1) * lat_dev, levels_of(tile))
    g_own[:ntr] = g_tracers[...]
    for f in range(EXTRA):
        g = jnp.zeros(tile, jnp.float32)
        for t in range(lat_dev):
            if f < EXTRA - 1:
                x = got[f * lat_dev + t]
            else:
                depth, light = (jnp.broadcast_to(got[flat + i, t : t + 1, :], tile) for i in range(2))
                x = jnp.where(level == 0, depth, jnp.where(level == 1, light, 0.0))
            ocean[f, half * lat_dev + t] = mine[f, t]
            ocean[f, (1 - half) * lat_dev + t] = x
            g = window(x, t, g)
        g_own[ntr + f] = jnp.where(own_lanes, to_partner[flat + 2 + f], pltpu.roll(g, shift, 1))
    edge_rows(turned, ocean, edge_starts(chip, 2 * lat_dev)[0], rows_a)
    lane = lanes_of(tile)
    front, near = (lane % WIN < 2, in_half(tile, 0, 2 * lat_dev))
    side = (1 - half) * (lon - 2)
    for i in range(nf // 4):
        a, b, c, d = [pltpu.roll(g_own[4 * i + k], side, 1) for k in range(4)]
        low = jnp.where(front, a, pltpu.roll(b, 2, 1))
        high = jnp.where(front, c, pltpu.roll(d, 2, 1))
        to_outer[i] = jnp.where(near, low, pltpu.roll(high, lon // 2, 1))


def edge_kernel(turned, ocean, inner, from_outer, z, to_a, to_b):
    nf, nz, lon = z.shape
    lat_blk = turned.shape[1]

    half, chip, column = place()
    tile = (nz, lon)
    lane = lanes_of(tile)
    outer_ok = jnp.where(half == 0, column > 0, column < lax.axis_size("col") - 1)
    from_partner = (lane % WIN < 2).astype(jnp.int32) == half
    outer_lanes = in_half(tile, 0, lat_blk) & outer_ok
    start_a, start_b = edge_starts(chip, lat_blk)
    corner_a = corner_b = jnp.zeros(tile, jnp.float32)
    for f in range(nf):
        k = f % 4
        moved = pltpu.roll(from_outer[f // 4], lon + 2 * half - 2 * (k % 2) - lon // 2 * (k // 2), 1)
        cols = jnp.where(from_partner, inner[f], jnp.where(outer_lanes, moved, 0.0))
        z[f] = cols
        at = (lane >= WIN * f) & (lane < WIN * f + WIN)
        low = pltpu.roll(cols, (WIN * f - WIN) % lon, 1)
        high = pltpu.roll(cols, (WIN * f - WIN * lat_blk) % lon, 1)
        corner_a = jnp.where(at, jnp.where(start_a > 0, high, low), corner_a)
        corner_b = jnp.where(at, jnp.where(start_b > 0, high, low), corner_b)
    to_a[...] = corner_a
    edge_rows(turned, ocean, start_b, to_b)
    to_b[2 * nf] = corner_b


def kappa_of(u, v):
    du, dv = (u - down(u), v - down(v))
    sq = jnp.where(levels_of(u.shape) < u.shape[-2] - 1, du * du + dv * dv, 0.0)
    return kappa_base + kappa_shear * sq / (1.0 + sq)


def sum_above(x):
    level = levels_of(x.shape)
    k = 1
    while k < x.shape[-2]:
        x = x + jnp.where(level >= k, pltpu.roll(x, k, x.ndim - 2), 0.0)
        k *= 2
    return x


def sum_below(x):
    level, nz = (levels_of(x.shape), x.shape[-2])
    k = 1
    while k < nz:
        x = x + jnp.where(level < nz - k, pltpu.roll(x, nz - k, x.ndim - 2), 0.0)
        k *= 2
    return x


def pressure_of(heat):
    return -expansion * sum_above(heat)


def wet_of(aux):
    depth = jnp.broadcast_to(aux[..., 0:1, :], aux.shape)
    return (levels_of(aux.shape).astype(jnp.float32) < depth).astype(jnp.float32)


def light_of(aux):
    return jnp.broadcast_to(aux[..., 1:2, :], aux.shape)


def dynamics(u, v, wet, kap, prs, coriolis):
    um, ue, uw, un, us = u
    vm, ve, vw, vn, vs = v
    wm, we, ww, wn, ws = wet
    km, ke, kw, kn, ks = kap
    _, pe, pw, pn, ps = prs
    level, nz = (levels_of(um.shape), um.shape[-2])
    oe, ow, on, os_ = (wm * we, wm * ww, wm * wn, wm * ws)
    fe, fw, fn, fs = (0.5 * (um + ue) * oe, 0.5 * (um + uw) * ow, 0.5 * (vm + vn) * on, 0.5 * (vm + vs) * os_)
    ce, cw, cn, cs = (0.5 * (km + ke) * oe, 0.5 * (km + kw) * ow, 0.5 * (km + kn) * on, 0.5 * (km + ks) * os_)
    div = fe - fw + fn - fs
    total = sum_below(div)
    w_top = jnp.where(level >= 1, -total, 0.0)
    w_bot = jnp.where(level < nz - 1, -down(total), 0.0)
    weights = (
        wm * (1.0 - time_step * (ce + cw + cn + cs + 0.5 * (div + w_top - w_bot))),
        time_step * (ce - 0.5 * fe),
        time_step * (cw + 0.5 * fw),
        time_step * (cn - 0.5 * fn),
        time_step * (cs + 0.5 * fs),
        (-0.5 * time_step) * wm * w_top,
        (0.5 * time_step) * wm * w_bot,
    )
    lap_u = oe * (ue - um) + ow * (uw - um) + on * (un - um) + os_ * (us - um)
    lap_v = oe * (ve - vm) + ow * (vw - vm) + on * (vn - vm) + os_ * (vs - vm)
    new_u = wm * (um + time_step * (coriolis * vm - 0.5 * (pe - pw) + viscosity * lap_u))
    new_v = wm * (vm + time_step * (-coriolis * um - 0.5 * (pn - ps) + viscosity * lap_v))
    return (new_u, new_v, weights)


def transport(weights, x, east, west, north, south):
    a0, ae, aw, an, as_, at, ab = weights
    return (a0 * x + ae * east) + (aw * west + an * north) + (as_ * south + at * up(x)) + ab * down(x)


def saturated(x):
    return x * lax.rsqrt(1.0 + x * x)


def absorbed(pigment):
    level = levels_of(pigment.shape)
    sq = pigment * pigment
    depth = water_absorb + pigment_absorb * (sq / (1.0 + sq))
    above = jnp.where(level >= 1, up(depth), 0.0)
    k = 1
    while k < KL:
        above = above + jnp.where(level >= k, pltpu.roll(above, k, above.ndim - 2), 0.0)
        k *= 2
    return jnp.where(level < KL, jnp.exp(-above) * (1.0 - jnp.exp(-depth)), 0.0)


def two_parts(x):
    high = x.astype(jnp.bfloat16)
    return (high, (x - high.astype(jnp.float32)).astype(jnp.bfloat16))


def mix_matrix(rates, nz):
    ntr = rates.shape[0]
    size = ntr * nz
    exact = dict(precision=lax.Precision.HIGHEST, preferred_element_type=jnp.float32)
    spread = lax.broadcasted_iota(jnp.int32, (size, ntr), 0) // nz == lax.broadcasted_iota(jnp.int32, (size, ntr), 1)
    spread = spread.astype(jnp.float32)
    wide = jnp.dot(spread, rates, **exact)
    full = lax.dot_general(wide, spread, (((1,), (1,)), ((), ())), **exact)
    same = lax.broadcasted_iota(jnp.int32, (size, size), 0) % nz == lax.broadcasted_iota(jnp.int32, (size, size), 1) % nz
    high, low = two_parts(jnp.where(same, full, 0.0))
    top = jnp.concatenate([high, high], axis=1)
    return jnp.concatenate([top, jnp.concatenate([low, jnp.zeros_like(low)], axis=1)], axis=0)


def beside(z, r, lon):
    return pltpu.roll(z, lon - 2 - WIN * (r - 1), z.ndim - 1)


def sides(x, edge):
    lane, lon = (lanes_of(x.shape), x.shape[-1])
    west = pltpu.roll(jnp.where(lane == lon - 1, edge, x), 1, x.ndim - 1)
    east = pltpu.roll(jnp.where(lane == 0, edge, x), lon - 1, x.ndim - 1)
    return (east, west)


def around_rows(m, f, z, r, count):
    x = m[f, pl.ds(r, count)]
    edge = jnp.stack([beside(z, r + i, x.shape[-1]) for i in range(count)])
    return (x, *sides(x, edge), m[f, pl.ds(r + 1, count)], m[f, pl.ds(r - 1, count)])


def around_columns(x, own):
    lane, lon = (lanes_of(x.shape), x.shape[-1])
    west = pltpu.roll(jnp.where(lane % WIN == 0, x, own), 1, x.ndim - 1)
    east = pltpu.roll(jnp.where(lane % WIN == WIN - 1, x, own), lon - 1, x.ndim - 1)
    return (x, east, west, pltpu.roll(x, lon - WIN, x.ndim - 1), pltpu.roll(x, WIN, x.ndim - 1))


def coriolis_at(lat, lat_blk):
    _, chip, _ = place()
    latitude = (lat + chip * lat_blk).astype(jnp.float32)
    return coriolis_base * (2.0 * (latitude + 0.5) / (lax.axis_size("row") // 2 * lat_blk) - 1.0)


KAP, PRS, WET = (0, 1, 2)
GROUP = 4
PACK = 8
PIECE = 3


def span(start, stop):
    return (start, stop - start, 1, stop - start)


def chunks(rows, most, body):
    first, apart, times, size = rows
    count = max(k for k in range(1, min(most, size) + 1) if size % k == 0)
    if times > 1 or count == size:
        for i in range(times):
            body(first + i * apart, size)
    else:

        def one(i, _):
            body(first + i * count, count)
            return 0

        lax.fori_loop(0, size // count, one, 0)


def derive_rows(m, dv, ntr, rows):
    def body(r, count):
        at = pl.ds(r, count)
        dv[KAP, at] = kappa_of(m[ntr, at], m[ntr + 1, at])
        dv[PRS, at] = pressure_of(m[ntr + 2, at])

    chunks(rows, 10, body)


def derive_columns(z, zd, ntr):
    zd[KAP] = kappa_of(z[ntr], z[ntr + 1])
    zd[PRS] = pressure_of(z[ntr + 2])


def ocean_rows(m, dv, z, zd, wts, new, ntr, rows):
    def body(r, count):
        at = pl.ds(r, count)
        lat = lax.broadcasted_iota(jnp.int32, (count, *m.shape[2:]), 0) + (r - 2)
        new_u, new_v, weights = dynamics(
            around_rows(m, ntr, z[ntr], r, count),
            around_rows(m, ntr + 1, z[ntr + 1], r, count),
            around_rows(dv, WET, zd[WET], r, count),
            around_rows(dv, KAP, zd[KAP], r, count),
            around_rows(dv, PRS, zd[PRS], r, count),
            coriolis_at(lat, m.shape[1] - 4),
        )
        new[ntr, at] = new_u
        new[ntr + 1, at] = new_v
        for i, w in enumerate(weights):
            wts[i, at] = w

    chunks(rows, 9, body)


def tracer_rows(m, z, wts, dv, mix, moved, sat, new, ntr, rows):
    nz, lon = m.shape[2:]
    half = ntr * nz
    first, apart, times, count = rows
    if times == 1:
        count = max(k for k in range(1, PIECE + 1) if rows[3] % k == 0)
        apart, times = (count, rows[3] // count)

    def move(r):
        weights = [wts[i, r] for i in range(7)]
        for n in range(0, ntr, GROUP):
            x = m[n : n + GROUP, r]
            edge = beside(z[n : n + GROUP], r, lon)
            done = transport(weights, x, *sides(x, edge), m[n : n + GROUP, r + 1], m[n : n + GROUP, r - 1])
            moved[n : n + GROUP, r] = done
            high, low = two_parts(saturated(done).reshape(GROUP * nz, lon))
            sat[r, n * nz : (n + GROUP) * nz, :] = high
            sat[r, half + n * nz : half + (n + GROUP) * nz, :] = low
        h = ntr + 2
        x = m[h, r]
        moved[ntr, r] = transport(weights, x, *sides(x, beside(z[h], r, lon)), m[h, r + 1], m[h, r - 1])

    def react(r):
        both = jnp.concatenate([sat[r + i] for i in range(count)], axis=1)
        res = jnp.dot(mix[...], both, preferred_element_type=jnp.float32)
        res = res[:half] + res[half:]
        for i in range(count):
            gain = react_step * dv[WET, r + i]
            for n in range(ntr):
                new[n, r + i] = moved[n, r + i] + gain * res[n * nz : (n + 1) * nz, i * lon : (i + 1) * lon]

    def move_all(r):
        for i in range(count):
            move(r + i)

    def both_parts(i, _):
        react(first + (i - 1) * apart)
        move_all(first + i * apart)
        return 0

    move_all(first)
    if rows[2] > 1:
        for i in range(1, times):
            both_parts(i, 0)
    else:
        lax.fori_loop(1, times, both_parts, 0)
    react(first + (times - 1) * apart)


def light_rows(m, dv, moved, new, ntr, rows):
    def body(r, count):
        at = pl.ds(r, count)
        light = light_of(m[ntr + 3, at]) * dv[WET, at] * absorbed(new[0, at])
        new[ntr + 2, at] = moved[ntr, at] + heat_gain * light

    chunks(rows, 9, body)


def column_step(z0, g0, zd, gd, z1, mix, ntr, lat_blk):
    nz, lon = z0.shape[1:]
    half = ntr * nz
    wet = zd[WET]
    new_u, new_v, weights = dynamics(
        around_columns(z0[ntr], g0[ntr]),
        around_columns(z0[ntr + 1], g0[ntr + 1]),
        around_columns(wet, gd[WET]),
        around_columns(zd[KAP], gd[KAP]),
        around_columns(zd[PRS], gd[PRS]),
        coriolis_at(lanes_of((nz, lon)) // WIN - 1, lat_blk),
    )
    moved = transport(weights, *around_columns(z0[:ntr], g0[:ntr]))
    high, low = two_parts(saturated(moved).reshape(half, lon))
    res = jnp.dot(mix[...], jnp.concatenate([high, low], axis=0), preferred_element_type=jnp.float32)
    done = moved + (react_step * wet) * (res[:half] + res[half:]).reshape(ntr, nz, lon)
    z1[:ntr] = done
    z1[ntr] = new_u
    z1[ntr + 1] = new_v
    heat = transport(weights, *around_columns(z0[ntr + 2], g0[ntr + 2]))
    z1[ntr + 2] = heat + heat_gain * light_of(z0[ntr + 3]) * wet * absorbed(done[0])


def fill_kernel(turned, ocean, g_own, g_partner, got, g_other, rates, m0, dv, mix, g0, gd, inner):
    ntr, lat_blk, nz, lon = turned.shape
    half, _, _ = place()
    inner[:ntr] = g_partner[...]
    for f in range(EXTRA):
        theirs = got[(EXTRA - 1) * (lat_blk // 2) + 2 + f]
        inner[ntr + f] = jnp.where(in_half((nz, lon), half, lat_blk // 2), g_other[f], theirs)
    mix[...] = mix_matrix(rates[...], nz)
    own = span(2, lat_blk + 2)

    def wets(r, count):
        at = pl.ds(r, count)
        for f in range(EXTRA):
            m0[ntr + f, at] = ocean[f, pl.ds(r - 2, count)]
        dv[WET, at] = wet_of(ocean[EXTRA - 1, pl.ds(r - 2, count)])

    chunks(own, 8, wets)

    def some(r, count):
        wet = dv[WET, r]
        for n in range(ntr):
            m0[n, r] = turned[n, r - 2] * wet

    chunks(own, 1, some)
    derive_rows(m0, dv, ntr, own)
    mask_columns([g_own[f] for f in range(ntr + EXTRA)], g0, gd)


def mask_columns(fields, z, zd):
    ntr = len(fields) - EXTRA
    wet = wet_of(fields[-1])
    zd[WET] = wet
    for f, cols in enumerate(fields):
        z[f] = cols * wet if f < ntr else cols
    derive_columns(z, zd, ntr)


def inner_kernel(m0, dv, mix, g0, gd, z_in, m1, m2, dv1, wts, sat, moved, z0, z1, zd):
    nf, rows, _, _ = m0.shape
    ntr = nf - EXTRA
    mask_columns([z_in[f] for f in range(nf)], z0, zd)
    column_step(z0, g0, zd, gd, z1, mix, ntr, rows - 4)
    now = span(3, rows - 3)
    ocean_rows(m0, dv, z0, zd, wts, m1, ntr, now)
    tracer_rows(m0, z0, wts, dv, mix, moved, sat, m1, ntr, now)
    light_rows(m0, dv, moved, m1, ntr, now)
    dv1[WET, 3 : rows - 3] = dv[WET, 3 : rows - 3]
    derive_rows(m1, dv1, ntr, now)
    derive_columns(z1, zd, ntr)
    now = span(4, rows - 4)
    ocean_rows(m1, dv1, z1, zd, wts, m2, ntr, now)
    tracer_rows(m1, z1, wts, dv1, mix, moved, sat, m2, ntr, now)
    light_rows(m0, dv1, moved, m2, ntr, now)


def outer_kernel(m_own, dv_own, mix, g0, gd, z_in, rows_a, rows_b, edge_a, m1_in, m2_in, out, rim, keep, send, m0, m1, dv0, dv1, wts, sat, moved, z0, z1, zd, sem):
    nf, rows, nz, lon = m_own.shape
    ntr = nf - EXTRA
    lat_blk = rows - 4
    half, chip, _ = place()
    even = chip % 2 == 0
    south_ok, north_ok = (chip > 0, chip < lax.axis_size("row") // 2 - 1)
    copies = [
        pltpu.make_async_copy(m2_in.at[pl.ds(0, ntr), r], out.at[:, :, r - 2, :], sem.at[r - 4]) for r in range(4, rows - 4)
    ]
    for copy in copies:
        copy.start()

    def got(high, a, b):
        picked = jnp.where(even, a, b) if high else jnp.where(even, b, a)
        return jnp.where(north_ok if high else south_ok, picked, 0.0)

    for high, start in ((False, 0), (True, rows - 2)):
        for f in range(EXTRA):
            m0[ntr + f, start : start + 2] = got(high, *(x[pl.ds(2 * (ntr + f), 2)] for x in (rows_a, rows_b)))
        wet = wet_of(m0[nf - 1, start : start + 2])
        dv0[WET, start : start + 2] = wet
        for n in range(ntr):
            m0[n, start : start + 2] = got(high, *(x[pl.ds(2 * n, 2)] for x in (rows_a, rows_b))) * wet
        derive_rows(m0, dv0, ntr, span(start, start + 2))
    for start in (2, rows - 4):
        m0[:, start : start + 2] = m_own[:, start : start + 2]
        dv0[:, start : start + 2] = dv_own[:, start : start + 2]
    lane = lanes_of((nz, lon))
    low, high = (got(side, edge_a[...], rows_b[2 * nf]) for side in (False, True))
    at_low, at_high = (lane < WIN, (lane >= WIN * (lat_blk + 1)) & (lane < WIN * (lat_blk + 2)))
    fields = []
    for f in range(nf):
        cols = jnp.where(at_low, pltpu.roll(low, (-WIN * f) % lon, 1), z_in[f])
        fields.append(jnp.where(at_high, pltpu.roll(high, (WIN * (lat_blk + 1) - WIN * f) % lon, 1), cols))
    mask_columns(fields, z0, zd)
    column_step(z0, g0, zd, gd, z1, mix, ntr, lat_blk)
    now = (1, lat_blk, 2, 2)
    ocean_rows(m0, dv0, z0, zd, wts, m1, ntr, now)
    tracer_rows(m0, z0, wts, dv0, mix, moved, sat, m1, ntr, now)
    light_rows(m0, dv0, moved, m1, ntr, now)
    for start in (3, rows - 5):
        m1[:, start : start + 2] = m1_in[:, start : start + 2]
    for start in (1, rows - 3):
        dv1[WET, start : start + 2] = dv0[WET, start : start + 2]
    for start in (3, rows - 5):
        dv1[WET, start : start + 2] = dv_own[WET, start : start + 2]
    derive_rows(m1, dv1, ntr, (1, rows - 6, 2, 4))
    derive_columns(z1, zd, ntr)
    now = (2, rows - 6, 2, 2)
    ocean_rows(m1, dv1, z1, zd, wts, m0, ntr, now)
    tracer_rows(m1, z1, wts, dv1, mix, moved, sat, m0, ntr, now)
    light_rows(m0, dv1, moved, m0, ntr, now)

    rim[:, 0:2] = m0[:ntr, 2:4]
    rim[:, 2:4] = m0[:ntr, rows - 4 : rows - 2]
    m0[ntr : ntr + 3, 4 : rows - 4] = m2_in[ntr : ntr + 3, 4 : rows - 4]
    count = lat_blk // 2
    for f in range(3):
        keep[f] = m0[ntr + f, pl.ds(2 + half * count, count)]
        send[f] = m0[ntr + f, pl.ds(2 + (1 - half) * count, count)]
    for copy in copies:
        copy.wait()


def finish_kernel(keep, got, rim, out_in, flow_out, temp_out, out, flow, temp, sem):
    _, lat_dev, nz, lon = keep.shape
    lat_blk = 2 * lat_dev
    copies = [
        pltpu.make_async_copy(rim.at[:, i], out.at[:, :, t, :], sem.at[i])
        for i, t in enumerate((0, 1, lat_blk - 2, lat_blk - 1))
    ]
    for copy in copies:
        copy.start()
    first = place()[0] == 0
    for f in range(3):
        for t in range(lat_dev):
            a, b = (keep[f, t], got[f, t])
            low, high = (jnp.where(first, a, b), jnp.where(first, b, a))
            if f < 2:
                flow[f, :, t, :lon] = low
                flow[f, :, t, lon:] = high
            else:
                temp[:, t, :lon] = low
                temp[:, t, lon:] = high
        if f == 1:
            copies.append(pltpu.make_async_copy(flow, flow_out, sem.at[4]))
            copies[-1].start()
    copies.append(pltpu.make_async_copy(temp, temp_out, sem.at[5]))
    copies[-1].start()
    for copy in copies:
        copy.wait()


def call(kernel, outs, *args, scratch=(), far=(), away=(), aliases=None, cost=1):
    vmem, anywhere = (pl.BlockSpec(memory_space=pltpu.VMEM), pl.BlockSpec(memory_space=pl.ANY))
    return pl.pallas_call(
        kernel,
        out_shape=[jax.ShapeDtypeStruct(s, jnp.float32) if isinstance(s, tuple) else s for s in outs],
        in_specs=[anywhere if i in far else vmem for i in range(len(args))],
        out_specs=[anywhere if i in away else vmem for i in range(len(outs))],
        scratch_shapes=[pltpu.VMEM(s, jnp.float32) if isinstance(s, tuple) else s for s in scratch],
        input_output_aliases=aliases or {},
        compiler_params=pltpu.CompilerParams(vmem_limit_bytes=40 * 2**20),
        cost_estimate=pl.CostEstimate(
            flops=int(cost * 10**9), transcendentals=0, bytes_accessed=int(cost * 4 * 2**20)
        ),
    )(*args)


def both_ways(pairs):
    return sorted(pairs + [(b, a) for a, b in pairs])


def exchanges(n_row, n_col):
    chips = n_row // 2

    def dev(p, h, c):
        return (2 * p + h) * n_col + c

    partner = [(dev(p, 0, c), dev(p, 1, c)) for p in range(chips) for c in range(n_col)]
    outer = [(dev(p, 1, c), dev(p, 0, c + 1)) for p in range(chips) for c in range(n_col - 1)]
    for p in range(0, chips - 1, 2):
        outer += [(dev(p, 0, 0), dev(p + 1, 0, 0)), (dev(p, 1, n_col - 1), dev(p + 1, 1, n_col - 1))]
    lat_a = [(dev(p, h, c), dev(p + 1, h, c)) for p in range(0, chips - 1, 2) for h in (0, 1) for c in range(n_col)]
    lat_b = [(dev(p, h, c), dev(p + 1, h, c)) for p in range(1, chips - 1, 2) for h in (0, 1) for c in range(n_col)]
    ends = [0] if chips % 2 else [0, chips - 1]
    lat_b += [(dev(p, 0, c), dev(p, 1, c)) for p in ends for c in range(n_col)]
    return [both_ways(x) for x in (partner, outer, lat_a, lat_b)]


def on_device(n_row, n_col, flow, temp, tracers, bottom, sunlight, rates):
    nz, lat_dev, lon_dev = temp.shape
    _, ntr, _, lat_blk, lon = tracers.shape
    nf = ntr + EXTRA
    partner, outer, lat_a, lat_b = exchanges(n_row, n_col)

    def swap(x, pairs):
        return lax.ppermute(x, ("row", "col"), pairs)

    block = tracers[0]
    rows = lat_blk + 4
    cols, extra, some = ((nf, nz, lon), (EXTRA, nz, lon), (3, nz, lon))
    sent = ((EXTRA - 1) * lat_dev + 2 + EXTRA, nz, lon)
    given = (flow, temp, bottom, sunlight, block)
    mine, to_partner, g_other, block = call(
        pack_ocean_kernel,
        [(EXTRA, lat_dev, nz, lon), sent, extra, block.shape],
        *[pltpu.with_memory_space_constraint(x, pltpu.HBM) for x in given],
        scratch=[
            flow.shape,
            temp.shape,
            pltpu.VMEM(bottom.shape, jnp.int32),
            sunlight.shape,
            pltpu.SemaphoreType.DMA((len(given),)),
        ],
        far=range(len(given)),
    )
    got = swap(to_partner, partner)
    turned, g_tracers = call(pack_tracers_kernel, [(ntr, lat_blk, nz, lon), (ntr, nz, lon)], block)
    rim = (2 * nf, nz, lon)
    ocean, g_own, to_outer, rows_a = call(
        join_kernel,
        [(EXTRA, lat_blk, nz, lon), cols, (nf // 4, nz, lon), rim],
        mine,
        got,
        to_partner,
        g_tracers,
        turned,
    )
    rows_a = swap(rows_a, lat_a)
    from_outer = swap(to_outer, outer)
    g_partner = swap(g_tracers, partner)
    full, derived = ((nf, rows, nz, lon), (3, rows, nz, lon))
    m0, dv, mix, g0, gd, inner = call(
        fill_kernel,
        [full, derived, jax.ShapeDtypeStruct((2 * ntr * nz, 2 * ntr * nz), jnp.bfloat16), cols, some, cols],
        turned,
        ocean,
        g_own,
        g_partner,
        got,
        g_other,
        rates,
    )
    z, edge_a, rows_b = call(
        edge_kernel, [cols, (nz, lon), (2 * nf + 1, nz, lon)], turned, ocean, inner, from_outer
    )
    rows_b, edge_a = (swap(rows_b, lat_b), swap(edge_a, lat_a))
    work = [(7, rows, nz, lon), pltpu.VMEM((rows, 2 * ntr * nz, lon), jnp.bfloat16)]
    work += [(ntr + 1, rows, nz, lon), cols, cols, some]
    m1, m2 = call(inner_kernel, [full, full], m0, dv, mix, g0, gd, z, scratch=[derived] + work, cost=20)
    third = (3, lat_dev, nz, lon)
    out, rim, keep, send = call(
        outer_kernel,
        [(ntr, nz, lat_blk, lon), (ntr, 4, nz, lon), third, third],
        m0,
        dv,
        mix,
        g0,
        gd,
        z,
        rows_a,
        rows_b,
        edge_a,
        m1,
        m2,
        scratch=[full, full, derived, derived] + work + [pltpu.SemaphoreType.DMA((lat_blk - 4,))],
        away=(0,),
    )
    flow_out, temp_out, out = call(
        finish_kernel,
        [flow.shape, temp.shape, out.shape],
        keep,
        swap(send, partner),
        rim,
        out,
        scratch=[flow.shape, temp.shape, pltpu.SemaphoreType.DMA((6,))],
        far=(3,),
        away=(0, 1, 2),
        aliases={3: 2},
    )
    return (flow_out, temp_out, out[None])


def solution(mesh):
    in_specs = (
        P(None, None, "row", "col"),
        P(None, "row", "col"),
        P("row", None, None, None, "col"),
        P("row", "col"),
        P("row", "col"),
        P(),
    )
    out_specs = (
        P(None, None, "row", "col"),
        P(None, "row", "col"),
        P("row", None, None, None, "col"),
    )
    return jax.shard_map(
        functools.partial(on_device, mesh.shape["row"], mesh.shape["col"]),
        mesh=mesh,
        in_specs=in_specs,
        out_specs=out_specs,
        check_vma=False,
    )
```

```python
import functools
import jax
import jax.numpy as jnp
from jax import lax
from jax.experimental import pallas as pl
from jax.experimental.pallas import tpu as pltpu
from jax.sharding import PartitionSpec as P

KL = 4
STEPS = 2

time_step = 0.2
viscosity = 0.2
expansion = 0.05
coriolis_base = 0.5
kappa_base = 0.05
kappa_shear = 0.2
react_step = 0.25
water_absorb = 0.1
pigment_absorb = 0.6
heat_gain = 1.0

EXTRA = 4
WIN = 4


def up(x):
    return pltpu.roll(x, 1, x.ndim - 2)


def down(x):
    return pltpu.roll(x, x.shape[-2] - 1, x.ndim - 2)


def lanes_of(shape):
    return lax.broadcasted_iota(jnp.int32, shape, len(shape) - 1)


def levels_of(shape):
    return lax.broadcasted_iota(jnp.int32, shape, len(shape) - 2)


def window(x, lat, into):
    lon = x.shape[1]
    lane = lanes_of(x.shape)
    base = WIN * (lat + 1)
    moved = pltpu.roll(x, (base + 2) % lon, 1)
    return jnp.where((lane >= base) & (lane < base + WIN), moved, into)


def place():
    row = lax.axis_index("row")
    return (row % 2, row // 2, lax.axis_index("col"))


def edge_starts(chip, lat_blk):
    odd = chip % 2
    return ((1 - odd) * (lat_blk - 2), odd * (lat_blk - 2))


def pack_ocean_kernel(flow_in, temp_in, bottom_in, sunlight_in, tracers_in, mine, to_partner, g_other, tracers, flow, temp, bottom, sunlight, sem):
    copies = [
        pltpu.make_async_copy(src, dst, sem.at[i])
        for i, (src, dst) in enumerate(
            ((flow_in, flow), (temp_in, temp), (bottom_in, bottom), (sunlight_in, sunlight), (tracers_in, tracers))
        )
    ]
    for copy in copies:
        copy.start()
    for copy in copies[:-1]:
        copy.wait()
    lat_dev, nz, lon = mine.shape[1:]
    lon_dev = temp.shape[2]
    half, _, _ = place()
    first = half == 0
    zero = jnp.zeros((nz, lon), jnp.float32)
    level = levels_of((nz, lon_dev))
    own = [zero] * EXTRA
    far = [zero] * EXTRA
    for t in range(lat_dev):
        depth = jnp.broadcast_to(bottom[t : t + 1, :], (nz, lon_dev))
        light = jnp.broadcast_to(sunlight[t : t + 1, :], (nz, lon_dev))
        wet = (level < depth).astype(jnp.float32)
        aux = jnp.where(level == 0, depth.astype(jnp.float32), jnp.where(level == 1, light, 0.0))
        for f, tile in enumerate((flow[0, :, t, :] * wet, flow[1, :, t, :] * wet, temp[:, t, :] * wet, aux)):
            low, high = (tile[:, :lon], tile[:, lon:])
            a, b = (jnp.where(first, low, high), jnp.where(first, high, low))
            mine[f, t] = a
            if f < EXTRA - 1:
                to_partner[f * lat_dev + t] = b
            own[f] = window(a, t, own[f])
            far[f] = window(b, t, far[f])
    flat = (EXTRA - 1) * lat_dev
    for i, both in enumerate((bottom[...].astype(jnp.float32), sunlight[...])):
        to_partner[flat + i, :lat_dev, :] = jnp.where(first, both[:, lon:], both[:, :lon])
    shift = half * (WIN * lat_dev)
    for f in range(EXTRA):
        to_partner[flat + 2 + f] = pltpu.roll(own[f], shift, 1)
        g_other[f] = pltpu.roll(far[f], shift, 1)
    copies[-1].wait()


def pack_tracers_kernel(tracers, turned, g_tracers):
    ntr, nz, lat_blk, lon = tracers.shape

    def some(i, _):
        g = [jnp.zeros((nz, lon), jnp.float32)] * PACK
        for t in range(lat_blk):
            for k in range(PACK):
                x = tracers[i * PACK + k, :, t, :]
                turned[i * PACK + k, t] = x
                g[k] = window(x, t, g[k])
        for k in range(PACK):
            g_tracers[i * PACK + k] = g[k]
        return 0

    lax.fori_loop(0, ntr // PACK, some, 0)


def in_half(shape, half, lat_dev):
    lane = lanes_of(shape)
    base = WIN * (lat_dev * half + 1)
    return (lane >= base) & (lane < base + WIN * lat_dev)


def edge_rows(turned, ocean, start, out):
    ntr = turned.shape[0]
    for n in range(ntr):
        out[2 * n : 2 * n + 2] = turned[n, pl.ds(start, 2)]
    for f in range(EXTRA):
        out[2 * (ntr + f) : 2 * (ntr + f) + 2] = ocean[f, pl.ds(start, 2)]


def join_kernel(mine, got, to_partner, g_tracers, turned, ocean, g_own, to_outer, rows_a):
    _, lat_dev, nz, lon = mine.shape
    ntr = g_tracers.shape[0]
    nf = ntr + EXTRA
    half, chip, _ = place()
    tile = (nz, lon)
    own_lanes = in_half(tile, half, lat_dev)
    shift = (1 - half) * (WIN * lat_dev)
    flat, level = ((EXTRA - 1) * lat_dev, levels_of(tile))
    g_own[:ntr] = g_tracers[...]
    for f in range(EXTRA):
        g = jnp.zeros(tile, jnp.float32)
        for t in range(lat_dev):
            if f < EXTRA - 1:
                x = got[f * lat_dev + t]
            else:
                depth, light = (jnp.broadcast_to(got[flat + i, t : t + 1, :], tile) for i in range(2))
                x = jnp.where(level == 0, depth, jnp.where(level == 1, light, 0.0))
            ocean[f, half * lat_dev + t] = mine[f, t]
            ocean[f, (1 - half) * lat_dev + t] = x
            g = window(x, t, g)
        g_own[ntr + f] = jnp.where(own_lanes, to_partner[flat + 2 + f], pltpu.roll(g, shift, 1))
    edge_rows(turned, ocean, edge_starts(chip, 2 * lat_dev)[0], rows_a)
    lane = lanes_of(tile)
    front, near = (lane % WIN < 2, in_half(tile, 0, 2 * lat_dev))
    side = (1 - half) * (lon - 2)
    for i in range(nf // 4):
        a, b, c, d = [pltpu.roll(g_own[4 * i + k], side, 1) for k in range(4)]
        low = jnp.where(front, a, pltpu.roll(b, 2, 1))
        high = jnp.where(front, c, pltpu.roll(d, 2, 1))
        to_outer[i] = jnp.where(near, low, pltpu.roll(high, lon // 2, 1))


def edge_kernel(turned, ocean, inner, from_outer, z, to_a, to_b):
    nf, nz, lon = z.shape
    lat_blk = turned.shape[1]

    half, chip, column = place()
    tile = (nz, lon)
    lane = lanes_of(tile)
    outer_ok = jnp.where(half == 0, column > 0, column < lax.axis_size("col") - 1)
    from_partner = (lane % WIN < 2).astype(jnp.int32) == half
    outer_lanes = in_half(tile, 0, lat_blk) & outer_ok
    start_a, start_b = edge_starts(chip, lat_blk)
    corner_a = corner_b = jnp.zeros(tile, jnp.float32)
    for f in range(nf):
        k = f % 4
        moved = pltpu.roll(from_outer[f // 4], lon + 2 * half - 2 * (k % 2) - lon // 2 * (k // 2), 1)
        cols = jnp.where(from_partner, inner[f], jnp.where(outer_lanes, moved, 0.0))
        z[f] = cols
        at = (lane >= WIN * f) & (lane < WIN * f + WIN)
        low = pltpu.roll(cols, (WIN * f - WIN) % lon, 1)
        high = pltpu.roll(cols, (WIN * f - WIN * lat_blk) % lon, 1)
        corner_a = jnp.where(at, jnp.where(start_a > 0, high, low), corner_a)
        corner_b = jnp.where(at, jnp.where(start_b > 0, high, low), corner_b)
    to_a[...] = corner_a
    edge_rows(turned, ocean, start_b, to_b)
    to_b[2 * nf] = corner_b


def kappa_of(u, v):
    du, dv = (u - down(u), v - down(v))
    sq = jnp.where(levels_of(u.shape) < u.shape[-2] - 1, du * du + dv * dv, 0.0)
    return kappa_base + kappa_shear * sq / (1.0 + sq)


def sum_above(x):
    level = levels_of(x.shape)
    k = 1
    while k < x.shape[-2]:
        x = x + jnp.where(level >= k, pltpu.roll(x, k, x.ndim - 2), 0.0)
        k *= 2
    return x


def sum_below(x):
    level, nz = (levels_of(x.shape), x.shape[-2])
    k = 1
    while k < nz:
        x = x + jnp.where(level < nz - k, pltpu.roll(x, nz - k, x.ndim - 2), 0.0)
        k *= 2
    return x


def pressure_of(heat):
    return -expansion * sum_above(heat)


def wet_of(aux):
    depth = jnp.broadcast_to(aux[..., 0:1, :], aux.shape)
    return (levels_of(aux.shape).astype(jnp.float32) < depth).astype(jnp.float32)


def light_of(aux):
    return jnp.broadcast_to(aux[..., 1:2, :], aux.shape)


def dynamics(u, v, wet, kap, prs, coriolis):
    um, ue, uw, un, us = u
    vm, ve, vw, vn, vs = v
    wm, we, ww, wn, ws = wet
    km, ke, kw, kn, ks = kap
    _, pe, pw, pn, ps = prs
    level, nz = (levels_of(um.shape), um.shape[-2])
    oe, ow, on, os_ = (wm * we, wm * ww, wm * wn, wm * ws)
    fe, fw, fn, fs = (0.5 * (um + ue) * oe, 0.5 * (um + uw) * ow, 0.5 * (vm + vn) * on, 0.5 * (vm + vs) * os_)
    ce, cw, cn, cs = (0.5 * (km + ke) * oe, 0.5 * (km + kw) * ow, 0.5 * (km + kn) * on, 0.5 * (km + ks) * os_)
    div = fe - fw + fn - fs
    total = sum_below(div)
    w_top = jnp.where(level >= 1, -total, 0.0)
    w_bot = jnp.where(level < nz - 1, -down(total), 0.0)
    weights = (
        wm * (1.0 - time_step * (ce + cw + cn + cs + 0.5 * (div + w_top - w_bot))),
        time_step * (ce - 0.5 * fe),
        time_step * (cw + 0.5 * fw),
        time_step * (cn - 0.5 * fn),
        time_step * (cs + 0.5 * fs),
        (-0.5 * time_step) * wm * w_top,
        (0.5 * time_step) * wm * w_bot,
    )
    lap_u = oe * (ue - um) + ow * (uw - um) + on * (un - um) + os_ * (us - um)
    lap_v = oe * (ve - vm) + ow * (vw - vm) + on * (vn - vm) + os_ * (vs - vm)
    new_u = wm * (um + time_step * (coriolis * vm - 0.5 * (pe - pw) + viscosity * lap_u))
    new_v = wm * (vm + time_step * (-coriolis * um - 0.5 * (pn - ps) + viscosity * lap_v))
    return (new_u, new_v, weights)


def transport(weights, x, east, west, north, south):
    a0, ae, aw, an, as_, at, ab = weights
    return (a0 * x + ae * east) + (aw * west + an * north) + (as_ * south + at * up(x)) + ab * down(x)


def saturated(x):
    return x * lax.rsqrt(1.0 + x * x)


def absorbed(pigment):
    level = levels_of(pigment.shape)
    sq = pigment * pigment
    depth = water_absorb + pigment_absorb * (sq / (1.0 + sq))
    above = jnp.where(level >= 1, up(depth), 0.0)
    k = 1
    while k < KL:
        above = above + jnp.where(level >= k, pltpu.roll(above, k, above.ndim - 2), 0.0)
        k *= 2
    return jnp.where(level < KL, jnp.exp(-above) * (1.0 - jnp.exp(-depth)), 0.0)


def two_parts(x):
    high = x.astype(jnp.bfloat16)
    return (high, (x - high.astype(jnp.float32)).astype(jnp.bfloat16))


def mix_matrix(rates, nz):
    ntr = rates.shape[0]
    size = ntr * nz
    exact = dict(precision=lax.Precision.HIGHEST, preferred_element_type=jnp.float32)
    spread = lax.broadcasted_iota(jnp.int32, (size, ntr), 0) // nz == lax.broadcasted_iota(jnp.int32, (size, ntr), 1)
    spread = spread.astype(jnp.float32)
    wide = jnp.dot(spread, rates, **exact)
    full = lax.dot_general(wide, spread, (((1,), (1,)), ((), ())), **exact)
    same = lax.broadcasted_iota(jnp.int32, (size, size), 0) % nz == lax.broadcasted_iota(jnp.int32, (size, size), 1) % nz
    high, low = two_parts(jnp.where(same, full, 0.0))
    top = jnp.concatenate([high, high], axis=1)
    return jnp.concatenate([top, jnp.concatenate([low, jnp.zeros_like(low)], axis=1)], axis=0)


def beside(z, r, lon):
    return pltpu.roll(z, lon - 2 - WIN * (r - 1), z.ndim - 1)


def sides(x, edge):
    lane, lon = (lanes_of(x.shape), x.shape[-1])
    west = pltpu.roll(jnp.where(lane == lon - 1, edge, x), 1, x.ndim - 1)
    east = pltpu.roll(jnp.where(lane == 0, edge, x), lon - 1, x.ndim - 1)
    return (east, west)


def around_rows(m, f, z, r, count):
    x = m[f, pl.ds(r, count)]
    edge = jnp.stack([beside(z, r + i, x.shape[-1]) for i in range(count)])
    return (x, *sides(x, edge), m[f, pl.ds(r + 1, count)], m[f, pl.ds(r - 1, count)])


def around_columns(x, own):
    lane, lon = (lanes_of(x.shape), x.shape[-1])
    west = pltpu.roll(jnp.where(lane % WIN == 0, x, own), 1, x.ndim - 1)
    east = pltpu.roll(jnp.where(lane % WIN == WIN - 1, x, own), lon - 1, x.ndim - 1)
    return (x, east, west, pltpu.roll(x, lon - WIN, x.ndim - 1), pltpu.roll(x, WIN, x.ndim - 1))


def coriolis_at(lat, lat_blk):
    _, chip, _ = place()
    latitude = (lat + chip * lat_blk).astype(jnp.float32)
    return coriolis_base * (2.0 * (latitude + 0.5) / (lax.axis_size("row") // 2 * lat_blk) - 1.0)


KAP, PRS, WET = (0, 1, 2)
GROUP = 4
PACK = 8
PIECE = 3


def span(start, stop):
    return (start, stop - start, 1, stop - start)


def chunks(rows, most, body):
    first, apart, times, size = rows
    count = max(k for k in range(1, min(most, size) + 1) if size % k == 0)
    if times > 1 or count == size:
        for i in range(times):
            body(first + i * apart, size)
    else:

        def one(i, _):
            body(first + i * count, count)
            return 0

        lax.fori_loop(0, size // count, one, 0)


def derive_rows(m, dv, ntr, rows):
    def body(r, count):
        at = pl.ds(r, count)
        dv[KAP, at] = kappa_of(m[ntr, at], m[ntr + 1, at])
        dv[PRS, at] = pressure_of(m[ntr + 2, at])

    chunks(rows, 10, body)


def derive_columns(z, zd, ntr):
    zd[KAP] = kappa_of(z[ntr], z[ntr + 1])
    zd[PRS] = pressure_of(z[ntr + 2])


def ocean_rows(m, dv, z, zd, wts, new, ntr, rows):
    def body(r, count):
        at = pl.ds(r, count)
        lat = lax.broadcasted_iota(jnp.int32, (count, *m.shape[2:]), 0) + (r - 2)
        new_u, new_v, weights = dynamics(
            around_rows(m, ntr, z[ntr], r, count),
            around_rows(m, ntr + 1, z[ntr + 1], r, count),
            around_rows(dv, WET, zd[WET], r, count),
            around_rows(dv, KAP, zd[KAP], r, count),
            around_rows(dv, PRS, zd[PRS], r, count),
            coriolis_at(lat, m.shape[1] - 4),
        )
        new[ntr, at] = new_u
        new[ntr + 1, at] = new_v
        for i, w in enumerate(weights):
            wts[i, at] = w

    chunks(rows, 9, body)


def tracer_rows(m, z, wts, dv, mix, moved, sat, new, ntr, rows):
    nz, lon = m.shape[2:]
    half = ntr * nz
    first, apart, times, count = rows
    if times == 1:
        count = max(k for k in range(1, PIECE + 1) if rows[3] % k == 0)
        apart, times = (count, rows[3] // count)

    def move(r):
        weights = [wts[i, r] for i in range(7)]
        for n in range(0, ntr, GROUP):
            x = m[n : n + GROUP, r]
            edge = beside(z[n : n + GROUP], r, lon)
            done = transport(weights, x, *sides(x, edge), m[n : n + GROUP, r + 1], m[n : n + GROUP, r - 1])
            moved[n : n + GROUP, r] = done
            high, low = two_parts(saturated(done).reshape(GROUP * nz, lon))
            sat[r, n * nz : (n + GROUP) * nz, :] = high
            sat[r, half + n * nz : half + (n + GROUP) * nz, :] = low
        h = ntr + 2
        x = m[h, r]
        moved[ntr, r] = transport(weights, x, *sides(x, beside(z[h], r, lon)), m[h, r + 1], m[h, r - 1])

    def react(every):
        both = jnp.concatenate([sat[r] for r in every], axis=1)
        res = jnp.dot(mix[...], both, preferred_element_type=jnp.float32)
        res = res[:half] + res[half:]
        for i, r in enumerate(every):
            gain = react_step * dv[WET, r]
            for n in range(ntr):
                new[n, r] = moved[n, r] + gain * res[n * nz : (n + 1) * nz, i * lon : (i + 1) * lon]

    def piece(i):
        return [first + i * apart + k for k in range(count)]

    def both_parts(i, _):
        react(piece(i - 1))
        for r in piece(i):
            move(r)
        return 0

    if rows[2] > 1:
        every = [r for i in range(times) for r in piece(i)]
        for r in every:
            move(r)
        react(every)
    else:
        for r in piece(0):
            move(r)
        lax.fori_loop(1, times, both_parts, 0)
        react(piece(times - 1))


def light_rows(m, dv, moved, new, ntr, rows):
    def body(r, count):
        at = pl.ds(r, count)
        light = light_of(m[ntr + 3, at]) * dv[WET, at] * absorbed(new[0, at])
        new[ntr + 2, at] = moved[ntr, at] + heat_gain * light

    chunks(rows, 9, body)


def column_step(z0, g0, zd, gd, z1, mix, ntr, lat_blk):
    nz, lon = z0.shape[1:]
    half = ntr * nz
    wet = zd[WET]
    new_u, new_v, weights = dynamics(
        around_columns(z0[ntr], g0[ntr]),
        around_columns(z0[ntr + 1], g0[ntr + 1]),
        around_columns(wet, gd[WET]),
        around_columns(zd[KAP], gd[KAP]),
        around_columns(zd[PRS], gd[PRS]),
        coriolis_at(lanes_of((nz, lon)) // WIN - 1, lat_blk),
    )
    moved = transport(weights, *around_columns(z0[:ntr], g0[:ntr]))
    high, low = two_parts(saturated(moved).reshape(half, lon))
    res = jnp.dot(mix[...], jnp.concatenate([high, low], axis=0), preferred_element_type=jnp.float32)
    done = moved + (react_step * wet) * (res[:half] + res[half:]).reshape(ntr, nz, lon)
    z1[:ntr] = done
    z1[ntr] = new_u
    z1[ntr + 1] = new_v
    heat = transport(weights, *around_columns(z0[ntr + 2], g0[ntr + 2]))
    z1[ntr + 2] = heat + heat_gain * light_of(z0[ntr + 3]) * wet * absorbed(done[0])


def fill_kernel(turned, ocean, g_own, g_partner, got, g_other, rates, m0, dv, mix, g0, gd, inner):
    ntr, lat_blk, nz, lon = turned.shape
    half, _, _ = place()
    inner[:ntr] = g_partner[...]
    for f in range(EXTRA):
        theirs = got[(EXTRA - 1) * (lat_blk // 2) + 2 + f]
        inner[ntr + f] = jnp.where(in_half((nz, lon), half, lat_blk // 2), g_other[f], theirs)
    mix[...] = mix_matrix(rates[...], nz)
    own = span(2, lat_blk + 2)

    def wets(r, count):
        at = pl.ds(r, count)
        for f in range(EXTRA):
            m0[ntr + f, at] = ocean[f, pl.ds(r - 2, count)]
        dv[WET, at] = wet_of(ocean[EXTRA - 1, pl.ds(r - 2, count)])

    chunks(own, 8, wets)

    def some(r, count):
        wet = dv[WET, r]
        for n in range(ntr):
            m0[n, r] = turned[n, r - 2] * wet

    chunks(own, 1, some)
    derive_rows(m0, dv, ntr, own)
    mask_columns([g_own[f] for f in range(ntr + EXTRA)], g0, gd)


def mask_columns(fields, z, zd):
    ntr = len(fields) - EXTRA
    wet = wet_of(fields[-1])
    zd[WET] = wet
    for f, cols in enumerate(fields):
        z[f] = cols * wet if f < ntr else cols
    derive_columns(z, zd, ntr)


def inner_kernel(m0, dv, mix, g0, gd, z_in, m1, m2, dv1, wts, sat, moved, z0, z1, zd):
    nf, rows, _, _ = m0.shape
    ntr = nf - EXTRA
    mask_columns([z_in[f] for f in range(nf)], z0, zd)
    column_step(z0, g0, zd, gd, z1, mix, ntr, rows - 4)
    now = span(3, rows - 3)
    ocean_rows(m0, dv, z0, zd, wts, m1, ntr, now)
    tracer_rows(m0, z0, wts, dv, mix, moved, sat, m1, ntr, now)
    light_rows(m0, dv, moved, m1, ntr, now)
    dv1[WET, 3 : rows - 3] = dv[WET, 3 : rows - 3]
    derive_rows(m1, dv1, ntr, now)
    derive_columns(z1, zd, ntr)
    now = span(4, rows - 4)
    ocean_rows(m1, dv1, z1, zd, wts, m2, ntr, now)
    tracer_rows(m1, z1, wts, dv1, mix, moved, sat, m2, ntr, now)
    light_rows(m0, dv1, moved, m2, ntr, now)


def outer_kernel(m_own, dv_own, mix, g0, gd, z_in, rows_a, rows_b, edge_a, m1_in, m2_in, out, rim, keep, send, m0, m1, dv0, dv1, wts, sat, moved, z0, z1, zd, sem):
    nf, rows, nz, lon = m_own.shape
    ntr = nf - EXTRA
    lat_blk = rows - 4
    half, chip, _ = place()
    even = chip % 2 == 0
    south_ok, north_ok = (chip > 0, chip < lax.axis_size("row") // 2 - 1)
    copies = [
        pltpu.make_async_copy(m2_in.at[pl.ds(0, ntr), r], out.at[:, :, r - 2, :], sem.at[r - 4]) for r in range(4, rows - 4)
    ]
    for copy in copies:
        copy.start()

    def got(high, a, b):
        picked = jnp.where(even, a, b) if high else jnp.where(even, b, a)
        return jnp.where(north_ok if high else south_ok, picked, 0.0)

    for high, start in ((False, 0), (True, rows - 2)):
        for f in range(EXTRA):
            m0[ntr + f, start : start + 2] = got(high, *(x[pl.ds(2 * (ntr + f), 2)] for x in (rows_a, rows_b)))
        wet = wet_of(m0[nf - 1, start : start + 2])
        dv0[WET, start : start + 2] = wet
        for n in range(ntr):
            m0[n, start : start + 2] = got(high, *(x[pl.ds(2 * n, 2)] for x in (rows_a, rows_b))) * wet
        derive_rows(m0, dv0, ntr, span(start, start + 2))
    for start in (2, rows - 4):
        m0[:, start : start + 2] = m_own[:, start : start + 2]
        dv0[:, start : start + 2] = dv_own[:, start : start + 2]
    lane = lanes_of((nz, lon))
    low, high = (got(side, edge_a[...], rows_b[2 * nf]) for side in (False, True))
    at_low, at_high = (lane < WIN, (lane >= WIN * (lat_blk + 1)) & (lane < WIN * (lat_blk + 2)))
    fields = []
    for f in range(nf):
        cols = jnp.where(at_low, pltpu.roll(low, (-WIN * f) % lon, 1), z_in[f])
        fields.append(jnp.where(at_high, pltpu.roll(high, (WIN * (lat_blk + 1) - WIN * f) % lon, 1), cols))
    mask_columns(fields, z0, zd)
    column_step(z0, g0, zd, gd, z1, mix, ntr, lat_blk)
    now = (1, lat_blk, 2, 2)
    ocean_rows(m0, dv0, z0, zd, wts, m1, ntr, now)
    tracer_rows(m0, z0, wts, dv0, mix, moved, sat, m1, ntr, now)
    light_rows(m0, dv0, moved, m1, ntr, now)
    for start in (3, rows - 5):
        m1[:, start : start + 2] = m1_in[:, start : start + 2]
    for start in (1, rows - 3):
        dv1[WET, start : start + 2] = dv0[WET, start : start + 2]
    for start in (3, rows - 5):
        dv1[WET, start : start + 2] = dv_own[WET, start : start + 2]
    derive_rows(m1, dv1, ntr, (1, rows - 6, 2, 4))
    derive_columns(z1, zd, ntr)
    now = (2, rows - 6, 2, 2)
    ocean_rows(m1, dv1, z1, zd, wts, m0, ntr, now)
    tracer_rows(m1, z1, wts, dv1, mix, moved, sat, m0, ntr, now)
    light_rows(m0, dv1, moved, m0, ntr, now)

    rim[:, 0:2] = m0[:ntr, 2:4]
    rim[:, 2:4] = m0[:ntr, rows - 4 : rows - 2]
    m0[ntr : ntr + 3, 4 : rows - 4] = m2_in[ntr : ntr + 3, 4 : rows - 4]
    count = lat_blk // 2
    for f in range(3):
        keep[f] = m0[ntr + f, pl.ds(2 + half * count, count)]
        send[f] = m0[ntr + f, pl.ds(2 + (1 - half) * count, count)]
    for copy in copies:
        copy.wait()


def half_copies(part, core, buffer, flow_out, temp_out, sem):
    _, lat_dev, _, lon = part.shape
    for f in range(3):
        for t in range(lat_dev):
            buffer[f, :, t, :] = part[f, t]
    at = pl.ds(pl.multiple_of(core * lon, lon), lon)
    return [
        pltpu.make_async_copy(buffer.at[pl.ds(0, 2)], flow_out.at[:, :, :, at], sem.at[0]),
        pltpu.make_async_copy(buffer.at[2], temp_out.at[:, :, at], sem.at[1]),
    ]


def finish_own_kernel(keep, rim, out_in, flow_out, temp_out, out, buffer, sem):
    lat_blk = 2 * keep.shape[1]
    copies = [
        pltpu.make_async_copy(rim.at[:, i], out.at[:, :, t, :], sem.at[2 + i])
        for i, t in enumerate((0, 1, lat_blk - 2, lat_blk - 1))
    ]
    for copy in copies:
        copy.start()
    more = half_copies(keep, place()[0], buffer, flow_out, temp_out, sem)
    for copy in more:
        copy.start()
    for copy in copies + more:
        copy.wait()


def finish_other_kernel(got, flow_in, temp_in, flow_out, temp_out, buffer, sem):
    copies = half_copies(got, 1 - place()[0], buffer, flow_out, temp_out, sem)
    for copy in copies:
        copy.start()
    for copy in copies:
        copy.wait()


def call(kernel, outs, *args, scratch=(), far=(), away=(), aliases=None, cost=1):
    vmem, anywhere = (pl.BlockSpec(memory_space=pltpu.VMEM), pl.BlockSpec(memory_space=pl.ANY))
    return pl.pallas_call(
        kernel,
        out_shape=[jax.ShapeDtypeStruct(s, jnp.float32) if isinstance(s, tuple) else s for s in outs],
        in_specs=[anywhere if i in far else vmem for i in range(len(args))],
        out_specs=[anywhere if i in away else vmem for i in range(len(outs))],
        scratch_shapes=[pltpu.VMEM(s, jnp.float32) if isinstance(s, tuple) else s for s in scratch],
        input_output_aliases=aliases or {},
        compiler_params=pltpu.CompilerParams(vmem_limit_bytes=40 * 2**20),
        cost_estimate=pl.CostEstimate(
            flops=int(cost * 10**9), transcendentals=0, bytes_accessed=int(cost * 4 * 2**20)
        ),
    )(*args)


def both_ways(pairs):
    return sorted(pairs + [(b, a) for a, b in pairs])


def exchanges(n_row, n_col):
    chips = n_row // 2

    def dev(p, h, c):
        return (2 * p + h) * n_col + c

    partner = [(dev(p, 0, c), dev(p, 1, c)) for p in range(chips) for c in range(n_col)]
    outer = [(dev(p, 1, c), dev(p, 0, c + 1)) for p in range(chips) for c in range(n_col - 1)]
    for p in range(0, chips - 1, 2):
        outer += [(dev(p, 0, 0), dev(p + 1, 0, 0)), (dev(p, 1, n_col - 1), dev(p + 1, 1, n_col - 1))]
    lat_a = [(dev(p, h, c), dev(p + 1, h, c)) for p in range(0, chips - 1, 2) for h in (0, 1) for c in range(n_col)]
    lat_b = [(dev(p, h, c), dev(p + 1, h, c)) for p in range(1, chips - 1, 2) for h in (0, 1) for c in range(n_col)]
    ends = [0] if chips % 2 else [0, chips - 1]
    lat_b += [(dev(p, 0, c), dev(p, 1, c)) for p in ends for c in range(n_col)]
    return [both_ways(x) for x in (partner, outer, lat_a, lat_b)]


def on_device(n_row, n_col, flow, temp, tracers, bottom, sunlight, rates):
    nz, lat_dev, lon_dev = temp.shape
    _, ntr, _, lat_blk, lon = tracers.shape
    nf = ntr + EXTRA
    partner, outer, lat_a, lat_b = exchanges(n_row, n_col)

    def swap(x, pairs):
        return lax.ppermute(x, ("row", "col"), pairs)

    block = tracers[0]
    rows = lat_blk + 4
    cols, extra, some = ((nf, nz, lon), (EXTRA, nz, lon), (3, nz, lon))
    sent = ((EXTRA - 1) * lat_dev + 2 + EXTRA, nz, lon)
    given = (flow, temp, bottom, sunlight, block)
    mine, to_partner, g_other, block = call(
        pack_ocean_kernel,
        [(EXTRA, lat_dev, nz, lon), sent, extra, block.shape],
        *[pltpu.with_memory_space_constraint(x, pltpu.HBM) for x in given],
        scratch=[
            flow.shape,
            temp.shape,
            pltpu.VMEM(bottom.shape, jnp.int32),
            sunlight.shape,
            pltpu.SemaphoreType.DMA((len(given),)),
        ],
        far=range(len(given)),
    )
    got = swap(to_partner, partner)
    turned, g_tracers = call(pack_tracers_kernel, [(ntr, lat_blk, nz, lon), (ntr, nz, lon)], block)
    rim = (2 * nf, nz, lon)
    ocean, g_own, to_outer, rows_a = call(
        join_kernel,
        [(EXTRA, lat_blk, nz, lon), cols, (nf // 4, nz, lon), rim],
        mine,
        got,
        to_partner,
        g_tracers,
        turned,
    )
    rows_a = swap(rows_a, lat_a)
    from_outer = swap(to_outer, outer)
    g_partner = swap(g_tracers, partner)
    full, derived = ((nf, rows, nz, lon), (3, rows, nz, lon))
    m0, dv, mix, g0, gd, inner = call(
        fill_kernel,
        [full, derived, jax.ShapeDtypeStruct((2 * ntr * nz, 2 * ntr * nz), jnp.bfloat16), cols, some, cols],
        turned,
        ocean,
        g_own,
        g_partner,
        got,
        g_other,
        rates,
    )
    z, edge_a, rows_b = call(
        edge_kernel, [cols, (nz, lon), (2 * nf + 1, nz, lon)], turned, ocean, inner, from_outer
    )
    rows_b, edge_a = (swap(rows_b, lat_b), swap(edge_a, lat_a))
    work = [(7, rows, nz, lon), pltpu.VMEM((rows, 2 * ntr * nz, lon), jnp.bfloat16)]
    work += [(ntr + 1, rows, nz, lon), cols, cols, some]
    m1, m2 = call(inner_kernel, [full, full], m0, dv, mix, g0, gd, z, scratch=[derived] + work, cost=20)
    third = (3, lat_dev, nz, lon)
    out, rim, keep, send = call(
        outer_kernel,
        [(ntr, nz, lat_blk, lon), (ntr, 4, nz, lon), third, third],
        m0,
        dv,
        mix,
        g0,
        gd,
        z,
        rows_a,
        rows_b,
        edge_a,
        m1,
        m2,
        scratch=[full, full, derived, derived] + work + [pltpu.SemaphoreType.DMA((lat_blk - 4,))],
        away=(0,),
    )
    returned = swap(send, partner)
    buffer = (3, nz, lat_dev, lon)
    flow_out, temp_out, out = call(
        finish_own_kernel,
        [flow.shape, temp.shape, out.shape],
        keep,
        rim,
        out,
        scratch=[buffer, pltpu.SemaphoreType.DMA((6,))],
        far=(2,),
        away=(0, 1, 2),
        aliases={2: 2},
    )
    flow_out, temp_out = call(
        finish_other_kernel,
        [flow.shape, temp.shape],
        returned,
        flow_out,
        temp_out,
        scratch=[buffer, pltpu.SemaphoreType.DMA((2,))],
        far=(1, 2),
        away=(0, 1),
        aliases={1: 0, 2: 1},
    )
    return (flow_out, temp_out, out[None])


def solution(mesh):
    in_specs = (
        P(None, None, "row", "col"),
        P(None, "row", "col"),
        P("row", None, None, None, "col"),
        P("row", "col"),
        P("row", "col"),
        P(),
    )
    out_specs = (
        P(None, None, "row", "col"),
        P(None, "row", "col"),
        P("row", None, None, None, "col"),
    )
    return jax.shard_map(
        functools.partial(on_device, mesh.shape["row"], mesh.shape["col"]),
        mesh=mesh,
        in_specs=in_specs,
        out_specs=out_specs,
        check_vma=False,
    )
```

```python
import functools
import jax
import jax.numpy as jnp
from jax import lax
from jax.experimental import pallas as pl
from jax.experimental.pallas import tpu as pltpu
from jax.sharding import PartitionSpec as P

KL = 4
STEPS = 2

time_step = 0.2
viscosity = 0.2
expansion = 0.05
coriolis_base = 0.5
kappa_base = 0.05
kappa_shear = 0.2
react_step = 0.25
water_absorb = 0.1
pigment_absorb = 0.6
heat_gain = 1.0

EXTRA = 4
WIN = 4


def up(x):
    return pltpu.roll(x, 1, x.ndim - 2)


def down(x):
    return pltpu.roll(x, x.shape[-2] - 1, x.ndim - 2)


def lanes_of(shape):
    return lax.broadcasted_iota(jnp.int32, shape, len(shape) - 1)


def levels_of(shape):
    return lax.broadcasted_iota(jnp.int32, shape, len(shape) - 2)


def window(x, lat, into):
    lon = x.shape[1]
    lane = lanes_of(x.shape)
    base = WIN * (lat + 1)
    moved = pltpu.roll(x, (base + 2) % lon, 1)
    return jnp.where((lane >= base) & (lane < base + WIN), moved, into)


def place():
    row = lax.axis_index("row")
    return (row % 2, row // 2, lax.axis_index("col"))


def edge_starts(chip, lat_blk):
    odd = chip % 2
    return ((1 - odd) * (lat_blk - 2), odd * (lat_blk - 2))


def pack_ocean_kernel(flow_in, temp_in, bottom_in, sunlight_in, tracers_in, mine, to_partner, g_other, tracers, flow, temp, bottom, sunlight, sem):
    copies = [
        pltpu.make_async_copy(src, dst, sem.at[i])
        for i, (src, dst) in enumerate(
            ((flow_in, flow), (temp_in, temp), (bottom_in, bottom), (sunlight_in, sunlight), (tracers_in, tracers))
        )
    ]
    for copy in copies:
        copy.start()
    for copy in copies[:-1]:
        copy.wait()
    lat_dev, nz, lon = mine.shape[1:]
    lon_dev = temp.shape[2]
    half, _, _ = place()
    first = half == 0
    zero = jnp.zeros((nz, lon), jnp.float32)
    level = levels_of((nz, lon_dev))
    own = [zero] * EXTRA
    far = [zero] * EXTRA
    for t in range(lat_dev):
        depth = jnp.broadcast_to(bottom[t : t + 1, :], (nz, lon_dev))
        light = jnp.broadcast_to(sunlight[t : t + 1, :], (nz, lon_dev))
        wet = (level < depth).astype(jnp.float32)
        aux = jnp.where(level == 0, depth.astype(jnp.float32), jnp.where(level == 1, light, 0.0))
        for f, tile in enumerate((flow[0, :, t, :] * wet, flow[1, :, t, :] * wet, temp[:, t, :] * wet, aux)):
            low, high = (tile[:, :lon], tile[:, lon:])
            a, b = (jnp.where(first, low, high), jnp.where(first, high, low))
            mine[f, t] = a
            if f < EXTRA - 1:
                to_partner[f * lat_dev + t] = b
            own[f] = window(a, t, own[f])
            far[f] = window(b, t, far[f])
    flat = (EXTRA - 1) * lat_dev
    for i, both in enumerate((bottom[...].astype(jnp.float32), sunlight[...])):
        to_partner[flat + i, :lat_dev, :] = jnp.where(first, both[:, lon:], both[:, :lon])
    shift = half * (WIN * lat_dev)
    for f in range(EXTRA):
        to_partner[flat + 2 + f] = pltpu.roll(own[f], shift, 1)
        g_other[f] = pltpu.roll(far[f], shift, 1)
    copies[-1].wait()


def pack_tracers_kernel(tracers, turned, g_tracers):
    ntr, nz, lat_blk, lon = tracers.shape

    def some(i, _):
        g = [jnp.zeros((nz, lon), jnp.float32)] * PACK
        for t in range(lat_blk):
            for k in range(PACK):
                x = tracers[i * PACK + k, :, t, :]
                turned[i * PACK + k, t] = x
                g[k] = window(x, t, g[k])
        for k in range(PACK):
            g_tracers[i * PACK + k] = g[k]
        return 0

    lax.fori_loop(0, ntr // PACK, some, 0)


def in_half(shape, half, lat_dev):
    lane = lanes_of(shape)
    base = WIN * (lat_dev * half + 1)
    return (lane >= base) & (lane < base + WIN * lat_dev)


def edge_rows(turned, ocean, start, out):
    ntr = turned.shape[0]
    for n in range(ntr):
        out[2 * n : 2 * n + 2] = turned[n, pl.ds(start, 2)]
    for f in range(EXTRA):
        out[2 * (ntr + f) : 2 * (ntr + f) + 2] = ocean[f, pl.ds(start, 2)]


def join_kernel(mine, got, to_partner, g_tracers, turned, ocean, g_own, to_outer, rows_a):
    _, lat_dev, nz, lon = mine.shape
    ntr = g_tracers.shape[0]
    nf = ntr + EXTRA
    half, chip, _ = place()
    tile = (nz, lon)
    own_lanes = in_half(tile, half, lat_dev)
    shift = (1 - half) * (WIN * lat_dev)
    flat, level = ((EXTRA - 1) * lat_dev, levels_of(tile))
    g_own[:ntr] = g_tracers[...]
    for f in range(EXTRA):
        g = jnp.zeros(tile, jnp.float32)
        for t in range(lat_dev):
            if f < EXTRA - 1:
                x = got[f * lat_dev + t]
            else:
                depth, light = (jnp.broadcast_to(got[flat + i, t : t + 1, :], tile) for i in range(2))
                x = jnp.where(level == 0, depth, jnp.where(level == 1, light, 0.0))
            ocean[f, half * lat_dev + t] = mine[f, t]
            ocean[f, (1 - half) * lat_dev + t] = x
            g = window(x, t, g)
        g_own[ntr + f] = jnp.where(own_lanes, to_partner[flat + 2 + f], pltpu.roll(g, shift, 1))
    edge_rows(turned, ocean, edge_starts(chip, 2 * lat_dev)[0], rows_a)
    lane = lanes_of(tile)
    front, near = (lane % WIN < 2, in_half(tile, 0, 2 * lat_dev))
    side = (1 - half) * (lon - 2)
    for i in range(nf // 4):
        a, b, c, d = [pltpu.roll(g_own[4 * i + k], side, 1) for k in range(4)]
        low = jnp.where(front, a, pltpu.roll(b, 2, 1))
        high = jnp.where(front, c, pltpu.roll(d, 2, 1))
        to_outer[i] = jnp.where(near, low, pltpu.roll(high, lon // 2, 1))


def edge_kernel(turned, ocean, inner, from_outer, z, to_a, to_b):
    nf, nz, lon = z.shape
    lat_blk = turned.shape[1]

    half, chip, column = place()
    tile = (nz, lon)
    lane = lanes_of(tile)
    outer_ok = jnp.where(half == 0, column > 0, column < lax.axis_size("col") - 1)
    from_partner = (lane % WIN < 2).astype(jnp.int32) == half
    outer_lanes = in_half(tile, 0, lat_blk) & outer_ok
    start_a, start_b = edge_starts(chip, lat_blk)
    corner_a = corner_b = jnp.zeros(tile, jnp.float32)
    for f in range(nf):
        k = f % 4
        moved = pltpu.roll(from_outer[f // 4], lon + 2 * half - 2 * (k % 2) - lon // 2 * (k // 2), 1)
        cols = jnp.where(from_partner, inner[f], jnp.where(outer_lanes, moved, 0.0))
        z[f] = cols
        at = (lane >= WIN * f) & (lane < WIN * f + WIN)
        low = pltpu.roll(cols, (WIN * f - WIN) % lon, 1)
        high = pltpu.roll(cols, (WIN * f - WIN * lat_blk) % lon, 1)
        corner_a = jnp.where(at, jnp.where(start_a > 0, high, low), corner_a)
        corner_b = jnp.where(at, jnp.where(start_b > 0, high, low), corner_b)
    to_a[...] = corner_a
    edge_rows(turned, ocean, start_b, to_b)
    to_b[2 * nf] = corner_b


def kappa_of(u, v):
    du, dv = (u - down(u), v - down(v))
    sq = jnp.where(levels_of(u.shape) < u.shape[-2] - 1, du * du + dv * dv, 0.0)
    return kappa_base + kappa_shear * sq / (1.0 + sq)


def sum_above(x):
    level = levels_of(x.shape)
    k = 1
    while k < x.shape[-2]:
        x = x + jnp.where(level >= k, pltpu.roll(x, k, x.ndim - 2), 0.0)
        k *= 2
    return x


def sum_below(x):
    level, nz = (levels_of(x.shape), x.shape[-2])
    k = 1
    while k < nz:
        x = x + jnp.where(level < nz - k, pltpu.roll(x, nz - k, x.ndim - 2), 0.0)
        k *= 2
    return x


def pressure_of(heat):
    return -expansion * sum_above(heat)


def wet_of(aux):
    depth = jnp.broadcast_to(aux[..., 0:1, :], aux.shape)
    return (levels_of(aux.shape).astype(jnp.float32) < depth).astype(jnp.float32)


def light_of(aux):
    return jnp.broadcast_to(aux[..., 1:2, :], aux.shape)


def dynamics(u, v, wet, kap, prs, coriolis):
    um, ue, uw, un, us = u
    vm, ve, vw, vn, vs = v
    wm, we, ww, wn, ws = wet
    km, ke, kw, kn, ks = kap
    _, pe, pw, pn, ps = prs
    level, nz = (levels_of(um.shape), um.shape[-2])
    oe, ow, on, os_ = (wm * we, wm * ww, wm * wn, wm * ws)
    fe, fw, fn, fs = (0.5 * (um + ue) * oe, 0.5 * (um + uw) * ow, 0.5 * (vm + vn) * on, 0.5 * (vm + vs) * os_)
    ce, cw, cn, cs = (0.5 * (km + ke) * oe, 0.5 * (km + kw) * ow, 0.5 * (km + kn) * on, 0.5 * (km + ks) * os_)
    div = fe - fw + fn - fs
    total = sum_below(div)
    w_top = jnp.where(level >= 1, -total, 0.0)
    w_bot = jnp.where(level < nz - 1, -down(total), 0.0)
    weights = (
        wm * (1.0 - time_step * (ce + cw + cn + cs + 0.5 * (div + w_top - w_bot))),
        time_step * (ce - 0.5 * fe),
        time_step * (cw + 0.5 * fw),
        time_step * (cn - 0.5 * fn),
        time_step * (cs + 0.5 * fs),
        (-0.5 * time_step) * wm * w_top,
        (0.5 * time_step) * wm * w_bot,
    )
    lap_u = oe * (ue - um) + ow * (uw - um) + on * (un - um) + os_ * (us - um)
    lap_v = oe * (ve - vm) + ow * (vw - vm) + on * (vn - vm) + os_ * (vs - vm)
    new_u = wm * (um + time_step * (coriolis * vm - 0.5 * (pe - pw) + viscosity * lap_u))
    new_v = wm * (vm + time_step * (-coriolis * um - 0.5 * (pn - ps) + viscosity * lap_v))
    return (new_u, new_v, weights)


def transport(weights, x, east, west, north, south):
    a0, ae, aw, an, as_, at, ab = weights
    return (a0 * x + ae * east) + (aw * west + an * north) + (as_ * south + at * up(x)) + ab * down(x)


def saturated(x):
    return x * lax.rsqrt(1.0 + x * x)


def absorbed(pigment):
    level = levels_of(pigment.shape)
    sq = pigment * pigment
    depth = water_absorb + pigment_absorb * (sq / (1.0 + sq))
    above = jnp.where(level >= 1, up(depth), 0.0)
    k = 1
    while k < KL:
        above = above + jnp.where(level >= k, pltpu.roll(above, k, above.ndim - 2), 0.0)
        k *= 2
    return jnp.where(level < KL, jnp.exp(-above) * (1.0 - jnp.exp(-depth)), 0.0)


def two_parts(x):
    high = x.astype(jnp.bfloat16)
    return (high, (x - high.astype(jnp.float32)).astype(jnp.bfloat16))


def mix_matrix(rates, nz):
    ntr = rates.shape[0]
    size = ntr * nz
    exact = dict(precision=lax.Precision.HIGHEST, preferred_element_type=jnp.float32)
    spread = lax.broadcasted_iota(jnp.int32, (size, ntr), 0) // nz == lax.broadcasted_iota(jnp.int32, (size, ntr), 1)
    spread = spread.astype(jnp.float32)
    wide = jnp.dot(spread, rates, **exact)
    full = lax.dot_general(wide, spread, (((1,), (1,)), ((), ())), **exact)
    same = lax.broadcasted_iota(jnp.int32, (size, size), 0) % nz == lax.broadcasted_iota(jnp.int32, (size, size), 1) % nz
    high, low = two_parts(jnp.where(same, full, 0.0))
    top = jnp.concatenate([high, high], axis=1)
    return jnp.concatenate([top, jnp.concatenate([low, jnp.zeros_like(low)], axis=1)], axis=0)


def beside(z, r, lon):
    return pltpu.roll(z, lon - 2 - WIN * (r - 1), z.ndim - 1)


def sides(x, edge):
    lane, lon = (lanes_of(x.shape), x.shape[-1])
    west = pltpu.roll(jnp.where(lane == lon - 1, edge, x), 1, x.ndim - 1)
    east = pltpu.roll(jnp.where(lane == 0, edge, x), lon - 1, x.ndim - 1)
    return (east, west)


def around_rows(m, f, z, r, count):
    x = m[f, pl.ds(r, count)]
    edge = jnp.stack([beside(z, r + i, x.shape[-1]) for i in range(count)])
    return (x, *sides(x, edge), m[f, pl.ds(r + 1, count)], m[f, pl.ds(r - 1, count)])


def around_columns(x, own):
    lane, lon = (lanes_of(x.shape), x.shape[-1])
    west = pltpu.roll(jnp.where(lane % WIN == 0, x, own), 1, x.ndim - 1)
    east = pltpu.roll(jnp.where(lane % WIN == WIN - 1, x, own), lon - 1, x.ndim - 1)
    return (x, east, west, pltpu.roll(x, lon - WIN, x.ndim - 1), pltpu.roll(x, WIN, x.ndim - 1))


def coriolis_at(lat, lat_blk):
    _, chip, _ = place()
    latitude = (lat + chip * lat_blk).astype(jnp.float32)
    return coriolis_base * (2.0 * (latitude + 0.5) / (lax.axis_size("row") // 2 * lat_blk) - 1.0)


KAP, PRS, WET = (0, 1, 2)
GROUP = 8
PACK = 8
PIECE = 3


def span(start, stop):
    return (start, stop - start, 1, stop - start)


def chunks(rows, most, body):
    first, apart, times, size = rows
    count = max(k for k in range(1, min(most, size) + 1) if size % k == 0)
    if times > 1 or count == size:
        for i in range(times):
            body(first + i * apart, size)
    else:

        def one(i, _):
            body(first + i * count, count)
            return 0

        lax.fori_loop(0, size // count, one, 0)


def derive_rows(m, dv, ntr, rows):
    def body(r, count):
        at = pl.ds(r, count)
        dv[KAP, at] = kappa_of(m[ntr, at], m[ntr + 1, at])
        dv[PRS, at] = pressure_of(m[ntr + 2, at])

    chunks(rows, 10, body)


def derive_columns(z, zd, ntr):
    zd[KAP] = kappa_of(z[ntr], z[ntr + 1])
    zd[PRS] = pressure_of(z[ntr + 2])


def ocean_rows(m, dv, z, zd, wts, new, ntr, rows):
    def body(r, count):
        at = pl.ds(r, count)
        lat = lax.broadcasted_iota(jnp.int32, (count, *m.shape[2:]), 0) + (r - 2)
        new_u, new_v, weights = dynamics(
            around_rows(m, ntr, z[ntr], r, count),
            around_rows(m, ntr + 1, z[ntr + 1], r, count),
            around_rows(dv, WET, zd[WET], r, count),
            around_rows(dv, KAP, zd[KAP], r, count),
            around_rows(dv, PRS, zd[PRS], r, count),
            coriolis_at(lat, m.shape[1] - 4),
        )
        new[ntr, at] = new_u
        new[ntr + 1, at] = new_v
        for i, w in enumerate(weights):
            wts[i, at] = w

    chunks(rows, 9, body)


def tracer_rows(m, z, wts, dv, mix, moved, sat, new, ntr, rows):
    nz, lon = m.shape[2:]
    half = ntr * nz
    first, apart, times, count = rows
    if times == 1:
        count = max(k for k in range(1, PIECE + 1) if rows[3] % k == 0)
        apart, times = (count, rows[3] // count)

    def move(r):
        weights = [wts[i, r] for i in range(7)]
        for n in range(0, ntr, GROUP):
            x = m[n : n + GROUP, r]
            edge = beside(z[n : n + GROUP], r, lon)
            done = transport(weights, x, *sides(x, edge), m[n : n + GROUP, r + 1], m[n : n + GROUP, r - 1])
            moved[n : n + GROUP, r] = done
            high, low = two_parts(saturated(done).reshape(GROUP * nz, lon))
            sat[r, n * nz : (n + GROUP) * nz, :] = high
            sat[r, half + n * nz : half + (n + GROUP) * nz, :] = low
        h = ntr + 2
        x = m[h, r]
        moved[ntr, r] = transport(weights, x, *sides(x, beside(z[h], r, lon)), m[h, r + 1], m[h, r - 1])

    def react(every):
        both = jnp.concatenate([sat[r] for r in every], axis=1)
        res = jnp.dot(mix[...], both, preferred_element_type=jnp.float32)
        res = res[:half] + res[half:]
        for i, r in enumerate(every):
            gain = react_step * dv[WET, r]
            for n in range(ntr):
                new[n, r] = moved[n, r] + gain * res[n * nz : (n + 1) * nz, i * lon : (i + 1) * lon]

    def piece(i):
        return [first + i * apart + k for k in range(count)]

    def both_parts(i, _):
        react(piece(i - 1))
        for r in piece(i):
            move(r)
        return 0

    if rows[2] > 1:
        every = [r for i in range(times) for r in piece(i)]
        for r in every:
            move(r)
        react(every)
    else:
        for r in piece(0):
            move(r)
        lax.fori_loop(1, times, both_parts, 0)
        react(piece(times - 1))


def light_rows(m, dv, moved, new, ntr, rows):
    def body(r, count):
        at = pl.ds(r, count)
        light = light_of(m[ntr + 3, at]) * dv[WET, at] * absorbed(new[0, at])
        new[ntr + 2, at] = moved[ntr, at] + heat_gain * light

    chunks(rows, 9, body)


def column_step(z0, g0, zd, gd, z1, mix, ntr, lat_blk):
    nz, lon = z0.shape[1:]
    half = ntr * nz
    wet = zd[WET]
    new_u, new_v, weights = dynamics(
        around_columns(z0[ntr], g0[ntr]),
        around_columns(z0[ntr + 1], g0[ntr + 1]),
        around_columns(wet, gd[WET]),
        around_columns(zd[KAP], gd[KAP]),
        around_columns(zd[PRS], gd[PRS]),
        coriolis_at(lanes_of((nz, lon)) // WIN - 1, lat_blk),
    )
    moved = transport(weights, *around_columns(z0[:ntr], g0[:ntr]))
    high, low = two_parts(saturated(moved).reshape(half, lon))
    res = jnp.dot(mix[...], jnp.concatenate([high, low], axis=0), preferred_element_type=jnp.float32)
    done = moved + (react_step * wet) * (res[:half] + res[half:]).reshape(ntr, nz, lon)
    z1[:ntr] = done
    z1[ntr] = new_u
    z1[ntr + 1] = new_v
    heat = transport(weights, *around_columns(z0[ntr + 2], g0[ntr + 2]))
    z1[ntr + 2] = heat + heat_gain * light_of(z0[ntr + 3]) * wet * absorbed(done[0])


def fill_kernel(turned, ocean, g_own, g_partner, got, g_other, rates, m0, dv, mix, g0, gd, inner):
    ntr, lat_blk, nz, lon = turned.shape
    half, _, _ = place()
    inner[:ntr] = g_partner[...]
    for f in range(EXTRA):
        theirs = got[(EXTRA - 1) * (lat_blk // 2) + 2 + f]
        inner[ntr + f] = jnp.where(in_half((nz, lon), half, lat_blk // 2), g_other[f], theirs)
    mix[...] = mix_matrix(rates[...], nz)
    own = span(2, lat_blk + 2)

    def wets(r, count):
        at = pl.ds(r, count)
        for f in range(EXTRA):
            m0[ntr + f, at] = ocean[f, pl.ds(r - 2, count)]
        dv[WET, at] = wet_of(ocean[EXTRA - 1, pl.ds(r - 2, count)])

    chunks(own, 8, wets)

    def some(r, count):
        wet = dv[WET, r]
        for n in range(ntr):
            m0[n, r] = turned[n, r - 2] * wet

    chunks(own, 1, some)
    derive_rows(m0, dv, ntr, own)
    mask_columns([g_own[f] for f in range(ntr + EXTRA)], g0, gd)


def mask_columns(fields, z, zd):
    ntr = len(fields) - EXTRA
    wet = wet_of(fields[-1])
    zd[WET] = wet
    for f, cols in enumerate(fields):
        z[f] = cols * wet if f < ntr else cols
    derive_columns(z, zd, ntr)


def inner_kernel(m0, dv, mix, g0, gd, z_in, m1, m2, dv1, wts, sat, moved, z0, z1, zd):
    nf, rows, _, _ = m0.shape
    ntr = nf - EXTRA
    mask_columns([z_in[f] for f in range(nf)], z0, zd)
    column_step(z0, g0, zd, gd, z1, mix, ntr, rows - 4)
    now = span(3, rows - 3)
    ocean_rows(m0, dv, z0, zd, wts, m1, ntr, now)
    tracer_rows(m0, z0, wts, dv, mix, moved, sat, m1, ntr, now)
    light_rows(m0, dv, moved, m1, ntr, now)
    dv1[WET, 3 : rows - 3] = dv[WET, 3 : rows - 3]
    derive_rows(m1, dv1, ntr, now)
    derive_columns(z1, zd, ntr)
    now = span(4, rows - 4)
    ocean_rows(m1, dv1, z1, zd, wts, m2, ntr, now)
    tracer_rows(m1, z1, wts, dv1, mix, moved, sat, m2, ntr, now)
    light_rows(m0, dv1, moved, m2, ntr, now)


def outer_kernel(m_own, dv_own, mix, g0, gd, z_in, rows_a, rows_b, edge_a, m1_in, m2_in, out, rim, keep, send, m0, m1, dv0, dv1, wts, sat, moved, z0, z1, zd, sem):
    nf, rows, nz, lon = m_own.shape
    ntr = nf - EXTRA
    lat_blk = rows - 4
    half, chip, _ = place()
    even = chip % 2 == 0
    south_ok, north_ok = (chip > 0, chip < lax.axis_size("row") // 2 - 1)
    copies = [
        pltpu.make_async_copy(m2_in.at[pl.ds(0, ntr), r], out.at[:, :, r - 2, :], sem.at[r - 4]) for r in range(4, rows // 2)
    ]
    for copy in copies:
        copy.start()

    def got(high, a, b):
        picked = jnp.where(even, a, b) if high else jnp.where(even, b, a)
        return jnp.where(north_ok if high else south_ok, picked, 0.0)

    for high, start in ((False, 0), (True, rows - 2)):
        for f in range(EXTRA):
            m0[ntr + f, start : start + 2] = got(high, *(x[pl.ds(2 * (ntr + f), 2)] for x in (rows_a, rows_b)))
        wet = wet_of(m0[nf - 1, start : start + 2])
        dv0[WET, start : start + 2] = wet
        for n in range(ntr):
            m0[n, start : start + 2] = got(high, *(x[pl.ds(2 * n, 2)] for x in (rows_a, rows_b))) * wet
        derive_rows(m0, dv0, ntr, span(start, start + 2))
    for start in (2, rows - 4):
        m0[:, start : start + 2] = m_own[:, start : start + 2]
        dv0[:, start : start + 2] = dv_own[:, start : start + 2]
    lane = lanes_of((nz, lon))
    low, high = (got(side, edge_a[...], rows_b[2 * nf]) for side in (False, True))
    at_low, at_high = (lane < WIN, (lane >= WIN * (lat_blk + 1)) & (lane < WIN * (lat_blk + 2)))
    fields = []
    for f in range(nf):
        cols = jnp.where(at_low, pltpu.roll(low, (-WIN * f) % lon, 1), z_in[f])
        fields.append(jnp.where(at_high, pltpu.roll(high, (WIN * (lat_blk + 1) - WIN * f) % lon, 1), cols))
    mask_columns(fields, z0, zd)
    column_step(z0, g0, zd, gd, z1, mix, ntr, lat_blk)
    now = (1, lat_blk, 2, 2)
    ocean_rows(m0, dv0, z0, zd, wts, m1, ntr, now)
    tracer_rows(m0, z0, wts, dv0, mix, moved, sat, m1, ntr, now)
    light_rows(m0, dv0, moved, m1, ntr, now)
    for start in (3, rows - 5):
        m1[:, start : start + 2] = m1_in[:, start : start + 2]
    for start in (1, rows - 3):
        dv1[WET, start : start + 2] = dv0[WET, start : start + 2]
    for start in (3, rows - 5):
        dv1[WET, start : start + 2] = dv_own[WET, start : start + 2]
    derive_rows(m1, dv1, ntr, (1, rows - 6, 2, 4))
    derive_columns(z1, zd, ntr)
    now = (2, rows - 6, 2, 2)
    ocean_rows(m1, dv1, z1, zd, wts, m0, ntr, now)
    tracer_rows(m1, z1, wts, dv1, mix, moved, sat, m0, ntr, now)
    light_rows(m0, dv1, moved, m0, ntr, now)

    rim[:, 0:2] = m0[:ntr, 2:4]
    rim[:, 2:4] = m0[:ntr, rows - 4 : rows - 2]
    m0[ntr : ntr + 3, 4 : rows - 4] = m2_in[ntr : ntr + 3, 4 : rows - 4]
    count = lat_blk // 2
    for f in range(3):
        keep[f] = m0[ntr + f, pl.ds(2 + half * count, count)]
        send[f] = m0[ntr + f, pl.ds(2 + (1 - half) * count, count)]
    for copy in copies:
        copy.wait()


def half_copies(part, core, buffer, flow_out, temp_out, sem):
    _, lat_dev, _, lon = part.shape
    for f in range(3):
        for t in range(lat_dev):
            buffer[f, :, t, :] = part[f, t]
    at = pl.ds(pl.multiple_of(core * lon, lon), lon)
    return [
        pltpu.make_async_copy(buffer.at[pl.ds(0, 2)], flow_out.at[:, :, :, at], sem.at[0]),
        pltpu.make_async_copy(buffer.at[2], temp_out.at[:, :, at], sem.at[1]),
    ]


def finish_own_kernel(keep, rim, m, out_in, flow_out, temp_out, out, buffer, sem):
    lat_blk = 2 * keep.shape[1]
    copies = [
        pltpu.make_async_copy(rim.at[:, i], out.at[:, :, t, :], sem.at[2 + i])
        for i, t in enumerate((0, 1, lat_blk - 2, lat_blk - 1))
    ]
    rows, ntr = (m.shape[1], rim.shape[0])
    copies += [
        pltpu.make_async_copy(m.at[pl.ds(0, ntr), r], out.at[:, :, r - 2, :], sem.at[6 + r - rows // 2])
        for r in range(rows // 2, rows - 4)
    ]
    for copy in copies:
        copy.start()
    more = half_copies(keep, place()[0], buffer, flow_out, temp_out, sem)
    for copy in more:
        copy.start()
    for copy in copies + more:
        copy.wait()


def finish_other_kernel(got, flow_in, temp_in, flow_out, temp_out, buffer, sem):
    copies = half_copies(got, 1 - place()[0], buffer, flow_out, temp_out, sem)
    for copy in copies:
        copy.start()
    for copy in copies:
        copy.wait()


def call(kernel, outs, *args, scratch=(), far=(), away=(), aliases=None, cost=1):
    vmem, anywhere = (pl.BlockSpec(memory_space=pltpu.VMEM), pl.BlockSpec(memory_space=pl.ANY))
    return pl.pallas_call(
        kernel,
        out_shape=[jax.ShapeDtypeStruct(s, jnp.float32) if isinstance(s, tuple) else s for s in outs],
        in_specs=[anywhere if i in far else vmem for i in range(len(args))],
        out_specs=[anywhere if i in away else vmem for i in range(len(outs))],
        scratch_shapes=[pltpu.VMEM(s, jnp.float32) if isinstance(s, tuple) else s for s in scratch],
        input_output_aliases=aliases or {},
        compiler_params=pltpu.CompilerParams(vmem_limit_bytes=40 * 2**20),
        cost_estimate=pl.CostEstimate(
            flops=int(cost * 10**9), transcendentals=0, bytes_accessed=int(cost * 4 * 2**20)
        ),
    )(*args)


def both_ways(pairs):
    return sorted(pairs + [(b, a) for a, b in pairs])


def exchanges(n_row, n_col):
    chips = n_row // 2

    def dev(p, h, c):
        return (2 * p + h) * n_col + c

    partner = [(dev(p, 0, c), dev(p, 1, c)) for p in range(chips) for c in range(n_col)]
    outer = [(dev(p, 1, c), dev(p, 0, c + 1)) for p in range(chips) for c in range(n_col - 1)]
    for p in range(0, chips - 1, 2):
        outer += [(dev(p, 0, 0), dev(p + 1, 0, 0)), (dev(p, 1, n_col - 1), dev(p + 1, 1, n_col - 1))]
    lat_a = [(dev(p, h, c), dev(p + 1, h, c)) for p in range(0, chips - 1, 2) for h in (0, 1) for c in range(n_col)]
    lat_b = [(dev(p, h, c), dev(p + 1, h, c)) for p in range(1, chips - 1, 2) for h in (0, 1) for c in range(n_col)]
    ends = [0] if chips % 2 else [0, chips - 1]
    lat_b += [(dev(p, 0, c), dev(p, 1, c)) for p in ends for c in range(n_col)]
    return [both_ways(x) for x in (partner, outer, lat_a, lat_b)]


def on_device(n_row, n_col, flow, temp, tracers, bottom, sunlight, rates):
    nz, lat_dev, lon_dev = temp.shape
    _, ntr, _, lat_blk, lon = tracers.shape
    nf = ntr + EXTRA
    partner, outer, lat_a, lat_b = exchanges(n_row, n_col)

    def swap(x, pairs):
        return lax.ppermute(x, ("row", "col"), pairs)

    block = tracers[0]
    rows = lat_blk + 4
    cols, extra, some = ((nf, nz, lon), (EXTRA, nz, lon), (3, nz, lon))
    sent = ((EXTRA - 1) * lat_dev + 2 + EXTRA, nz, lon)
    given = (flow, temp, bottom, sunlight, block)
    mine, to_partner, g_other, block = call(
        pack_ocean_kernel,
        [(EXTRA, lat_dev, nz, lon), sent, extra, block.shape],
        *[pltpu.with_memory_space_constraint(x, pltpu.HBM) for x in given],
        scratch=[
            flow.shape,
            temp.shape,
            pltpu.VMEM(bottom.shape, jnp.int32),
            sunlight.shape,
            pltpu.SemaphoreType.DMA((len(given),)),
        ],
        far=range(len(given)),
    )
    got = swap(to_partner, partner)
    turned, g_tracers = call(pack_tracers_kernel, [(ntr, lat_blk, nz, lon), (ntr, nz, lon)], block)
    rim = (2 * nf, nz, lon)
    ocean, g_own, to_outer, rows_a = call(
        join_kernel,
        [(EXTRA, lat_blk, nz, lon), cols, (nf // 4, nz, lon), rim],
        mine,
        got,
        to_partner,
        g_tracers,
        turned,
    )
    rows_a = swap(rows_a, lat_a)
    from_outer = swap(to_outer, outer)
    g_partner = swap(g_tracers, partner)
    full, derived = ((nf, rows, nz, lon), (3, rows, nz, lon))
    m0, dv, mix, g0, gd, inner = call(
        fill_kernel,
        [full, derived, jax.ShapeDtypeStruct((2 * ntr * nz, 2 * ntr * nz), jnp.bfloat16), cols, some, cols],
        turned,
        ocean,
        g_own,
        g_partner,
        got,
        g_other,
        rates,
    )
    z, edge_a, rows_b = call(
        edge_kernel, [cols, (nz, lon), (2 * nf + 1, nz, lon)], turned, ocean, inner, from_outer
    )
    rows_b, edge_a = (swap(rows_b, lat_b), swap(edge_a, lat_a))
    work = [(7, rows, nz, lon), pltpu.VMEM((rows, 2 * ntr * nz, lon), jnp.bfloat16)]
    work += [(ntr + 1, rows, nz, lon), cols, cols, some]
    m1, m2 = call(inner_kernel, [full, full], m0, dv, mix, g0, gd, z, scratch=[derived] + work, cost=20)
    third = (3, lat_dev, nz, lon)
    out, rim, keep, send = call(
        outer_kernel,
        [(ntr, nz, lat_blk, lon), (ntr, 4, nz, lon), third, third],
        m0,
        dv,
        mix,
        g0,
        gd,
        z,
        rows_a,
        rows_b,
        edge_a,
        m1,
        m2,
        scratch=[full, full, derived, derived] + work + [pltpu.SemaphoreType.DMA((lat_blk - 4,))],
        away=(0,),
    )
    returned = swap(send, partner)
    buffer = (3, nz, lat_dev, lon)
    flow_out, temp_out, out = call(
        finish_own_kernel,
        [flow.shape, temp.shape, out.shape],
        keep,
        rim,
        m2,
        out,
        scratch=[buffer, pltpu.SemaphoreType.DMA((6 + rows // 2 - 4,))],
        far=(3,),
        away=(0, 1, 2),
        aliases={3: 2},
    )
    flow_out, temp_out = call(
        finish_other_kernel,
        [flow.shape, temp.shape],
        returned,
        flow_out,
        temp_out,
        scratch=[buffer, pltpu.SemaphoreType.DMA((2,))],
        far=(1, 2),
        away=(0, 1),
        aliases={1: 0, 2: 1},
    )
    return (flow_out, temp_out, out[None])


def solution(mesh):
    in_specs = (
        P(None, None, "row", "col"),
        P(None, "row", "col"),
        P("row", None, None, None, "col"),
        P("row", "col"),
        P("row", "col"),
        P(),
    )
    out_specs = (
        P(None, None, "row", "col"),
        P(None, "row", "col"),
        P("row", None, None, None, "col"),
    )
    return jax.shard_map(
        functools.partial(on_device, mesh.shape["row"], mesh.shape["col"]),
        mesh=mesh,
        in_specs=in_specs,
        out_specs=out_specs,
        check_vma=False,
    )
```

```python
import functools
import jax
import jax.numpy as jnp
from jax import lax
from jax.experimental import pallas as pl
from jax.experimental.pallas import tpu as pltpu
from jax.sharding import PartitionSpec as P

KL = 4
STEPS = 2

time_step = 0.2
viscosity = 0.2
expansion = 0.05
coriolis_base = 0.5
kappa_base = 0.05
kappa_shear = 0.2
react_step = 0.25
water_absorb = 0.1
pigment_absorb = 0.6
heat_gain = 1.0

EXTRA = 4
WIN = 4


def up(x):
    return pltpu.roll(x, 1, x.ndim - 2)


def down(x):
    return pltpu.roll(x, x.shape[-2] - 1, x.ndim - 2)


def lanes_of(shape):
    return lax.broadcasted_iota(jnp.int32, shape, len(shape) - 1)


def levels_of(shape):
    return lax.broadcasted_iota(jnp.int32, shape, len(shape) - 2)


def window(x, lat, into):
    lon = x.shape[1]
    lane = lanes_of(x.shape)
    base = WIN * (lat + 1)
    moved = pltpu.roll(x, (base + 2) % lon, 1)
    return jnp.where((lane >= base) & (lane < base + WIN), moved, into)


def place():
    row = lax.axis_index("row")
    return (row % 2, row // 2, lax.axis_index("col"))


def edge_starts(chip, lat_blk):
    odd = chip % 2
    return ((1 - odd) * (lat_blk - 2), odd * (lat_blk - 2))


def pack_ocean_kernel(flow_in, temp_in, bottom_in, sunlight_in, tracers_in, mine, to_partner, g_other, tracers, flow, temp, bottom, sunlight, sem):
    copies = [
        pltpu.make_async_copy(src, dst, sem.at[i])
        for i, (src, dst) in enumerate(
            ((flow_in, flow), (temp_in, temp), (bottom_in, bottom), (sunlight_in, sunlight), (tracers_in, tracers))
        )
    ]
    for copy in copies:
        copy.start()
    for copy in copies[:-1]:
        copy.wait()
    lat_dev, nz, lon = mine.shape[1:]
    lon_dev = temp.shape[2]
    half, _, _ = place()
    first = half == 0
    zero = jnp.zeros((nz, lon), jnp.float32)
    level = levels_of((nz, lon_dev))
    own = [zero] * EXTRA
    far = [zero] * EXTRA
    for t in range(lat_dev):
        depth = jnp.broadcast_to(bottom[t : t + 1, :], (nz, lon_dev))
        light = jnp.broadcast_to(sunlight[t : t + 1, :], (nz, lon_dev))
        wet = (level < depth).astype(jnp.float32)
        aux = jnp.where(level == 0, depth.astype(jnp.float32), jnp.where(level == 1, light, 0.0))
        for f, tile in enumerate((flow[0, :, t, :] * wet, flow[1, :, t, :] * wet, temp[:, t, :] * wet, aux)):
            low, high = (tile[:, :lon], tile[:, lon:])
            a, b = (jnp.where(first, low, high), jnp.where(first, high, low))
            mine[f, t] = a
            if f < EXTRA - 1:
                to_partner[f * lat_dev + t] = b
            own[f] = window(a, t, own[f])
            far[f] = window(b, t, far[f])
    flat = (EXTRA - 1) * lat_dev
    for i, both in enumerate((bottom[...].astype(jnp.float32), sunlight[...])):
        to_partner[flat + i, :lat_dev, :] = jnp.where(first, both[:, lon:], both[:, :lon])
    shift = half * (WIN * lat_dev)
    for f in range(EXTRA):
        to_partner[flat + 2 + f] = pltpu.roll(own[f], shift, 1)
        g_other[f] = pltpu.roll(far[f], shift, 1)
    copies[-1].wait()


def pack_tracers_kernel(tracers, turned, g_tracers):
    ntr, nz, lat_blk, lon = tracers.shape

    def some(i, _):
        g = [jnp.zeros((nz, lon), jnp.float32)] * PACK
        for t in range(lat_blk):
            for k in range(PACK):
                x = tracers[i * PACK + k, :, t, :]
                turned[i * PACK + k, t] = x
                g[k] = window(x, t, g[k])
        for k in range(PACK):
            g_tracers[i * PACK + k] = g[k]
        return 0

    lax.fori_loop(0, ntr // PACK, some, 0)


def in_half(shape, half, lat_dev):
    lane = lanes_of(shape)
    base = WIN * (lat_dev * half + 1)
    return (lane >= base) & (lane < base + WIN * lat_dev)


def edge_rows(turned, ocean, start, out):
    ntr = turned.shape[0]
    for n in range(ntr):
        out[2 * n : 2 * n + 2] = turned[n, pl.ds(start, 2)]
    for f in range(EXTRA):
        out[2 * (ntr + f) : 2 * (ntr + f) + 2] = ocean[f, pl.ds(start, 2)]


def join_kernel(mine, got, to_partner, g_tracers, turned, ocean, g_own, to_outer, rows_a):
    _, lat_dev, nz, lon = mine.shape
    ntr = g_tracers.shape[0]
    nf = ntr + EXTRA
    half, chip, _ = place()
    tile = (nz, lon)
    own_lanes = in_half(tile, half, lat_dev)
    shift = (1 - half) * (WIN * lat_dev)
    flat, level = ((EXTRA - 1) * lat_dev, levels_of(tile))
    g_own[:ntr] = g_tracers[...]
    for f in range(EXTRA):
        g = jnp.zeros(tile, jnp.float32)
        for t in range(lat_dev):
            if f < EXTRA - 1:
                x = got[f * lat_dev + t]
            else:
                depth, light = (jnp.broadcast_to(got[flat + i, t : t + 1, :], tile) for i in range(2))
                x = jnp.where(level == 0, depth, jnp.where(level == 1, light, 0.0))
            ocean[f, half * lat_dev + t] = mine[f, t]
            ocean[f, (1 - half) * lat_dev + t] = x
            g = window(x, t, g)
        g_own[ntr + f] = jnp.where(own_lanes, to_partner[flat + 2 + f], pltpu.roll(g, shift, 1))
    edge_rows(turned, ocean, edge_starts(chip, 2 * lat_dev)[0], rows_a)
    lane = lanes_of(tile)
    front, near = (lane % WIN < 2, in_half(tile, 0, 2 * lat_dev))
    side = (1 - half) * (lon - 2)
    for i in range(nf // 4):
        a, b, c, d = [pltpu.roll(g_own[4 * i + k], side, 1) for k in range(4)]
        low = jnp.where(front, a, pltpu.roll(b, 2, 1))
        high = jnp.where(front, c, pltpu.roll(d, 2, 1))
        to_outer[i] = jnp.where(near, low, pltpu.roll(high, lon // 2, 1))


def edge_kernel(turned, ocean, inner, from_outer, z, to_a, to_b):
    nf, nz, lon = z.shape
    lat_blk = turned.shape[1]

    half, chip, column = place()
    tile = (nz, lon)
    lane = lanes_of(tile)
    outer_ok = jnp.where(half == 0, column > 0, column < lax.axis_size("col") - 1)
    from_partner = (lane % WIN < 2).astype(jnp.int32) == half
    outer_lanes = in_half(tile, 0, lat_blk) & outer_ok
    start_a, start_b = edge_starts(chip, lat_blk)
    corner_a = corner_b = jnp.zeros(tile, jnp.float32)
    for f in range(nf):
        k = f % 4
        moved = pltpu.roll(from_outer[f // 4], lon + 2 * half - 2 * (k % 2) - lon // 2 * (k // 2), 1)
        cols = jnp.where(from_partner, inner[f], jnp.where(outer_lanes, moved, 0.0))
        z[f] = cols
        at = (lane >= WIN * f) & (lane < WIN * f + WIN)
        low = pltpu.roll(cols, (WIN * f - WIN) % lon, 1)
        high = pltpu.roll(cols, (WIN * f - WIN * lat_blk) % lon, 1)
        corner_a = jnp.where(at, jnp.where(start_a > 0, high, low), corner_a)
        corner_b = jnp.where(at, jnp.where(start_b > 0, high, low), corner_b)
    to_a[...] = corner_a
    edge_rows(turned, ocean, start_b, to_b)
    to_b[2 * nf] = corner_b


def kappa_of(u, v):
    du, dv = (u - down(u), v - down(v))
    sq = jnp.where(levels_of(u.shape) < u.shape[-2] - 1, du * du + dv * dv, 0.0)
    return kappa_base + kappa_shear * sq / (1.0 + sq)


def sum_above(x):
    level = levels_of(x.shape)
    k = 1
    while k < x.shape[-2]:
        x = x + jnp.where(level >= k, pltpu.roll(x, k, x.ndim - 2), 0.0)
        k *= 2
    return x


def sum_below(x):
    level, nz = (levels_of(x.shape), x.shape[-2])
    k = 1
    while k < nz:
        x = x + jnp.where(level < nz - k, pltpu.roll(x, nz - k, x.ndim - 2), 0.0)
        k *= 2
    return x


def pressure_of(heat):
    return -expansion * sum_above(heat)


def wet_of(aux):
    depth = jnp.broadcast_to(aux[..., 0:1, :], aux.shape)
    return (levels_of(aux.shape).astype(jnp.float32) < depth).astype(jnp.float32)


def light_of(aux):
    return jnp.broadcast_to(aux[..., 1:2, :], aux.shape)


def dynamics(u, v, wet, kap, prs, coriolis):
    um, ue, uw, un, us = u
    vm, ve, vw, vn, vs = v
    wm, we, ww, wn, ws = wet
    km, ke, kw, kn, ks = kap
    _, pe, pw, pn, ps = prs
    level, nz = (levels_of(um.shape), um.shape[-2])
    oe, ow, on, os_ = (wm * we, wm * ww, wm * wn, wm * ws)
    fe, fw, fn, fs = (0.5 * (um + ue) * oe, 0.5 * (um + uw) * ow, 0.5 * (vm + vn) * on, 0.5 * (vm + vs) * os_)
    ce, cw, cn, cs = (0.5 * (km + ke) * oe, 0.5 * (km + kw) * ow, 0.5 * (km + kn) * on, 0.5 * (km + ks) * os_)
    div = fe - fw + fn - fs
    total = sum_below(div)
    w_top = jnp.where(level >= 1, -total, 0.0)
    w_bot = jnp.where(level < nz - 1, -down(total), 0.0)
    weights = (
        wm * (1.0 - time_step * (ce + cw + cn + cs + 0.5 * (div + w_top - w_bot))),
        time_step * (ce - 0.5 * fe),
        time_step * (cw + 0.5 * fw),
        time_step * (cn - 0.5 * fn),
        time_step * (cs + 0.5 * fs),
        (-0.5 * time_step) * wm * w_top,
        (0.5 * time_step) * wm * w_bot,
    )
    lap_u = oe * (ue - um) + ow * (uw - um) + on * (un - um) + os_ * (us - um)
    lap_v = oe * (ve - vm) + ow * (vw - vm) + on * (vn - vm) + os_ * (vs - vm)
    new_u = wm * (um + time_step * (coriolis * vm - 0.5 * (pe - pw) + viscosity * lap_u))
    new_v = wm * (vm + time_step * (-coriolis * um - 0.5 * (pn - ps) + viscosity * lap_v))
    return (new_u, new_v, weights)


def transport(weights, x, east, west, north, south):
    a0, ae, aw, an, as_, at, ab = weights
    return (a0 * x + ae * east) + (aw * west + an * north) + (as_ * south + at * up(x)) + ab * down(x)


def saturated(x):
    return x * lax.rsqrt(1.0 + x * x)


def absorbed(pigment):
    level = levels_of(pigment.shape)
    sq = pigment * pigment
    depth = water_absorb + pigment_absorb * (sq / (1.0 + sq))
    above = jnp.where(level >= 1, up(depth), 0.0)
    k = 1
    while k < KL:
        above = above + jnp.where(level >= k, pltpu.roll(above, k, above.ndim - 2), 0.0)
        k *= 2
    return jnp.where(level < KL, jnp.exp(-above) * (1.0 - jnp.exp(-depth)), 0.0)


def two_parts(x):
    high = x.astype(jnp.bfloat16)
    return (high, (x - high.astype(jnp.float32)).astype(jnp.bfloat16))


def mix_matrix(rates, nz):
    ntr = rates.shape[0]
    size = ntr * nz
    exact = dict(precision=lax.Precision.HIGHEST, preferred_element_type=jnp.float32)
    spread = lax.broadcasted_iota(jnp.int32, (size, ntr), 0) // nz == lax.broadcasted_iota(jnp.int32, (size, ntr), 1)
    spread = spread.astype(jnp.float32)
    wide = jnp.dot(spread, rates, **exact)
    full = lax.dot_general(wide, spread, (((1,), (1,)), ((), ())), **exact)
    same = lax.broadcasted_iota(jnp.int32, (size, size), 0) % nz == lax.broadcasted_iota(jnp.int32, (size, size), 1) % nz
    high, low = two_parts(jnp.where(same, full, 0.0))
    top = jnp.concatenate([high, high], axis=1)
    return jnp.concatenate([top, jnp.concatenate([low, jnp.zeros_like(low)], axis=1)], axis=0)


def beside(z, r, lon):
    return pltpu.roll(z, lon - 2 - WIN * (r - 1), z.ndim - 1)


def sides(x, edge):
    lane, lon = (lanes_of(x.shape), x.shape[-1])
    west = pltpu.roll(jnp.where(lane == lon - 1, edge, x), 1, x.ndim - 1)
    east = pltpu.roll(jnp.where(lane == 0, edge, x), lon - 1, x.ndim - 1)
    return (east, west)


def around_rows(m, f, z, r, count):
    x = m[f, pl.ds(r, count)]
    edge = jnp.stack([beside(z, r + i, x.shape[-1]) for i in range(count)])
    return (x, *sides(x, edge), m[f, pl.ds(r + 1, count)], m[f, pl.ds(r - 1, count)])


def around_columns(x, own):
    lane, lon = (lanes_of(x.shape), x.shape[-1])
    west = pltpu.roll(jnp.where(lane % WIN == 0, x, own), 1, x.ndim - 1)
    east = pltpu.roll(jnp.where(lane % WIN == WIN - 1, x, own), lon - 1, x.ndim - 1)
    return (x, east, west, pltpu.roll(x, lon - WIN, x.ndim - 1), pltpu.roll(x, WIN, x.ndim - 1))


def coriolis_at(lat, lat_blk):
    _, chip, _ = place()
    latitude = (lat + chip * lat_blk).astype(jnp.float32)
    return coriolis_base * (2.0 * (latitude + 0.5) / (lax.axis_size("row") // 2 * lat_blk) - 1.0)


KAP, PRS, WET = (0, 1, 2)
GROUP = 8
PACK = 16
PIECE = 3


def span(start, stop):
    return (start, stop - start, 1, stop - start)


def chunks(rows, most, body):
    first, apart, times, size = rows
    count = max(k for k in range(1, min(most, size) + 1) if size % k == 0)
    if times > 1 or count == size:
        for i in range(times):
            body(first + i * apart, size)
    else:

        def one(i, _):
            body(first + i * count, count)
            return 0

        lax.fori_loop(0, size // count, one, 0)


def derive_rows(m, dv, ntr, rows):
    def body(r, count):
        at = pl.ds(r, count)
        dv[KAP, at] = kappa_of(m[ntr, at], m[ntr + 1, at])
        dv[PRS, at] = pressure_of(m[ntr + 2, at])

    chunks(rows, 10, body)


def derive_columns(z, zd, ntr):
    zd[KAP] = kappa_of(z[ntr], z[ntr + 1])
    zd[PRS] = pressure_of(z[ntr + 2])


def ocean_rows(m, dv, z, zd, wts, new, ntr, rows):
    def body(r, count):
        at = pl.ds(r, count)
        lat = lax.broadcasted_iota(jnp.int32, (count, *m.shape[2:]), 0) + (r - 2)
        new_u, new_v, weights = dynamics(
            around_rows(m, ntr, z[ntr], r, count),
            around_rows(m, ntr + 1, z[ntr + 1], r, count),
            around_rows(dv, WET, zd[WET], r, count),
            around_rows(dv, KAP, zd[KAP], r, count),
            around_rows(dv, PRS, zd[PRS], r, count),
            coriolis_at(lat, m.shape[1] - 4),
        )
        new[ntr, at] = new_u
        new[ntr + 1, at] = new_v
        for i, w in enumerate(weights):
            wts[i, at] = w

    chunks(rows, 9, body)


def tracer_rows(m, z, wts, dv, mix, moved, sat, new, ntr, rows):
    nz, lon = m.shape[2:]
    half = ntr * nz
    first, apart, times, count = rows
    if times == 1:
        count = max(k for k in range(1, PIECE + 1) if rows[3] % k == 0)
        apart, times = (count, rows[3] // count)

    def move(r):
        weights = [wts[i, r] for i in range(7)]
        for n in range(0, ntr, GROUP):
            x = m[n : n + GROUP, r]
            edge = beside(z[n : n + GROUP], r, lon)
            done = transport(weights, x, *sides(x, edge), m[n : n + GROUP, r + 1], m[n : n + GROUP, r - 1])
            moved[n : n + GROUP, r] = done
            high, low = two_parts(saturated(done).reshape(GROUP * nz, lon))
            sat[r, n * nz : (n + GROUP) * nz, :] = high
            sat[r, half + n * nz : half + (n + GROUP) * nz, :] = low
        h = ntr + 2
        x = m[h, r]
        moved[ntr, r] = transport(weights, x, *sides(x, beside(z[h], r, lon)), m[h, r + 1], m[h, r - 1])

    def react(every):
        both = jnp.concatenate([sat[r] for r in every], axis=1)
        res = jnp.dot(mix[...], both, preferred_element_type=jnp.float32)
        res = res[:half] + res[half:]
        for i, r in enumerate(every):
            gain = react_step * dv[WET, r]
            for n in range(ntr):
                new[n, r] = moved[n, r] + gain * res[n * nz : (n + 1) * nz, i * lon : (i + 1) * lon]

    def piece(i):
        return [first + i * apart + k for k in range(count)]

    def both_parts(i, _):
        react(piece(i - 1))
        for r in piece(i):
            move(r)
        return 0

    if rows[2] > 1:
        every = [r for i in range(times) for r in piece(i)]
        for r in every:
            move(r)
        react(every)
    else:
        for r in piece(0):
            move(r)
        lax.fori_loop(1, times, both_parts, 0)
        react(piece(times - 1))


def light_rows(m, dv, moved, new, ntr, rows):
    def body(r, count):
        at = pl.ds(r, count)
        light = light_of(m[ntr + 3, at]) * dv[WET, at] * absorbed(new[0, at])
        new[ntr + 2, at] = moved[ntr, at] + heat_gain * light

    chunks(rows, 9, body)


def column_step(z0, g0, zd, gd, z1, mix, ntr, lat_blk):
    nz, lon = z0.shape[1:]
    half = ntr * nz
    wet = zd[WET]
    new_u, new_v, weights = dynamics(
        around_columns(z0[ntr], g0[ntr]),
        around_columns(z0[ntr + 1], g0[ntr + 1]),
        around_columns(wet, gd[WET]),
        around_columns(zd[KAP], gd[KAP]),
        around_columns(zd[PRS], gd[PRS]),
        coriolis_at(lanes_of((nz, lon)) // WIN - 1, lat_blk),
    )
    moved = transport(weights, *around_columns(z0[:ntr], g0[:ntr]))
    high, low = two_parts(saturated(moved).reshape(half, lon))
    res = jnp.dot(mix[...], jnp.concatenate([high, low], axis=0), preferred_element_type=jnp.float32)
    done = moved + (react_step * wet) * (res[:half] + res[half:]).reshape(ntr, nz, lon)
    z1[:ntr] = done
    z1[ntr] = new_u
    z1[ntr + 1] = new_v
    heat = transport(weights, *around_columns(z0[ntr + 2], g0[ntr + 2]))
    z1[ntr + 2] = heat + heat_gain * light_of(z0[ntr + 3]) * wet * absorbed(done[0])


def fill_kernel(turned, ocean, g_own, g_partner, got, g_other, rates, m0, dv, mix, g0, gd, inner):
    ntr, lat_blk, nz, lon = turned.shape
    half, _, _ = place()
    inner[:ntr] = g_partner[...]
    for f in range(EXTRA):
        theirs = got[(EXTRA - 1) * (lat_blk // 2) + 2 + f]
        inner[ntr + f] = jnp.where(in_half((nz, lon), half, lat_blk // 2), g_other[f], theirs)
    mix[...] = mix_matrix(rates[...], nz)
    own = span(2, lat_blk + 2)

    def wets(r, count):
        at = pl.ds(r, count)
        for f in range(EXTRA):
            m0[ntr + f, at] = ocean[f, pl.ds(r - 2, count)]
        dv[WET, at] = wet_of(ocean[EXTRA - 1, pl.ds(r - 2, count)])

    chunks(own, 8, wets)

    def some(r, count):
        wet = dv[WET, r]
        for n in range(ntr):
            m0[n, r] = turned[n, r - 2] * wet

    chunks(own, 1, some)
    derive_rows(m0, dv, ntr, own)
    mask_columns([g_own[f] for f in range(ntr + EXTRA)], g0, gd)


def mask_columns(fields, z, zd):
    ntr = len(fields) - EXTRA
    wet = wet_of(fields[-1])
    zd[WET] = wet
    for f, cols in enumerate(fields):
        z[f] = cols * wet if f < ntr else cols
    derive_columns(z, zd, ntr)


def inner_kernel(m0, dv, mix, g0, gd, z_in, m1, m2, dv1, wts, sat, moved, z0, z1, zd):
    nf, rows, _, _ = m0.shape
    ntr = nf - EXTRA
    mask_columns([z_in[f] for f in range(nf)], z0, zd)
    column_step(z0, g0, zd, gd, z1, mix, ntr, rows - 4)
    now = span(3, rows - 3)
    ocean_rows(m0, dv, z0, zd, wts, m1, ntr, now)
    tracer_rows(m0, z0, wts, dv, mix, moved, sat, m1, ntr, now)
    light_rows(m0, dv, moved, m1, ntr, now)
    dv1[WET, 3 : rows - 3] = dv[WET, 3 : rows - 3]
    derive_rows(m1, dv1, ntr, now)
    derive_columns(z1, zd, ntr)
    now = span(4, rows - 4)
    ocean_rows(m1, dv1, z1, zd, wts, m2, ntr, now)
    tracer_rows(m1, z1, wts, dv1, mix, moved, sat, m2, ntr, now)
    light_rows(m0, dv1, moved, m2, ntr, now)


def outer_kernel(m_own, dv_own, mix, g0, gd, z_in, rows_a, rows_b, edge_a, m1_in, m2_in, out, rim, keep, send, m0, m1, dv0, dv1, wts, sat, moved, z0, z1, zd, sem):
    nf, rows, nz, lon = m_own.shape
    ntr = nf - EXTRA
    lat_blk = rows - 4
    half, chip, _ = place()
    even = chip % 2 == 0
    south_ok, north_ok = (chip > 0, chip < lax.axis_size("row") // 2 - 1)
    copies = [
        pltpu.make_async_copy(m2_in.at[pl.ds(0, ntr), r], out.at[:, :, r - 2, :], sem.at[r - 4]) for r in range(4, rows // 2)
    ]
    for copy in copies:
        copy.start()

    def got(high, a, b):
        picked = jnp.where(even, a, b) if high else jnp.where(even, b, a)
        return jnp.where(north_ok if high else south_ok, picked, 0.0)

    for high, start in ((False, 0), (True, rows - 2)):
        for f in range(EXTRA):
            m0[ntr + f, start : start + 2] = got(high, *(x[pl.ds(2 * (ntr + f), 2)] for x in (rows_a, rows_b)))
        wet = wet_of(m0[nf - 1, start : start + 2])
        dv0[WET, start : start + 2] = wet
        for n in range(ntr):
            m0[n, start : start + 2] = got(high, *(x[pl.ds(2 * n, 2)] for x in (rows_a, rows_b))) * wet
        derive_rows(m0, dv0, ntr, span(start, start + 2))
    for start in (2, rows - 4):
        m0[:, start : start + 2] = m_own[:, start : start + 2]
        dv0[:, start : start + 2] = dv_own[:, start : start + 2]
    lane = lanes_of((nz, lon))
    low, high = (got(side, edge_a[...], rows_b[2 * nf]) for side in (False, True))
    at_low, at_high = (lane < WIN, (lane >= WIN * (lat_blk + 1)) & (lane < WIN * (lat_blk + 2)))
    fields = []
    for f in range(nf):
        cols = jnp.where(at_low, pltpu.roll(low, (-WIN * f) % lon, 1), z_in[f])
        fields.append(jnp.where(at_high, pltpu.roll(high, (WIN * (lat_blk + 1) - WIN * f) % lon, 1), cols))
    mask_columns(fields, z0, zd)
    column_step(z0, g0, zd, gd, z1, mix, ntr, lat_blk)
    now = (1, lat_blk, 2, 2)
    ocean_rows(m0, dv0, z0, zd, wts, m1, ntr, now)
    tracer_rows(m0, z0, wts, dv0, mix, moved, sat, m1, ntr, now)
    light_rows(m0, dv0, moved, m1, ntr, now)
    for start in (3, rows - 5):
        m1[:, start : start + 2] = m1_in[:, start : start + 2]
    for start in (1, rows - 3):
        dv1[WET, start : start + 2] = dv0[WET, start : start + 2]
    for start in (3, rows - 5):
        dv1[WET, start : start + 2] = dv_own[WET, start : start + 2]
    derive_rows(m1, dv1, ntr, (1, rows - 6, 2, 4))
    derive_columns(z1, zd, ntr)
    now = (2, rows - 6, 2, 2)
    ocean_rows(m1, dv1, z1, zd, wts, m0, ntr, now)
    tracer_rows(m1, z1, wts, dv1, mix, moved, sat, m0, ntr, now)
    light_rows(m0, dv1, moved, m0, ntr, now)

    rim[:, 0:2] = m0[:ntr, 2:4]
    rim[:, 2:4] = m0[:ntr, rows - 4 : rows - 2]
    m0[ntr : ntr + 3, 4 : rows - 4] = m2_in[ntr : ntr + 3, 4 : rows - 4]
    count = lat_blk // 2
    for f in range(3):
        keep[f] = m0[ntr + f, pl.ds(2 + half * count, count)]
        send[f] = m0[ntr + f, pl.ds(2 + (1 - half) * count, count)]
    for copy in copies:
        copy.wait()


def half_copies(part, core, buffer, flow_out, temp_out, sem):
    _, lat_dev, _, lon = part.shape
    for f in range(3):
        for t in range(lat_dev):
            buffer[f, :, t, :] = part[f, t]
    at = pl.ds(pl.multiple_of(core * lon, lon), lon)
    return [
        pltpu.make_async_copy(buffer.at[pl.ds(0, 2)], flow_out.at[:, :, :, at], sem.at[0]),
        pltpu.make_async_copy(buffer.at[2], temp_out.at[:, :, at], sem.at[1]),
    ]


def finish_own_kernel(keep, rim, m, out_in, flow_out, temp_out, out, buffer, sem):
    lat_blk = 2 * keep.shape[1]
    copies = [
        pltpu.make_async_copy(rim.at[:, i], out.at[:, :, t, :], sem.at[2 + i])
        for i, t in enumerate((0, 1, lat_blk - 2, lat_blk - 1))
    ]
    rows, ntr = (m.shape[1], rim.shape[0])
    copies += [
        pltpu.make_async_copy(m.at[pl.ds(0, ntr), r], out.at[:, :, r - 2, :], sem.at[6 + r - rows // 2])
        for r in range(rows // 2, rows - 4)
    ]
    for copy in copies:
        copy.start()
    more = half_copies(keep, place()[0], buffer, flow_out, temp_out, sem)
    for copy in more:
        copy.start()
    for copy in copies + more:
        copy.wait()


def finish_other_kernel(got, flow_in, temp_in, flow_out, temp_out, buffer, sem):
    copies = half_copies(got, 1 - place()[0], buffer, flow_out, temp_out, sem)
    for copy in copies:
        copy.start()
    for copy in copies:
        copy.wait()


def call(kernel, outs, *args, scratch=(), far=(), away=(), aliases=None, cost=1):
    vmem, anywhere = (pl.BlockSpec(memory_space=pltpu.VMEM), pl.BlockSpec(memory_space=pl.ANY))
    return pl.pallas_call(
        kernel,
        out_shape=[jax.ShapeDtypeStruct(s, jnp.float32) if isinstance(s, tuple) else s for s in outs],
        in_specs=[anywhere if i in far else vmem for i in range(len(args))],
        out_specs=[anywhere if i in away else vmem for i in range(len(outs))],
        scratch_shapes=[pltpu.VMEM(s, jnp.float32) if isinstance(s, tuple) else s for s in scratch],
        input_output_aliases=aliases or {},
        compiler_params=pltpu.CompilerParams(vmem_limit_bytes=40 * 2**20),
        cost_estimate=pl.CostEstimate(
            flops=int(cost * 10**9), transcendentals=0, bytes_accessed=int(cost * 4 * 2**20)
        ),
    )(*args)


def both_ways(pairs):
    return sorted(pairs + [(b, a) for a, b in pairs])


def exchanges(n_row, n_col):
    chips = n_row // 2

    def dev(p, h, c):
        return (2 * p + h) * n_col + c

    partner = [(dev(p, 0, c), dev(p, 1, c)) for p in range(chips) for c in range(n_col)]
    outer = [(dev(p, 1, c), dev(p, 0, c + 1)) for p in range(chips) for c in range(n_col - 1)]
    for p in range(0, chips - 1, 2):
        outer += [(dev(p, 0, 0), dev(p + 1, 0, 0)), (dev(p, 1, n_col - 1), dev(p + 1, 1, n_col - 1))]
    lat_a = [(dev(p, h, c), dev(p + 1, h, c)) for p in range(0, chips - 1, 2) for h in (0, 1) for c in range(n_col)]
    lat_b = [(dev(p, h, c), dev(p + 1, h, c)) for p in range(1, chips - 1, 2) for h in (0, 1) for c in range(n_col)]
    ends = [0] if chips % 2 else [0, chips - 1]
    lat_b += [(dev(p, 0, c), dev(p, 1, c)) for p in ends for c in range(n_col)]
    return [both_ways(x) for x in (partner, outer, lat_a, lat_b)]


def on_device(n_row, n_col, flow, temp, tracers, bottom, sunlight, rates):
    nz, lat_dev, lon_dev = temp.shape
    _, ntr, _, lat_blk, lon = tracers.shape
    nf = ntr + EXTRA
    partner, outer, lat_a, lat_b = exchanges(n_row, n_col)

    def swap(x, pairs):
        return lax.ppermute(x, ("row", "col"), pairs)

    block = tracers[0]
    rows = lat_blk + 4
    cols, extra, some = ((nf, nz, lon), (EXTRA, nz, lon), (3, nz, lon))
    sent = ((EXTRA - 1) * lat_dev + 2 + EXTRA, nz, lon)
    given = (flow, temp, bottom, sunlight, block)
    mine, to_partner, g_other, block = call(
        pack_ocean_kernel,
        [(EXTRA, lat_dev, nz, lon), sent, extra, block.shape],
        *[pltpu.with_memory_space_constraint(x, pltpu.HBM) for x in given],
        scratch=[
            flow.shape,
            temp.shape,
            pltpu.VMEM(bottom.shape, jnp.int32),
            sunlight.shape,
            pltpu.SemaphoreType.DMA((len(given),)),
        ],
        far=range(len(given)),
    )
    got = swap(to_partner, partner)
    turned, g_tracers = call(pack_tracers_kernel, [(ntr, lat_blk, nz, lon), (ntr, nz, lon)], block)
    rim = (2 * nf, nz, lon)
    ocean, g_own, to_outer, rows_a = call(
        join_kernel,
        [(EXTRA, lat_blk, nz, lon), cols, (nf // 4, nz, lon), rim],
        mine,
        got,
        to_partner,
        g_tracers,
        turned,
    )
    rows_a = swap(rows_a, lat_a)
    from_outer = swap(to_outer, outer)
    g_partner = swap(g_tracers, partner)
    full, derived = ((nf, rows, nz, lon), (3, rows, nz, lon))
    m0, dv, mix, g0, gd, inner = call(
        fill_kernel,
        [full, derived, jax.ShapeDtypeStruct((2 * ntr * nz, 2 * ntr * nz), jnp.bfloat16), cols, some, cols],
        turned,
        ocean,
        g_own,
        g_partner,
        got,
        g_other,
        rates,
    )
    z, edge_a, rows_b = call(
        edge_kernel, [cols, (nz, lon), (2 * nf + 1, nz, lon)], turned, ocean, inner, from_outer
    )
    rows_b, edge_a = (swap(rows_b, lat_b), swap(edge_a, lat_a))
    work = [(7, rows, nz, lon), pltpu.VMEM((rows, 2 * ntr * nz, lon), jnp.bfloat16)]
    work += [(ntr + 1, rows, nz, lon), cols, cols, some]
    m1, m2 = call(inner_kernel, [full, full], m0, dv, mix, g0, gd, z, scratch=[derived] + work, cost=20)
    third = (3, lat_dev, nz, lon)
    out, rim, keep, send = call(
        outer_kernel,
        [(ntr, nz, lat_blk, lon), (ntr, 4, nz, lon), third, third],
        m0,
        dv,
        mix,
        g0,
        gd,
        z,
        rows_a,
        rows_b,
        edge_a,
        m1,
        m2,
        scratch=[full, full, derived, derived] + work + [pltpu.SemaphoreType.DMA((lat_blk - 4,))],
        away=(0,),
    )
    returned = swap(send, partner)
    buffer = (3, nz, lat_dev, lon)
    flow_out, temp_out, out = call(
        finish_own_kernel,
        [flow.shape, temp.shape, out.shape],
        keep,
        rim,
        m2,
        out,
        scratch=[buffer, pltpu.SemaphoreType.DMA((6 + rows // 2 - 4,))],
        far=(3,),
        away=(0, 1, 2),
        aliases={3: 2},
    )
    flow_out, temp_out = call(
        finish_other_kernel,
        [flow.shape, temp.shape],
        returned,
        flow_out,
        temp_out,
        scratch=[buffer, pltpu.SemaphoreType.DMA((2,))],
        far=(1, 2),
        away=(0, 1),
        aliases={1: 0, 2: 1},
    )
    return (flow_out, temp_out, out[None])


def solution(mesh):
    in_specs = (
        P(None, None, "row", "col"),
        P(None, "row", "col"),
        P("row", None, None, None, "col"),
        P("row", "col"),
        P("row", "col"),
        P(),
    )
    out_specs = (
        P(None, None, "row", "col"),
        P(None, "row", "col"),
        P("row", None, None, None, "col"),
    )
    return jax.shard_map(
        functools.partial(on_device, mesh.shape["row"], mesh.shape["col"]),
        mesh=mesh,
        in_specs=in_specs,
        out_specs=out_specs,
        check_vma=False,
    )
```

```python
import functools
import jax
import jax.numpy as jnp
from jax import lax
from jax.experimental import pallas as pl
from jax.experimental.pallas import tpu as pltpu
from jax.sharding import PartitionSpec as P

KL = 4
STEPS = 2

time_step = 0.2
viscosity = 0.2
expansion = 0.05
coriolis_base = 0.5
kappa_base = 0.05
kappa_shear = 0.2
react_step = 0.25
water_absorb = 0.1
pigment_absorb = 0.6
heat_gain = 1.0

EXTRA = 4
WIN = 4


def up(x):
    return pltpu.roll(x, 1, x.ndim - 2)


def down(x):
    return pltpu.roll(x, x.shape[-2] - 1, x.ndim - 2)


def lanes_of(shape):
    return lax.broadcasted_iota(jnp.int32, shape, len(shape) - 1)


def levels_of(shape):
    return lax.broadcasted_iota(jnp.int32, shape, len(shape) - 2)


def window(x, lat, into):
    lon = x.shape[1]
    lane = lanes_of(x.shape)
    base = WIN * (lat + 1)
    moved = pltpu.roll(x, (base + 2) % lon, 1)
    return jnp.where((lane >= base) & (lane < base + WIN), moved, into)


def place():
    row = lax.axis_index("row")
    return (row % 2, row // 2, lax.axis_index("col"))


def edge_starts(chip, lat_blk):
    odd = chip % 2
    return ((1 - odd) * (lat_blk - 2), odd * (lat_blk - 2))


def pack_ocean_kernel(flow_in, temp_in, bottom_in, sunlight_in, tracers_in, mine, to_partner, g_other, tracers, flow, temp, bottom, sunlight, sem):
    copies = [
        pltpu.make_async_copy(src, dst, sem.at[i])
        for i, (src, dst) in enumerate(
            ((flow_in, flow), (temp_in, temp), (bottom_in, bottom), (sunlight_in, sunlight), (tracers_in, tracers))
        )
    ]
    for copy in copies:
        copy.start()
    for copy in copies[:-1]:
        copy.wait()
    lat_dev, nz, lon = mine.shape[1:]
    lon_dev = temp.shape[2]
    half, _, _ = place()
    first = half == 0
    zero = jnp.zeros((nz, lon), jnp.float32)
    level = levels_of((nz, lon_dev))
    own = [zero] * EXTRA
    far = [zero] * EXTRA
    for t in range(lat_dev):
        depth = jnp.broadcast_to(bottom[t : t + 1, :], (nz, lon_dev))
        light = jnp.broadcast_to(sunlight[t : t + 1, :], (nz, lon_dev))
        wet = (level < depth).astype(jnp.float32)
        aux = jnp.where(level == 0, depth.astype(jnp.float32), jnp.where(level == 1, light, 0.0))
        for f, tile in enumerate((flow[0, :, t, :] * wet, flow[1, :, t, :] * wet, temp[:, t, :] * wet, aux)):
            low, high = (tile[:, :lon], tile[:, lon:])
            a, b = (jnp.where(first, low, high), jnp.where(first, high, low))
            mine[f, t] = a
            if f < EXTRA - 1:
                to_partner[f * lat_dev + t] = b
            own[f] = window(a, t, own[f])
            far[f] = window(b, t, far[f])
    flat = (EXTRA - 1) * lat_dev
    for i, both in enumerate((bottom[...].astype(jnp.float32), sunlight[...])):
        to_partner[flat + i, :lat_dev, :] = jnp.where(first, both[:, lon:], both[:, :lon])
    shift = half * (WIN * lat_dev)
    for f in range(EXTRA):
        to_partner[flat + 2 + f] = pltpu.roll(own[f], shift, 1)
        g_other[f] = pltpu.roll(far[f], shift, 1)
    copies[-1].wait()


def pack_tracers_kernel(tracers, turned, g_tracers):
    ntr, nz, lat_blk, lon = tracers.shape

    def some(i, _):
        g = [jnp.zeros((nz, lon), jnp.float32)] * PACK
        for t in range(lat_blk):
            for k in range(PACK):
                x = tracers[i * PACK + k, :, t, :]
                turned[i * PACK + k, t] = x
                g[k] = window(x, t, g[k])
        for k in range(PACK):
            g_tracers[i * PACK + k] = g[k]
        return 0

    lax.fori_loop(0, ntr // PACK, some, 0)


def in_half(shape, half, lat_dev):
    lane = lanes_of(shape)
    base = WIN * (lat_dev * half + 1)
    return (lane >= base) & (lane < base + WIN * lat_dev)


def edge_rows(turned, ocean, start, out):
    ntr = turned.shape[0]
    for n in range(ntr):
        out[2 * n : 2 * n + 2] = turned[n, pl.ds(start, 2)]
    for f in range(EXTRA):
        out[2 * (ntr + f) : 2 * (ntr + f) + 2] = ocean[f, pl.ds(start, 2)]


def join_kernel(mine, got, to_partner, g_tracers, turned, ocean, g_own, to_outer, rows_a):
    _, lat_dev, nz, lon = mine.shape
    ntr = g_tracers.shape[0]
    nf = ntr + EXTRA
    half, chip, _ = place()
    tile = (nz, lon)
    own_lanes = in_half(tile, half, lat_dev)
    shift = (1 - half) * (WIN * lat_dev)
    flat, level = ((EXTRA - 1) * lat_dev, levels_of(tile))
    g_own[:ntr] = g_tracers[...]
    for f in range(EXTRA):
        g = jnp.zeros(tile, jnp.float32)
        for t in range(lat_dev):
            if f < EXTRA - 1:
                x = got[f * lat_dev + t]
            else:
                depth, light = (jnp.broadcast_to(got[flat + i, t : t + 1, :], tile) for i in range(2))
                x = jnp.where(level == 0, depth, jnp.where(level == 1, light, 0.0))
            ocean[f, half * lat_dev + t] = mine[f, t]
            ocean[f, (1 - half) * lat_dev + t] = x
            g = window(x, t, g)
        g_own[ntr + f] = jnp.where(own_lanes, to_partner[flat + 2 + f], pltpu.roll(g, shift, 1))
    edge_rows(turned, ocean, edge_starts(chip, 2 * lat_dev)[0], rows_a)
    lane = lanes_of(tile)
    front, near = (lane % WIN < 2, in_half(tile, 0, 2 * lat_dev))
    side = (1 - half) * (lon - 2)
    for i in range(nf // 4):
        a, b, c, d = [pltpu.roll(g_own[4 * i + k], side, 1) for k in range(4)]
        low = jnp.where(front, a, pltpu.roll(b, 2, 1))
        high = jnp.where(front, c, pltpu.roll(d, 2, 1))
        to_outer[i] = jnp.where(near, low, pltpu.roll(high, lon // 2, 1))


def edge_kernel(turned, ocean, inner, from_outer, z, to_a, to_b):
    nf, nz, lon = z.shape
    lat_blk = turned.shape[1]

    half, chip, column = place()
    tile = (nz, lon)
    lane = lanes_of(tile)
    outer_ok = jnp.where(half == 0, column > 0, column < lax.axis_size("col") - 1)
    from_partner = (lane % WIN < 2).astype(jnp.int32) == half
    outer_lanes = in_half(tile, 0, lat_blk) & outer_ok
    start_a, start_b = edge_starts(chip, lat_blk)
    corner_a = corner_b = jnp.zeros(tile, jnp.float32)
    for f in range(nf):
        k = f % 4
        moved = pltpu.roll(from_outer[f // 4], lon + 2 * half - 2 * (k % 2) - lon // 2 * (k // 2), 1)
        cols = jnp.where(from_partner, inner[f], jnp.where(outer_lanes, moved, 0.0))
        z[f] = cols
        at = (lane >= WIN * f) & (lane < WIN * f + WIN)
        low = pltpu.roll(cols, (WIN * f - WIN) % lon, 1)
        high = pltpu.roll(cols, (WIN * f - WIN * lat_blk) % lon, 1)
        corner_a = jnp.where(at, jnp.where(start_a > 0, high, low), corner_a)
        corner_b = jnp.where(at, jnp.where(start_b > 0, high, low), corner_b)
    to_a[...] = corner_a
    edge_rows(turned, ocean, start_b, to_b)
    to_b[2 * nf] = corner_b


def kappa_of(u, v):
    du, dv = (u - down(u), v - down(v))
    sq = jnp.where(levels_of(u.shape) < u.shape[-2] - 1, du * du + dv * dv, 0.0)
    return kappa_base + kappa_shear * sq / (1.0 + sq)


def sum_above(x):
    level = levels_of(x.shape)
    k = 1
    while k < x.shape[-2]:
        x = x + jnp.where(level >= k, pltpu.roll(x, k, x.ndim - 2), 0.0)
        k *= 2
    return x


def sum_below(x):
    level, nz = (levels_of(x.shape), x.shape[-2])
    k = 1
    while k < nz:
        x = x + jnp.where(level < nz - k, pltpu.roll(x, nz - k, x.ndim - 2), 0.0)
        k *= 2
    return x


def pressure_of(heat):
    return -expansion * sum_above(heat)


def wet_of(aux):
    depth = jnp.broadcast_to(aux[..., 0:1, :], aux.shape)
    return (levels_of(aux.shape).astype(jnp.float32) < depth).astype(jnp.float32)


def light_of(aux):
    return jnp.broadcast_to(aux[..., 1:2, :], aux.shape)


def dynamics(u, v, wet, kap, prs, coriolis):
    um, ue, uw, un, us = u
    vm, ve, vw, vn, vs = v
    wm, we, ww, wn, ws = wet
    km, ke, kw, kn, ks = kap
    _, pe, pw, pn, ps = prs
    level, nz = (levels_of(um.shape), um.shape[-2])
    oe, ow, on, os_ = (wm * we, wm * ww, wm * wn, wm * ws)
    fe, fw, fn, fs = (0.5 * (um + ue) * oe, 0.5 * (um + uw) * ow, 0.5 * (vm + vn) * on, 0.5 * (vm + vs) * os_)
    ce, cw, cn, cs = (0.5 * (km + ke) * oe, 0.5 * (km + kw) * ow, 0.5 * (km + kn) * on, 0.5 * (km + ks) * os_)
    div = fe - fw + fn - fs
    total = sum_below(div)
    w_top = jnp.where(level >= 1, -total, 0.0)
    w_bot = jnp.where(level < nz - 1, -down(total), 0.0)
    weights = (
        wm * (1.0 - time_step * (ce + cw + cn + cs + 0.5 * (div + w_top - w_bot))),
        time_step * (ce - 0.5 * fe),
        time_step * (cw + 0.5 * fw),
        time_step * (cn - 0.5 * fn),
        time_step * (cs + 0.5 * fs),
        (-0.5 * time_step) * wm * w_top,
        (0.5 * time_step) * wm * w_bot,
    )
    lap_u = oe * (ue - um) + ow * (uw - um) + on * (un - um) + os_ * (us - um)
    lap_v = oe * (ve - vm) + ow * (vw - vm) + on * (vn - vm) + os_ * (vs - vm)
    new_u = wm * (um + time_step * (coriolis * vm - 0.5 * (pe - pw) + viscosity * lap_u))
    new_v = wm * (vm + time_step * (-coriolis * um - 0.5 * (pn - ps) + viscosity * lap_v))
    return (new_u, new_v, weights)


def transport(weights, x, east, west, north, south):
    a0, ae, aw, an, as_, at, ab = weights
    return (a0 * x + ae * east) + (aw * west + an * north) + (as_ * south + at * up(x)) + ab * down(x)


def saturated(x):
    return x * lax.rsqrt(1.0 + x * x)


def absorbed(pigment):
    level = levels_of(pigment.shape)
    sq = pigment * pigment
    depth = water_absorb + pigment_absorb * (sq / (1.0 + sq))
    above = jnp.where(level >= 1, up(depth), 0.0)
    k = 1
    while k < KL:
        above = above + jnp.where(level >= k, pltpu.roll(above, k, above.ndim - 2), 0.0)
        k *= 2
    return jnp.where(level < KL, jnp.exp(-above) * (1.0 - jnp.exp(-depth)), 0.0)


def two_parts(x):
    high = x.astype(jnp.bfloat16)
    return (high, (x - high.astype(jnp.float32)).astype(jnp.bfloat16))


def mix_matrix(rates, nz):
    ntr = rates.shape[0]
    size = ntr * nz
    exact = dict(precision=lax.Precision.HIGHEST, preferred_element_type=jnp.float32)
    spread = lax.broadcasted_iota(jnp.int32, (size, ntr), 0) // nz == lax.broadcasted_iota(jnp.int32, (size, ntr), 1)
    spread = spread.astype(jnp.float32)
    wide = jnp.dot(spread, rates, **exact)
    full = lax.dot_general(wide, spread, (((1,), (1,)), ((), ())), **exact)
    same = lax.broadcasted_iota(jnp.int32, (size, size), 0) % nz == lax.broadcasted_iota(jnp.int32, (size, size), 1) % nz
    high, low = two_parts(jnp.where(same, full, 0.0))
    top = jnp.concatenate([high, high], axis=1)
    return jnp.concatenate([top, jnp.concatenate([low, jnp.zeros_like(low)], axis=1)], axis=0)


def beside(z, r, lon):
    return pltpu.roll(z, lon - 2 - WIN * (r - 1), z.ndim - 1)


def sides(x, edge):
    lane, lon = (lanes_of(x.shape), x.shape[-1])
    west = pltpu.roll(jnp.where(lane == lon - 1, edge, x), 1, x.ndim - 1)
    east = pltpu.roll(jnp.where(lane == 0, edge, x), lon - 1, x.ndim - 1)
    return (east, west)


def around_rows(m, f, z, r, count):
    x = m[f, pl.ds(r, count)]
    edge = jnp.stack([beside(z, r + i, x.shape[-1]) for i in range(count)])
    return (x, *sides(x, edge), m[f, pl.ds(r + 1, count)], m[f, pl.ds(r - 1, count)])


def around_columns(x, own):
    lane, lon = (lanes_of(x.shape), x.shape[-1])
    west = pltpu.roll(jnp.where(lane % WIN == 0, x, own), 1, x.ndim - 1)
    east = pltpu.roll(jnp.where(lane % WIN == WIN - 1, x, own), lon - 1, x.ndim - 1)
    return (x, east, west, pltpu.roll(x, lon - WIN, x.ndim - 1), pltpu.roll(x, WIN, x.ndim - 1))


def coriolis_at(lat, lat_blk):
    _, chip, _ = place()
    latitude = (lat + chip * lat_blk).astype(jnp.float32)
    return coriolis_base * (2.0 * (latitude + 0.5) / (lax.axis_size("row") // 2 * lat_blk) - 1.0)


KAP, PRS, WET = (0, 1, 2)
GROUP = 8
PACK = 16
PIECE = 2


def span(start, stop):
    return (start, stop - start, 1, stop - start)


def chunks(rows, most, body):
    first, apart, times, size = rows
    count = max(k for k in range(1, min(most, size) + 1) if size % k == 0)
    if times > 1 or count == size:
        for i in range(times):
            body(first + i * apart, size)
    else:

        def one(i, _):
            body(first + i * count, count)
            return 0

        lax.fori_loop(0, size // count, one, 0)


def derive_rows(m, dv, ntr, rows):
    def body(r, count):
        at = pl.ds(r, count)
        dv[KAP, at] = kappa_of(m[ntr, at], m[ntr + 1, at])
        dv[PRS, at] = pressure_of(m[ntr + 2, at])

    chunks(rows, 10, body)


def derive_columns(z, zd, ntr):
    zd[KAP] = kappa_of(z[ntr], z[ntr + 1])
    zd[PRS] = pressure_of(z[ntr + 2])


def ocean_rows(m, dv, z, zd, wts, new, ntr, rows):
    def body(r, count):
        at = pl.ds(r, count)
        lat = lax.broadcasted_iota(jnp.int32, (count, *m.shape[2:]), 0) + (r - 2)
        new_u, new_v, weights = dynamics(
            around_rows(m, ntr, z[ntr], r, count),
            around_rows(m, ntr + 1, z[ntr + 1], r, count),
            around_rows(dv, WET, zd[WET], r, count),
            around_rows(dv, KAP, zd[KAP], r, count),
            around_rows(dv, PRS, zd[PRS], r, count),
            coriolis_at(lat, m.shape[1] - 4),
        )
        new[ntr, at] = new_u
        new[ntr + 1, at] = new_v
        for i, w in enumerate(weights):
            wts[i, at] = w

    chunks(rows, 9, body)


def tracer_rows(m, z, wts, dv, mix, moved, sat, new, ntr, rows):
    nz, lon = m.shape[2:]
    half = ntr * nz
    first, apart, times, count = rows
    if times == 1:
        count = max(k for k in range(1, PIECE + 1) if rows[3] % k == 0)
        apart, times = (count, rows[3] // count)

    def move(r):
        weights = [wts[i, r] for i in range(7)]
        for n in range(0, ntr, GROUP):
            x = m[n : n + GROUP, r]
            edge = beside(z[n : n + GROUP], r, lon)
            done = transport(weights, x, *sides(x, edge), m[n : n + GROUP, r + 1], m[n : n + GROUP, r - 1])
            moved[n : n + GROUP, r] = done
            high, low = two_parts(saturated(done).reshape(GROUP * nz, lon))
            sat[r, n * nz : (n + GROUP) * nz, :] = high
            sat[r, half + n * nz : half + (n + GROUP) * nz, :] = low
        h = ntr + 2
        x = m[h, r]
        moved[ntr, r] = transport(weights, x, *sides(x, beside(z[h], r, lon)), m[h, r + 1], m[h, r - 1])

    def react(every):
        both = jnp.concatenate([sat[r] for r in every], axis=1)
        res = jnp.dot(mix[...], both, preferred_element_type=jnp.float32)
        res = res[:half] + res[half:]
        for i, r in enumerate(every):
            gain = react_step * dv[WET, r]
            for n in range(ntr):
                new[n, r] = moved[n, r] + gain * res[n * nz : (n + 1) * nz, i * lon : (i + 1) * lon]

    def piece(i):
        return [first + i * apart + k for k in range(count)]

    def both_parts(i, _):
        react(piece(i - 1))
        for r in piece(i):
            move(r)
        return 0

    if rows[2] > 1:
        every = [r for i in range(times) for r in piece(i)]
        for r in every:
            move(r)
        react(every)
    else:
        for r in piece(0):
            move(r)
        lax.fori_loop(1, times, both_parts, 0)
        react(piece(times - 1))


def light_rows(m, dv, moved, new, ntr, rows):
    def body(r, count):
        at = pl.ds(r, count)
        light = light_of(m[ntr + 3, at]) * dv[WET, at] * absorbed(new[0, at])
        new[ntr + 2, at] = moved[ntr, at] + heat_gain * light

    chunks(rows, 9, body)


def column_step(z0, g0, zd, gd, z1, mix, ntr, lat_blk):
    nz, lon = z0.shape[1:]
    half = ntr * nz
    wet = zd[WET]
    new_u, new_v, weights = dynamics(
        around_columns(z0[ntr], g0[ntr]),
        around_columns(z0[ntr + 1], g0[ntr + 1]),
        around_columns(wet, gd[WET]),
        around_columns(zd[KAP], gd[KAP]),
        around_columns(zd[PRS], gd[PRS]),
        coriolis_at(lanes_of((nz, lon)) // WIN - 1, lat_blk),
    )
    moved = transport(weights, *around_columns(z0[:ntr], g0[:ntr]))
    high, low = two_parts(saturated(moved).reshape(half, lon))
    res = jnp.dot(mix[...], jnp.concatenate([high, low], axis=0), preferred_element_type=jnp.float32)
    done = moved + (react_step * wet) * (res[:half] + res[half:]).reshape(ntr, nz, lon)
    z1[:ntr] = done
    z1[ntr] = new_u
    z1[ntr + 1] = new_v
    heat = transport(weights, *around_columns(z0[ntr + 2], g0[ntr + 2]))
    z1[ntr + 2] = heat + heat_gain * light_of(z0[ntr + 3]) * wet * absorbed(done[0])


def fill_kernel(turned, ocean, g_own, g_partner, got, g_other, rates, m0, dv, mix, g0, gd, inner):
    ntr, lat_blk, nz, lon = turned.shape
    half, _, _ = place()
    inner[:ntr] = g_partner[...]
    for f in range(EXTRA):
        theirs = got[(EXTRA - 1) * (lat_blk // 2) + 2 + f]
        inner[ntr + f] = jnp.where(in_half((nz, lon), half, lat_blk // 2), g_other[f], theirs)
    mix[...] = mix_matrix(rates[...], nz)
    own = span(2, lat_blk + 2)

    def wets(r, count):
        at = pl.ds(r, count)
        for f in range(EXTRA):
            m0[ntr + f, at] = ocean[f, pl.ds(r - 2, count)]
        dv[WET, at] = wet_of(ocean[EXTRA - 1, pl.ds(r - 2, count)])

    chunks(own, 8, wets)

    def some(r, count):
        wet = dv[WET, r]
        for n in range(ntr):
            m0[n, r] = turned[n, r - 2] * wet

    chunks(own, 1, some)
    derive_rows(m0, dv, ntr, own)
    mask_columns([g_own[f] for f in range(ntr + EXTRA)], g0, gd)


def mask_columns(fields, z, zd):
    ntr = len(fields) - EXTRA
    wet = wet_of(fields[-1])
    zd[WET] = wet
    for f, cols in enumerate(fields):
        z[f] = cols * wet if f < ntr else cols
    derive_columns(z, zd, ntr)


def inner_kernel(m0, dv, mix, g0, gd, z_in, m1, m2, dv1, wts, sat, moved, z0, z1, zd):
    nf, rows, _, _ = m0.shape
    ntr = nf - EXTRA
    mask_columns([z_in[f] for f in range(nf)], z0, zd)
    column_step(z0, g0, zd, gd, z1, mix, ntr, rows - 4)
    now = span(3, rows - 3)
    ocean_rows(m0, dv, z0, zd, wts, m1, ntr, now)
    tracer_rows(m0, z0, wts, dv, mix, moved, sat, m1, ntr, now)
    light_rows(m0, dv, moved, m1, ntr, now)
    dv1[WET, 3 : rows - 3] = dv[WET, 3 : rows - 3]
    derive_rows(m1, dv1, ntr, now)
    derive_columns(z1, zd, ntr)
    now = span(4, rows - 4)
    ocean_rows(m1, dv1, z1, zd, wts, m2, ntr, now)
    tracer_rows(m1, z1, wts, dv1, mix, moved, sat, m2, ntr, now)
    light_rows(m0, dv1, moved, m2, ntr, now)


def outer_kernel(m_own, dv_own, mix, g0, gd, z_in, rows_a, rows_b, edge_a, m1_in, m2_in, out, rim, keep, send, m0, m1, dv0, dv1, wts, sat, moved, z0, z1, zd, sem):
    nf, rows, nz, lon = m_own.shape
    ntr = nf - EXTRA
    lat_blk = rows - 4
    half, chip, _ = place()
    even = chip % 2 == 0
    south_ok, north_ok = (chip > 0, chip < lax.axis_size("row") // 2 - 1)
    copies = [
        pltpu.make_async_copy(m2_in.at[pl.ds(0, ntr), r], out.at[:, :, r - 2, :], sem.at[r - 4]) for r in range(4, rows // 2)
    ]
    for copy in copies:
        copy.start()

    def got(high, a, b):
        picked = jnp.where(even, a, b) if high else jnp.where(even, b, a)
        return jnp.where(north_ok if high else south_ok, picked, 0.0)

    for high, start in ((False, 0), (True, rows - 2)):
        for f in range(EXTRA):
            m0[ntr + f, start : start + 2] = got(high, *(x[pl.ds(2 * (ntr + f), 2)] for x in (rows_a, rows_b)))
        wet = wet_of(m0[nf - 1, start : start + 2])
        dv0[WET, start : start + 2] = wet
        for n in range(ntr):
            m0[n, start : start + 2] = got(high, *(x[pl.ds(2 * n, 2)] for x in (rows_a, rows_b))) * wet
        derive_rows(m0, dv0, ntr, span(start, start + 2))
    for start in (2, rows - 4):
        m0[:, start : start + 2] = m_own[:, start : start + 2]
        dv0[:, start : start + 2] = dv_own[:, start : start + 2]
    lane = lanes_of((nz, lon))
    low, high = (got(side, edge_a[...], rows_b[2 * nf]) for side in (False, True))
    at_low, at_high = (lane < WIN, (lane >= WIN * (lat_blk + 1)) & (lane < WIN * (lat_blk + 2)))
    fields = []
    for f in range(nf):
        cols = jnp.where(at_low, pltpu.roll(low, (-WIN * f) % lon, 1), z_in[f])
        fields.append(jnp.where(at_high, pltpu.roll(high, (WIN * (lat_blk + 1) - WIN * f) % lon, 1), cols))
    mask_columns(fields, z0, zd)
    column_step(z0, g0, zd, gd, z1, mix, ntr, lat_blk)
    now = (1, lat_blk, 2, 2)
    ocean_rows(m0, dv0, z0, zd, wts, m1, ntr, now)
    tracer_rows(m0, z0, wts, dv0, mix, moved, sat, m1, ntr, now)
    light_rows(m0, dv0, moved, m1, ntr, now)
    for start in (3, rows - 5):
        m1[:, start : start + 2] = m1_in[:, start : start + 2]
    for start in (1, rows - 3):
        dv1[WET, start : start + 2] = dv0[WET, start : start + 2]
    for start in (3, rows - 5):
        dv1[WET, start : start + 2] = dv_own[WET, start : start + 2]
    derive_rows(m1, dv1, ntr, (1, rows - 6, 2, 4))
    derive_columns(z1, zd, ntr)
    now = (2, rows - 6, 2, 2)
    ocean_rows(m1, dv1, z1, zd, wts, m0, ntr, now)
    tracer_rows(m1, z1, wts, dv1, mix, moved, sat, m0, ntr, now)
    light_rows(m0, dv1, moved, m0, ntr, now)

    rim[:, 0:2] = m0[:ntr, 2:4]
    rim[:, 2:4] = m0[:ntr, rows - 4 : rows - 2]
    m0[ntr : ntr + 3, 4 : rows - 4] = m2_in[ntr : ntr + 3, 4 : rows - 4]
    count = lat_blk // 2
    for f in range(3):
        keep[f] = m0[ntr + f, pl.ds(2 + half * count, count)]
        send[f] = m0[ntr + f, pl.ds(2 + (1 - half) * count, count)]
    for copy in copies:
        copy.wait()


def half_copies(part, core, buffer, flow_out, temp_out, sem):
    _, lat_dev, _, lon = part.shape
    for f in range(3):
        for t in range(lat_dev):
            buffer[f, :, t, :] = part[f, t]
    at = pl.ds(pl.multiple_of(core * lon, lon), lon)
    return [
        pltpu.make_async_copy(buffer.at[pl.ds(0, 2)], flow_out.at[:, :, :, at], sem.at[0]),
        pltpu.make_async_copy(buffer.at[2], temp_out.at[:, :, at], sem.at[1]),
    ]


def finish_own_kernel(keep, rim, m, out_in, flow_out, temp_out, out, buffer, sem):
    lat_blk = 2 * keep.shape[1]
    copies = [
        pltpu.make_async_copy(rim.at[:, i], out.at[:, :, t, :], sem.at[2 + i])
        for i, t in enumerate((0, 1, lat_blk - 2, lat_blk - 1))
    ]
    rows, ntr = (m.shape[1], rim.shape[0])
    copies += [
        pltpu.make_async_copy(m.at[pl.ds(0, ntr), r], out.at[:, :, r - 2, :], sem.at[6 + r - rows // 2])
        for r in range(rows // 2, rows - 4)
    ]
    for copy in copies:
        copy.start()
    more = half_copies(keep, place()[0], buffer, flow_out, temp_out, sem)
    for copy in more:
        copy.start()
    for copy in copies + more:
        copy.wait()


def finish_other_kernel(got, flow_in, temp_in, flow_out, temp_out, buffer, sem):
    copies = half_copies(got, 1 - place()[0], buffer, flow_out, temp_out, sem)
    for copy in copies:
        copy.start()
    for copy in copies:
        copy.wait()


def call(kernel, outs, *args, scratch=(), far=(), away=(), aliases=None, cost=1):
    vmem, anywhere = (pl.BlockSpec(memory_space=pltpu.VMEM), pl.BlockSpec(memory_space=pl.ANY))
    return pl.pallas_call(
        kernel,
        out_shape=[jax.ShapeDtypeStruct(s, jnp.float32) if isinstance(s, tuple) else s for s in outs],
        in_specs=[anywhere if i in far else vmem for i in range(len(args))],
        out_specs=[anywhere if i in away else vmem for i in range(len(outs))],
        scratch_shapes=[pltpu.VMEM(s, jnp.float32) if isinstance(s, tuple) else s for s in scratch],
        input_output_aliases=aliases or {},
        compiler_params=pltpu.CompilerParams(vmem_limit_bytes=40 * 2**20),
        cost_estimate=pl.CostEstimate(
            flops=int(cost * 10**9), transcendentals=0, bytes_accessed=int(cost * 4 * 2**20)
        ),
    )(*args)


def both_ways(pairs):
    return sorted(pairs + [(b, a) for a, b in pairs])


def exchanges(n_row, n_col):
    chips = n_row // 2

    def dev(p, h, c):
        return (2 * p + h) * n_col + c

    partner = [(dev(p, 0, c), dev(p, 1, c)) for p in range(chips) for c in range(n_col)]
    outer = [(dev(p, 1, c), dev(p, 0, c + 1)) for p in range(chips) for c in range(n_col - 1)]
    for p in range(0, chips - 1, 2):
        outer += [(dev(p, 0, 0), dev(p + 1, 0, 0)), (dev(p, 1, n_col - 1), dev(p + 1, 1, n_col - 1))]
    lat_a = [(dev(p, h, c), dev(p + 1, h, c)) for p in range(0, chips - 1, 2) for h in (0, 1) for c in range(n_col)]
    lat_b = [(dev(p, h, c), dev(p + 1, h, c)) for p in range(1, chips - 1, 2) for h in (0, 1) for c in range(n_col)]
    ends = [0] if chips % 2 else [0, chips - 1]
    lat_b += [(dev(p, 0, c), dev(p, 1, c)) for p in ends for c in range(n_col)]
    return [both_ways(x) for x in (partner, outer, lat_a, lat_b)]


def on_device(n_row, n_col, flow, temp, tracers, bottom, sunlight, rates):
    nz, lat_dev, lon_dev = temp.shape
    _, ntr, _, lat_blk, lon = tracers.shape
    nf = ntr + EXTRA
    partner, outer, lat_a, lat_b = exchanges(n_row, n_col)

    def swap(x, pairs):
        return lax.ppermute(x, ("row", "col"), pairs)

    block = tracers[0]
    rows = lat_blk + 4
    cols, extra, some = ((nf, nz, lon), (EXTRA, nz, lon), (3, nz, lon))
    sent = ((EXTRA - 1) * lat_dev + 2 + EXTRA, nz, lon)
    given = (flow, temp, bottom, sunlight, block)
    mine, to_partner, g_other, block = call(
        pack_ocean_kernel,
        [(EXTRA, lat_dev, nz, lon), sent, extra, block.shape],
        *[pltpu.with_memory_space_constraint(x, pltpu.HBM) for x in given],
        scratch=[
            flow.shape,
            temp.shape,
            pltpu.VMEM(bottom.shape, jnp.int32),
            sunlight.shape,
            pltpu.SemaphoreType.DMA((len(given),)),
        ],
        far=range(len(given)),
    )
    got = swap(to_partner, partner)
    turned, g_tracers = call(pack_tracers_kernel, [(ntr, lat_blk, nz, lon), (ntr, nz, lon)], block)
    rim = (2 * nf, nz, lon)
    ocean, g_own, to_outer, rows_a = call(
        join_kernel,
        [(EXTRA, lat_blk, nz, lon), cols, (nf // 4, nz, lon), rim],
        mine,
        got,
        to_partner,
        g_tracers,
        turned,
    )
    rows_a = swap(rows_a, lat_a)
    from_outer = swap(to_outer, outer)
    g_partner = swap(g_tracers, partner)
    full, derived = ((nf, rows, nz, lon), (3, rows, nz, lon))
    m0, dv, mix, g0, gd, inner = call(
        fill_kernel,
        [full, derived, jax.ShapeDtypeStruct((2 * ntr * nz, 2 * ntr * nz), jnp.bfloat16), cols, some, cols],
        turned,
        ocean,
        g_own,
        g_partner,
        got,
        g_other,
        rates,
    )
    z, edge_a, rows_b = call(
        edge_kernel, [cols, (nz, lon), (2 * nf + 1, nz, lon)], turned, ocean, inner, from_outer
    )
    rows_b, edge_a = (swap(rows_b, lat_b), swap(edge_a, lat_a))
    work = [(7, rows, nz, lon), pltpu.VMEM((rows, 2 * ntr * nz, lon), jnp.bfloat16)]
    work += [(ntr + 1, rows, nz, lon), cols, cols, some]
    m1, m2 = call(inner_kernel, [full, full], m0, dv, mix, g0, gd, z, scratch=[derived] + work, cost=20)
    third = (3, lat_dev, nz, lon)
    out, rim, keep, send = call(
        outer_kernel,
        [(ntr, nz, lat_blk, lon), (ntr, 4, nz, lon), third, third],
        m0,
        dv,
        mix,
        g0,
        gd,
        z,
        rows_a,
        rows_b,
        edge_a,
        m1,
        m2,
        scratch=[full, full, derived, derived] + work + [pltpu.SemaphoreType.DMA((lat_blk - 4,))],
        away=(0,),
    )
    returned = swap(send, partner)
    buffer = (3, nz, lat_dev, lon)
    flow_out, temp_out, out = call(
        finish_own_kernel,
        [flow.shape, temp.shape, out.shape],
        keep,
        rim,
        m2,
        out,
        scratch=[buffer, pltpu.SemaphoreType.DMA((6 + rows // 2 - 4,))],
        far=(3,),
        away=(0, 1, 2),
        aliases={3: 2},
    )
    flow_out, temp_out = call(
        finish_other_kernel,
        [flow.shape, temp.shape],
        returned,
        flow_out,
        temp_out,
        scratch=[buffer, pltpu.SemaphoreType.DMA((2,))],
        far=(1, 2),
        away=(0, 1),
        aliases={1: 0, 2: 1},
    )
    return (flow_out, temp_out, out[None])


def solution(mesh):
    in_specs = (
        P(None, None, "row", "col"),
        P(None, "row", "col"),
        P("row", None, None, None, "col"),
        P("row", "col"),
        P("row", "col"),
        P(),
    )
    out_specs = (
        P(None, None, "row", "col"),
        P(None, "row", "col"),
        P("row", None, None, None, "col"),
    )
    return jax.shard_map(
        functools.partial(on_device, mesh.shape["row"], mesh.shape["col"]),
        mesh=mesh,
        in_specs=in_specs,
        out_specs=out_specs,
        check_vma=False,
    )
```
